32 devices in a mesh: dp: 16 (over z, y, core), mp: 2 (over x).
Axes of the slice: x: 2, y: 2, z: 4, core: 2. Of those that a mesh axis runs over, the one named last changes fastest.
Arguments:
- tokens: bfloat16 [64, 256, 768], P('dp'), may hold values from -6 to 6
- segment: int32 [64, 256], P('dp'), may hold values from 0 to 63, as said below
- pairing: int32 [64, 64], P('dp'), may hold values from 0 to 1023
- images: bfloat16 [1024, 768], P('dp')
- qkv_weight: float32 [3, 768, 768], P(None, 'dp', 'mp'), may hold values from -0.21875 to 0.21875
- qkv_first: float32 [3, 768, 768], P(None, 'dp', 'mp'), may hold values from -80 to 80
- qkv_second: float32 [3, 768, 768], P(None, 'dp', 'mp'), may hold values from 16.384 to 65.536
- out_weight: float32 [768, 768], P('dp', 'mp'), may hold values from -0.4375 to 0.4375
- out_first: float32 [768, 768], P('dp', 'mp'), may hold values from -48 to 48
- out_second: float32 [768, 768], P('dp', 'mp'), may hold values from 5.89824 to 23.59296
- up_weight: float32 [768, 3072], P('dp', 'mp'), may hold values from -0.21875 to 0.21875
- up_first: float32 [768, 3072], P('dp', 'mp'), may hold values from -32 to 32
- up_second: float32 [768, 3072], P('dp', 'mp'), may hold values from 2.62144 to 10.48576
- down_weight: float32 [768, 3072], P('dp', 'mp'), may hold values from -0.109375 to 0.109375
- down_first: float32 [768, 3072], P('dp', 'mp'), may hold values from -80 to 80
- down_second: float32 [768, 3072], P('dp', 'mp'), may hold values from 13.27104 to 53.08416
- affine: float32 [6, 768], P(None, 'dp'), as said below
- affine_first: float32 [6, 768], P(None, 'dp'), may hold values from -96 to 96
- affine_second: float32 [6, 768], P(None, 'dp'), may hold values from 23.59296 to 94.37184
- head_bias: float32 [2, 768], P(None, ('mp', 'dp')), may hold values from -1.75 to 1.75
- head_first: float32 [2, 768], P(None, ('mp', 'dp')), may hold values from -80 to 80
- head_second: float32 [2, 768], P(None, ('mp', 'dp')), may hold values from 16.384 to 65.536
- inner_bias: float32 [3072], P(('mp', 'dp')), may hold values from -1.75 to 1.75
- inner_first: float32 [3072], P(('mp', 'dp')), may hold values from -32 to 32
- inner_second: float32 [3072], P(('mp', 'dp')), may hold values from 2.62144 to 10.48576
Outputs:
- mean_loss: float32 [], replicated
- grad_input: float32 [64, 256, 768], P('dp')
- qkv_next: float32 [3, 768, 768], P(None, 'dp', 'mp')
- qkv_first_next: float32 [3, 768, 768], P(None, 'dp', 'mp')
- qkv_second_next: float32 [3, 768, 768], P(None, 'dp', 'mp')
- out_next: float32 [768, 768], P('dp', 'mp')
- out_first_next: float32 [768, 768], P('dp', 'mp')
- out_second_next: float32 [768, 768], P('dp', 'mp')
- up_next: float32 [768, 3072], P('dp', 'mp')
- up_first_next: float32 [768, 3072], P('dp', 'mp')
- up_second_next: float32 [768, 3072], P('dp', 'mp')
- down_next: float32 [768, 3072], P('dp', 'mp')
- down_first_next: float32 [768, 3072], P('dp', 'mp')
- down_second_next: float32 [768, 3072], P('dp', 'mp')
- affine_next: float32 [6, 768], P(None, 'dp')
- affine_first_next: float32 [6, 768], P(None, 'dp')
- affine_second_next: float32 [6, 768], P(None, 'dp')
- head_next: float32 [2, 768], P(None, ('mp', 'dp'))
- head_first_next: float32 [2, 768], P(None, ('mp', 'dp'))
- head_second_next: float32 [2, 768], P(None, ('mp', 'dp'))
- inner_next: float32 [3072], P(('mp', 'dp'))
- inner_first_next: float32 [3072], P(('mp', 'dp'))
- inner_second_next: float32 [3072], P(('mp', 'dp'))
- tensor_norms: float32 [2, 15], replicated
The draws below stay inside these ranges and needn't reach their ends.
Inputs may be any that keep to these rules, and one draw needn't show every extreme that they name: `segment`: in every pack the slots start at 0 and rise by 0 or 1 from one position to the next; each slot holds a run of 1 to 16 positions. `pairing`: A slot that no token of its pack names has an entry too, and it is not read. `affine`: rows 0 and 2 are positive gains.
All inputs are finite; a program needn't handle non-finite values.
Results may differ from the reference program's by a relative error of at most 0.012.
The reference program's roundings to bfloat16 on the way count: a program that leaves them out, or rounds other values in their place, can miss the bound.
Values may be sent and summed in bfloat16 or wider, within the bound.
A program may use at most 192 MiB of HBM per device.

```python
import math
import jax
import jax.numpy as jnp
from jax import lax

D = 768
HEADS = 12
HD = 64
FF = 3072
PACK_LEN = 256
SEQ = 16
STEP = 10
PACK_DEV = 4
CAP = 64
PACKS = 64
NIMG = 1024
N_DP = 16


def draw_segment(key, part):
    key = jax.random.fold_in(key, 11)
    blocks = PACKS // PACK_DEV
    device = jnp.arange(PACKS, dtype=jnp.int32) // PACK_DEV
    longest = SEQ - (SEQ - 4) * device // max(blocks - 1, 1)
    shortest = jnp.maximum(longest * 3 // 4, 4)
    span = longest - shortest + 1
    raw = jax.random.randint(key, (PACKS, PACK_LEN), 0, 1 << 20, dtype=jnp.int32)
    lengths = shortest[:, None] + raw % span[:, None]
    ends = jnp.cumsum(lengths, 1)
    position = jnp.arange(PACK_LEN, dtype=jnp.int32)
    found = jax.vmap(lambda row: jnp.searchsorted(row, position, side='right'))(ends)
    return found.astype(jnp.int32)


def draw_images(key, part):
    key = jax.random.fold_in(key, 23)
    column = jnp.arange(D, dtype=jnp.float32) / (D - 1)
    base = jax.random.normal(key, (NIMG, D), jnp.float32)
    scale = 1.0 + 2.0 * column
    return (base * scale).astype(jnp.bfloat16)


def draw_affine(key, part):
    key = jax.random.fold_in(key, 37)
    column = jnp.arange(D, dtype=jnp.float32) / (D - 1)
    keys = jax.random.split(key, 2)
    ramp = 0.5 + column
    jitter = jnp.exp(jax.random.uniform(keys[0], (6, D), jnp.float32, -0.22, 0.22))
    shifts = 0.3 * jax.random.normal(keys[1], (6, D), jnp.float32)
    rows = jnp.arange(6)[:, None]
    is_gain = (rows == 0) | (rows == 2)
    return jnp.where(is_gain, ramp * jitter, shifts).astype(jnp.float32)


def plant(array, own_key, smallest, largest):
    index_at = [jax.random.randint(jax.random.fold_in(own_key, axis), (), 0, length) for axis, length in enumerate(array.shape)]
    widest = array.shape.index(max(array.shape))
    neighbour = index_at[:widest] + [(index_at[widest] + 1) % array.shape[widest]] + index_at[widest + 1:]
    return array.at[tuple(index_at)].set(smallest).at[tuple(neighbour)].set(largest)


def level_of(stream_key, shape, shards, least, top_value):
    def one(dim, blocks):
        heights = jax.random.uniform(jax.random.fold_in(jax.random.fold_in(stream_key, 6), dim), (blocks,), jnp.float32, least / len(shards), top_value / len(shards))
        return jnp.repeat(jnp.exp(heights), shape[dim] // blocks).reshape((-1,) + (1,) * (len(shape) - dim - 1))

    level = one(*shards[0])
    for cut in shards[1:]:
        level = level * one(*cut)
    return level


def noise(rng, shape, scale, limit, cuts=(), kind=jnp.bfloat16):
    loudness = level_of(rng, shape, cuts, -0.22, 0.18) if cuts else 1.0
    values = jax.random.normal(rng, shape, jnp.float32) * scale * loudness
    return jnp.minimum(jnp.maximum(values, -limit), limit).astype(kind)


def setup_inputs(seed: int = 0) -> dict:
    splits = jax.random.split(jax.random.key(seed), 26)
    tokens = noise(splits[0], (PACKS, PACK_LEN, D), 1.0, 6.0, ((0, 16),))
    segment = draw_segment(jax.random.fold_in(splits[25], 71), 0)
    pairing = plant(jax.random.randint(splits[2], (PACKS, CAP), 0, NIMG), jax.random.fold_in(splits[2], 1), 0, NIMG - 1).astype(jnp.int32)
    images = draw_images(jax.random.fold_in(splits[25], 71), 0)
    qkv_weight = noise(splits[4], (3, D, D), D ** -0.5, 0.21875, ((1, 16), (2, 2)), jnp.float32)
    qkv_first = noise(splits[5], (3, D, D), (0.111 * (PACKS * PACK_LEN) ** 0.5), 80.0, ((1, 16), (2, 2)), jnp.float32)
    qkv_second = jnp.clip(jnp.exp(math.log(65.536) - 1.3862944 * jax.random.uniform(splits[6], (3, D, D), jnp.float32) ** level_of(splits[6], (3, D, D), ((1, 16), (2, 2)), -0.2, 0.2)), 16.384, 65.536)
    out_weight = noise(splits[7], (D, D), (D // 4) ** -0.5, 0.4375, ((0, 16), (1, 2)), jnp.float32)
    out_first = noise(splits[8], (D, D), (0.067 * (PACKS * PACK_LEN) ** 0.5), 48.0, ((0, 16), (1, 2)), jnp.float32)
    out_second = jnp.clip(jnp.exp(math.log(23.59296) - 1.3862944 * jax.random.uniform(splits[9], (D, D), jnp.float32) ** level_of(splits[9], (D, D), ((0, 16), (1, 2)), -0.2, 0.2)), 5.89824, 23.59296)
    up_weight = noise(splits[10], (D, FF), D ** -0.5, 0.21875, ((0, 16), (1, 2)), jnp.float32)
    up_first = noise(splits[11], (D, FF), (0.044 * (PACKS * PACK_LEN) ** 0.5), 32.0, ((0, 16), (1, 2)), jnp.float32)
    up_second = jnp.clip(jnp.exp(math.log(10.48576) - 1.3862944 * jax.random.uniform(splits[12], (D, FF), jnp.float32) ** level_of(splits[12], (D, FF), ((0, 16), (1, 2)), -0.2, 0.2)), 2.62144, 10.48576)
    down_weight = noise(splits[13], (D, FF), FF ** -0.5, 0.109375, ((0, 16), (1, 2)), jnp.float32)
    down_first = noise(splits[14], (D, FF), (0.1 * (PACKS * PACK_LEN) ** 0.5), 80.0, ((0, 16), (1, 2)), jnp.float32)
    down_second = jnp.clip(jnp.exp(math.log(53.08416) - 1.3862944 * jax.random.uniform(splits[15], (D, FF), jnp.float32) ** level_of(splits[15], (D, FF), ((0, 16), (1, 2)), -0.2, 0.2)), 13.27104, 53.08416)
    affine = draw_affine(jax.random.fold_in(splits[25], 71), 0)
    affine_first = noise(splits[17], (6, D), (0.133 * (PACKS * PACK_LEN) ** 0.5), 96.0, ((1, 16),), jnp.float32)
    affine_second = jnp.clip(jnp.exp(math.log(94.37184) - 1.3862944 * jax.random.uniform(splits[18], (6, D), jnp.float32) ** level_of(splits[18], (6, D), ((1, 16),), -0.2, 0.2)), 23.59296, 94.37184)
    head_bias = noise(splits[19], (2, D), 0.3, 1.75, ((1, 32),), jnp.float32)
    head_first = noise(splits[20], (2, D), (0.111 * (PACKS * PACK_LEN) ** 0.5), 80.0, ((1, 32),), jnp.float32)
    head_second = jnp.clip(jnp.exp(math.log(65.536) - 1.3862944 * jax.random.uniform(splits[21], (2, D), jnp.float32) ** level_of(splits[21], (2, D), ((1, 32),), -0.2, 0.2)), 16.384, 65.536)
    inner_bias = noise(splits[22], (FF,), 0.3, 1.75, ((0, 32),), jnp.float32)
    inner_first = noise(splits[23], (FF,), (0.044 * (PACKS * PACK_LEN) ** 0.5), 32.0, ((0, 32),), jnp.float32)
    inner_second = jnp.clip(jnp.exp(math.log(10.48576) - 1.3862944 * jax.random.uniform(splits[24], (FF,), jnp.float32) ** level_of(splits[24], (FF,), ((0, 32),), -0.2, 0.2)), 2.62144, 10.48576)
    return {"tokens": tokens, "segment": segment, "pairing": pairing, "images": images, "qkv_weight": qkv_weight, "qkv_first": qkv_first, "qkv_second": qkv_second, "out_weight": out_weight, "out_first": out_first, "out_second": out_second, "up_weight": up_weight, "up_first": up_first, "up_second": up_second, "down_weight": down_weight, "down_first": down_first, "down_second": down_second, "affine": affine, "affine_first": affine_first, "affine_second": affine_second, "head_bias": head_bias, "head_first": head_first, "head_second": head_second, "inner_bias": inner_bias, "inner_first": inner_first, "inner_second": inner_second}


@jax.custom_vjp
def low(v):
    return lax.optimization_barrier(v.astype(jnp.bfloat16)).astype(jnp.float32)

@jax.custom_vjp
def summed_reverse_rule(v):
    return v

def low_keep(v):
    return (low(v), None)

def low_pass(kept, grad):
    return (grad,)

def back_keep(v):
    return (v, None)

def back_low(kept, grad):
    return (low(grad),)
low.defvjp(low_keep, low_pass)
summed_reverse_rule.defvjp(back_keep, back_low)
norm_epsilon = 1e-06
mask_value = -1000000000.0
sharpness_divisor = 50.0
loss_scale = 128.0
beta_first = 0.9
beta_second = 0.999
adam_epsilon = 1e-06
weight_decay = 0.01
learning_rate = 0.5
exact_arithmetic_mode = lax.Precision.HIGHEST

def both_round(values):
    return low(summed_reverse_rule(values))

def layer_norm(values, gain, shift):
    center = values - lax.optimization_barrier(jnp.mean(values, -1, keepdims=True))
    spread = lax.optimization_barrier(jnp.mean(center * center, -1, keepdims=True))
    return center * lax.rsqrt(spread + norm_epsilon) * gain + shift

def normalize(values):
    return values * lax.rsqrt(lax.optimization_barrier(jnp.sum(values * values, -1, keepdims=True)) + norm_epsilon)

def moments(weight, first, second, grad, decay):
    first_new = beta_first * first + (1.0 - beta_first) * grad
    second_new = beta_second * second + (1.0 - beta_second) * grad * grad
    first_hat = first_new / (1.0 - beta_first ** STEP)
    second_hat = second_new / (1.0 - beta_second ** STEP)
    update = first_hat / (jnp.sqrt(second_hat) + adam_epsilon) + decay * weight
    return (first_new, second_new, update)

def tensor_squares(qkv, out, upper, lower, affine, head, inner, replicas):
    return jnp.concatenate([lax.optimization_barrier(jnp.sum(qkv * qkv, (1, 2))), jnp.sum(out * out)[None], jnp.sum(upper * upper)[None], jnp.sum(lower * lower)[None], lax.optimization_barrier(jnp.sum(affine * affine, 1)) / replicas, lax.optimization_barrier(jnp.sum(head * head, 1)), jnp.sum(inner * inner)[None]])

def split_norms(norms):
    return (norms[0:3].reshape(3, 1, 1), norms[3], norms[4], norms[5], norms[6:12].reshape(6, 1), norms[12:14].reshape(2, 1), norms[14])

def scaled_step(weight, update, weight_norm, update_norm):
    return weight - learning_rate * weight_norm / update_norm * update

def pack_forward(params, tokens, segment):
    qkv_weight, out_weight, up_weight, down_weight, affine, head_bias, inner_bias = params
    packs = tokens.shape[0]
    normed = low(layer_norm(tokens, affine[0], affine[1]))
    projected = jnp.einsum('pld,kde->kple', normed, qkv_weight, precision=exact_arithmetic_mode)
    query = both_round(projected[0] + head_bias[0])
    keys = both_round(projected[1])
    values = both_round(projected[2] + head_bias[1])
    shape4 = (packs, PACK_LEN, HEADS, HD)
    scores = jnp.einsum('pqhe,pkhe->phqk', query.reshape(shape4), keys.reshape(shape4), precision=exact_arithmetic_mode) * HD ** (-0.5)
    scores = summed_reverse_rule(scores)
    same = segment[:, None, :, None] == segment[:, None, None, :]
    scores = jnp.where(same, scores, mask_value)
    top = lax.optimization_barrier(jnp.max(scores, -1, keepdims=True))
    expo = jnp.exp(scores - top)
    probs = low(expo / lax.optimization_barrier(jnp.sum(expo, -1, keepdims=True)))
    mixed = jnp.einsum('phqk,pkhe->pqhe', probs, values.reshape(shape4), precision=exact_arithmetic_mode).reshape(packs, PACK_LEN, D)
    mixed = both_round(mixed)
    attended = summed_reverse_rule(jnp.einsum('ple,de->pld', mixed, out_weight, precision=exact_arithmetic_mode))
    resid = tokens + attended + affine[4]
    second = low(layer_norm(resid, affine[2], affine[3]))
    upper = summed_reverse_rule(jnp.einsum('pld,df->plf', second, up_weight, precision=exact_arithmetic_mode) + inner_bias)
    hidden = low(jax.nn.gelu(upper))
    lowered = summed_reverse_rule(jnp.einsum('plf,df->pld', hidden, down_weight, precision=exact_arithmetic_mode))
    output = resid + lowered + affine[5]
    onehot = (segment[:, None, :] == jnp.arange(CAP, dtype=jnp.int32)[None, :, None]).astype(jnp.float32)
    counts = lax.optimization_barrier(jnp.sum(onehot, -1))
    pooled = jnp.einsum('pcl,pld->pcd', onehot, output, precision=exact_arithmetic_mode)
    return pooled / jnp.maximum(counts, 1.0)[..., None]

def reference(tokens, segment, pairing, images, qkv_weight, qkv_first, qkv_second, out_weight, out_first, out_second, up_weight, up_first, up_second, down_weight, down_first, down_second, affine, affine_first, affine_second, head_bias, head_first, head_second, inner_bias, inner_first, inner_second):
    weights = (qkv_weight, out_weight, up_weight, down_weight, affine, head_bias, inner_bias)
    picture_summed = low(normalize(images.astype(jnp.float32)))
    onehot = (segment[:, None, :] == jnp.arange(CAP, dtype=jnp.int32)[None, :, None]).astype(jnp.float32)
    counts = lax.optimization_barrier(jnp.sum(onehot, -1))
    live = (counts > 0).astype(jnp.float32).reshape(N_DP, PACK_DEV * CAP)
    targets = pairing.reshape(N_DP, PACK_DEV * CAP)
    grouped = segment.reshape(N_DP, PACK_DEV, PACK_LEN)

    def objective(params, inputs):
        rounded = jax.tree.map(low, params)

        def group(encoder_layer_unit):
            return pack_forward(rounded, encoder_layer_unit[0], encoder_layer_unit[1])
        pooled = lax.map(jax.checkpoint(group), (inputs.reshape(N_DP, PACK_DEV, PACK_LEN, D), grouped))
        sentence_words = low(normalize(pooled.reshape(N_DP, PACK_DEV * CAP, D)))

        def cross(encoder_layer_unit):
            similarity_grid = summed_reverse_rule(sharpness_divisor * jnp.dot(encoder_layer_unit[0], picture_summed.T, precision=exact_arithmetic_mode))
            top = lax.optimization_barrier(jnp.max(similarity_grid, -1, keepdims=True))
            log_sum = top[:, 0] + jnp.log(lax.optimization_barrier(jnp.sum(jnp.exp(similarity_grid - top), -1)))
            positive = jnp.take_along_axis(similarity_grid, encoder_layer_unit[1][:, None], 1)[:, 0]
            return log_sum - positive
        losses = lax.map(jax.checkpoint(cross), (sentence_words, targets))
        total = jnp.sum(live * losses)
        return (loss_scale * total, total)
    scaled, backward, total = jax.vjp(objective, weights, tokens.astype(jnp.float32), has_aux=True)
    grads, grad_input = backward(jnp.ones((), scaled.dtype))
    mean_loss = total / float(PACKS * CAP)
    firsts = (qkv_first, out_first, up_first, down_first, affine_first, head_first, inner_first)
    seconds = (qkv_second, out_second, up_second, down_second, affine_second, head_second, inner_second)
    decays = (weight_decay, weight_decay, weight_decay, weight_decay, 0.0, 0.0, 0.0)
    parts = [moments(weights[index], firsts[index], seconds[index], grads[index], decays[index]) for index in range(7)]
    updates = [packed_sequence_slice[2] for packed_sequence_slice in parts]
    weight_norm = jnp.sqrt(tensor_squares(*weights, 1.0))
    update_norm = jnp.sqrt(tensor_squares(*updates, 1.0))
    weight_split = split_norms(weight_norm)
    update_split = split_norms(update_norm)
    news = [scaled_step(weights[index], updates[index], weight_split[index], update_split[index]) for index in range(7)]
    return (mean_loss, grad_input, news[0], parts[0][0], parts[0][1], news[1], parts[1][0], parts[1][1], news[2], parts[2][0], parts[2][1], news[3], parts[3][0], parts[3][1], news[4], parts[4][0], parts[4][1], news[5], parts[5][0], parts[5][1], news[6], parts[6][0], parts[6][1], jnp.stack([weight_norm, update_norm]))
```

```python
import functools

import jax
import jax.numpy as jnp
from jax import lax
from jax.experimental import pallas as pl
from jax.experimental.pallas import tpu as pltpu
from jax.sharding import PartitionSpec as P

HD = 64
STEP = 10


norm_epsilon = 1e-06
mask_value = -1000000000.0
sharpness_divisor = 50.0
loss_scale = 128.0
beta_first = 0.9
beta_second = 0.999
adam_epsilon = 1e-06
weight_decay = 0.01
learning_rate = 0.5
exact_arithmetic_mode = lax.Precision.HIGHEST


def layer_norm(values, gain, shift):
    center = values - jnp.mean(values, -1, keepdims=True)
    spread = jnp.mean(center * center, -1, keepdims=True)
    return center * lax.rsqrt(spread + norm_epsilon) * gain + shift


def normalize(values):
    return values * lax.rsqrt(jnp.sum(values * values, -1, keepdims=True) + norm_epsilon)


def summation_axes_spec(left, right, left_dim, right_dim):
    return lax.dot_general(
        left, right, (((left_dim,), (right_dim,)), ((), ())), preferred_element_type=jnp.float32
    )


def moments(weight, first, second, grad, decay):
    first_new = beta_first * first + (1.0 - beta_first) * grad
    second_new = beta_second * second + (1.0 - beta_second) * grad * grad
    first_hat = first_new / (1.0 - beta_first**STEP)
    second_hat = second_new / (1.0 - beta_second**STEP)
    update = first_hat / (jnp.sqrt(second_hat) + adam_epsilon) + decay * weight
    return (first_new, second_new, update)


def tensor_squares(qkv, out, upper, lower, affine, head, inner, replicas):
    return jnp.concatenate(
        [
            jnp.sum(qkv * qkv, (1, 2)),
            jnp.sum(out * out)[None],
            jnp.sum(upper * upper)[None],
            jnp.sum(lower * lower)[None],
            jnp.sum(affine * affine, 1) / replicas,
            jnp.sum(head * head, 1),
            jnp.sum(inner * inner)[None],
        ]
    )


def split_norms(norms):
    return (
        norms[0:3].reshape(3, 1, 1),
        norms[3],
        norms[4],
        norms[5],
        norms[6:12].reshape(6, 1),
        norms[12:14].reshape(2, 1),
        norms[14],
    )


def scaled_step(weight, update, weight_norm, update_norm):
    return weight - learning_rate * weight_norm / update_norm * update


MESH = pl.DeviceIdType.MESH

class Place:
    def __init__(self, depth):
        self.depth = depth
        dp = lax.axis_index("dp")
        self.x = lax.axis_index("mp")
        self.z, self.y, self.c = dp // 4, (dp // 2) % 2, dp % 2
    def at(self, z, y, c, x):
        return ((z * 2 + y) * 2 + c, x)
    def over_x(self): return self.at(self.z, self.y, self.c, 1 - self.x)
    def over_y(self): return self.at(self.z, 1 - self.y, self.c, self.x)
    def over_c(self): return self.at(self.z, self.y, 1 - self.c, self.x)
    def over_z(self, k): return self.at(lax.rem(self.z + k, self.depth), self.y, self.c, self.x)
    def partners(self):
        return [self.over_x(), self.over_y(), self.over_c()] + [self.over_z(k) for k in range(1, self.depth)]
    def barrier(self):
        sem = pltpu.get_barrier_semaphore()
        peers = self.partners()
        for p in peers:
            pl.semaphore_signal(sem, inc=1, device_id=p, device_id_type=MESH)
        pl.semaphore_wait(sem, len(peers))

class Wire:
    def __init__(self, send, recv):
        self.send, self.recv, self.used = send, recv, 0
        self.started = []
    def start(self, src, dst, device):
        i = self.used; self.used += 1
        cp = pltpu.make_async_remote_copy(src_ref=src, dst_ref=dst, send_sem=self.send.at[i], recv_sem=self.recv.at[i], device_id=device, device_id_type=MESH)
        cp.start()
        self.started.append(cp)
        return cp

def gather_z(place, wire, items):
    out = []
    for full, own, u, n in items:
        for k in range(1, place.depth):
            out.append(wire.start(own.at[pl.ds(u, n)], full.at[place.x, pl.ds(u, n), place.z, place.y, place.c], place.over_z(k)))
    return out

def gather_one(place, wire, items):
    out = []
    h = place.depth // 2
    for full, own, u, n in items:
        r = full.at[place.x, pl.ds(u, n), pl.ds(0, h), place.y, place.c]
        out.append(wire.start(r, r, place.over_x()))
        r = full.at[place.x, pl.ds(u, n), pl.ds(h, place.depth - h), place.y, place.c]
        out.append(wire.start(r, r, place.over_y()))
    return out

def gather_two(place, wire, items):
    out = []
    h = place.depth // 2
    for full, own, u, n in items:
        r = full.at[:, pl.ds(u, n), pl.ds(0, h), place.y, place.c]
        out.append(wire.start(r, r, place.over_y()))
        r = full.at[place.x, pl.ds(u, n), pl.ds(h, place.depth - h), :, place.c]
        out.append(wire.start(r, r, place.over_x()))
    return out

def gather_core(place, wire, items):
    out = []
    for full, own, u, n in items:
        r = full.at[:, pl.ds(u, n), :, :, place.c]
        out.append(wire.start(r, r, place.over_c()))
    return out

def wait_recv(cps):
    for c in cps: c.wait_recv()

def gather_steps(place, wire, groups, ahead=2):
    G = len(groups)
    zs, ones, twos, cores = {}, {}, {}, {}
    for g in range(min(ahead, G)):
        zs[g] = gather_z(place, wire, groups[g])
    for t in range(G + 3):
        if t < G:
            wait_recv(zs[t])
            ones[t] = gather_one(place, wire, groups[t])
            if t + ahead < G:
                zs[t + ahead] = gather_z(place, wire, groups[t + ahead])
        if 0 <= t - 1 < G:
            wait_recv(ones[t - 1]); twos[t - 1] = gather_two(place, wire, groups[t - 1])
        if 0 <= t - 2 < G:
            wait_recv(twos[t - 2]); cores[t - 2] = gather_core(place, wire, groups[t - 2])
        if 0 <= t - 3 < G:
            wait_recv(cores[t - 3]); yield t - 3

def add_blocks(dst, src, count):
    def step(i, carry):
        d, s = dst(i), src(i)
        d[...] = (d[...].astype(jnp.float32) + s[...].astype(jnp.float32)).astype(d.dtype)
        return carry
    lax.fori_loop(0, count, step, 0)

class Reduce:
    def __init__(self, place, wire, part, from_core, one_a, one_b, two_a, two_b, from_z, total):
        self.p, self.wire, self.part = place, wire, part
        self.from_core, self.one_a, self.one_b, self.two_a, self.two_b, self.from_z, self.total = from_core, one_a, one_b, two_a, two_b, from_z, total
        self.h = place.depth // 2
        self.flight = {}
    def core(self, u, n):
        p = self.p
        self.flight["c", u] = [self.wire.start(self.part.at[:, pl.ds(u, n), :, :, 1 - p.c], self.from_core.at[:, pl.ds(u, n)], p.over_c())]
    def one(self, u, n):
        p, h, Z = self.p, self.h, self.p.depth
        wait_recv(self.flight["c", u])
        def idx(i):
            y = i % 2; z = (i // 2) % Z; k = (i // (2 * Z)) % n; x = i // (2 * Z * n)
            return x, u + k, z, y
        def dst(i):
            x, k, z, y = idx(i); return self.part.at[x, k, z, y, p.c]
        def src(i):
            x, k, z, y = idx(i); return self.from_core.at[x, k, z, y]
        add_blocks(dst, src, 2 * n * Z * 2)
        us = pl.ds(u, n)
        self.flight["1", u] = [
            self.wire.start(self.part.at[1 - p.x, us, pl.ds(0, h), :, p.c], self.one_a.at[us], p.over_x()),
            self.wire.start(self.part.at[:, us, pl.ds(h, Z - h), 1 - p.y, p.c], self.one_b.at[:, us], p.over_y())]
    def two(self, u, n):
        p, h, Z = self.p, self.h, self.p.depth
        wait_recv(self.flight["1", u])
        def ia(i): return u + i // (2 * h), (i // 2) % h, i % 2
        def da(i):
            k, z, y = ia(i); return self.part.at[p.x, k, z, y, p.c]
        def sa(i):
            k, z, y = ia(i); return self.one_a.at[k, z, y]
        add_blocks(da, sa, n * h * 2)
        def ib(i): return i // (n * (Z - h)), u + (i // (Z - h)) % n, i % (Z - h)
        def db(i):
            x, k, z = ib(i); return self.part.at[x, k, h + z, p.y, p.c]
        def sb(i):
            x, k, z = ib(i); return self.one_b.at[x, k, z]
        add_blocks(db, sb, 2 * n * (Z - h))
        us = pl.ds(u, n)
        self.flight["2", u] = [
            self.wire.start(self.part.at[p.x, us, pl.ds(0, h), 1 - p.y, p.c], self.two_a.at[us], p.over_y()),
            self.wire.start(self.part.at[1 - p.x, us, pl.ds(h, Z - h), p.y, p.c], self.two_b.at[us], p.over_x())]
    def far(self, u, n):
        p, h, Z = self.p, self.h, self.p.depth
        wait_recv(self.flight["2", u])
        def da(i): return self.part.at[p.x, u + i // h, i % h, p.y, p.c]
        def sa(i): return self.two_a.at[u + i // h, i % h]
        add_blocks(da, sa, n * h)
        w = Z - h
        def db(i): return self.part.at[p.x, u + i // w, h + i % w, p.y, p.c]
        def sb(i): return self.two_b.at[u + i // w, i % w]
        add_blocks(db, sb, n * w)
        us = pl.ds(u, n)
        self.flight["z", u] = [
            self.wire.start(self.part.at[p.x, us, lax.rem(p.z + k, Z), p.y, p.c], self.from_z.at[k - 1, us], p.over_z(k)) for k in range(1, Z)]
    def last(self, u, n):
        p, Z = self.p, self.p.depth
        wait_recv(self.flight["z", u])
        def step(i, carry):
            k = u + i
            t = self.part[p.x, k, p.z, p.y, p.c].astype(jnp.float32)
            for j in range(Z - 1):
                t = t + self.from_z[j, k].astype(jnp.float32)
            self.total[k] = t
            return carry
        lax.fori_loop(0, n, step, 0)

class SumAll:
    def __init__(self, place, wire, own, room):
        self.p, self.wire, self.own, self.room = place, wire, own, room
    def start(self, stage):
        p = self.p
        if stage < 3:
            device = (p.over_c, p.over_x, p.over_y)[stage]()
            self.flight = [self.wire.start(self.own, self.room.at[stage], device)]
        else:
            self.flight = [self.wire.start(self.own, self.room.at[3 + p.z], p.over_z(k)) for k in range(1, p.depth)]
    def finish(self, stage):
        p = self.p
        wait_recv(self.flight)
        for c in self.flight: c.wait_send()
        if stage < 3:
            self.own[...] = self.own[...] + self.room[stage]
        else:
            self.room[3 + p.z] = self.own[...]
            t = self.room[3]
            for z in range(1, p.depth): t = t + self.room[3 + z]
            self.own[...] = t


def gather_kernel(depth, own_ref, image_ref, small_ref, full_ref, images_ref, smalls_ref, send, recv, local):
    place = Place(depth)
    place.barrier()
    wire = Wire(send, recv)
    pairs = [(full_ref, own_ref), (images_ref, image_ref), (smalls_ref, small_ref)]
    copies = []
    for j, (full, own) in enumerate(pairs):
        copies.append(pltpu.make_async_copy(own, full.at[place.x, :, place.z, place.y, place.c], local.at[j]))
        copies[-1].start()
    units = own_ref.shape[0]
    groups = [[(smalls_ref, small_ref, 0, 1), (full_ref, own_ref, 0, 1)]]
    groups += [[(full_ref, own_ref, u, 1)] for u in range(1, units)]
    groups += [[(images_ref, image_ref, 0, 1)]]
    for copy in copies:
        copy.wait()
    for _ in gather_steps(place, wire, groups):
        pass
    for copy in wire.started:
        copy.wait_send()


def gather_all(depth, own, image, small):
    def whole(a):
        return jax.ShapeDtypeStruct((2, a.shape[0], depth, 2, 2) + a.shape[1:], a.dtype)
    count = (own.shape[0] + 2) * (depth - 1 + 5)
    return pl.pallas_call(
        functools.partial(gather_kernel, depth),
        out_shape=(whole(own), whole(image), whole(small)),
        in_specs=[pl.BlockSpec(memory_space=pltpu.VMEM)] * 3,
        out_specs=[pl.BlockSpec(memory_space=pl.ANY)] * 3,
        scratch_shapes=[pltpu.SemaphoreType.DMA((count,)), pltpu.SemaphoreType.DMA((count,)), pltpu.SemaphoreType.DMA((3,))],
        compiler_params=pltpu.CompilerParams(collective_id=1, has_side_effects=True, vmem_limit_bytes=56 << 20),
        name="gather_weights",
    )(own, image, small)


def reduce_kernel(depth, part_ref, small_ref, total_ref, sums_ref, part, from_core, one_a, one_b, two_a, two_b, from_z, room, send, recv, local):
    place = Place(depth)
    place.barrier()
    wire = Wire(send, recv)
    reduce = Reduce(place, wire, part, from_core, one_a, one_b, two_a, two_b, from_z, total_ref)
    units = part.shape[1]
    copies = []
    for u in range(units):
        copies.append(pltpu.make_async_copy(part_ref.at[:, pl.ds(u, 1)], part.at[:, pl.ds(u, 1)], local.at[u]))
        copies[-1].start()
    sums_ref[...] = small_ref[...]
    sums = SumAll(place, wire, sums_ref, room)
    for t in range(units + 4):
        if t < units:
            copies[t].wait()
            reduce.core(t, 1)
        if t < 4:
            sums.start(t)
        if 0 <= t - 1 < units:
            reduce.one(t - 1, 1)
        if 0 <= t - 2 < units:
            reduce.two(t - 2, 1)
        if 0 <= t - 3 < units:
            reduce.far(t - 3, 1)
        if 0 <= t - 4 < units:
            reduce.last(t - 4, 1)
        if t < 4:
            sums.finish(t)
    for flight in reduce.flight.values():
        for copy in flight:
            copy.wait_send()


def reduce_all(depth, part, small):
    _, units, _, _, _, rows, width = part.shape
    h = depth // 2
    low = [
        part.shape, (2, units, depth, 2, rows, width), (units, h, 2, rows, width), (2, units, depth - h, rows, width),
        (units, h, rows, width), (units, depth - h, rows, width), (depth - 1, units, rows, width),
    ]
    count = units * (5 + depth - 1) + 3 + depth - 1
    vmem = pl.BlockSpec(memory_space=pltpu.VMEM)
    return pl.pallas_call(
        functools.partial(reduce_kernel, depth),
        out_shape=(jax.ShapeDtypeStruct((units, rows, width), jnp.float32), jax.ShapeDtypeStruct(small.shape, jnp.float32)),
        in_specs=[pl.BlockSpec(memory_space=pl.ANY), vmem],
        out_specs=[vmem, vmem],
        scratch_shapes=[pltpu.VMEM(s, jnp.bfloat16) for s in low]
        + [pltpu.VMEM((3 + depth,) + small.shape, jnp.float32), pltpu.SemaphoreType.DMA((count,)), pltpu.SemaphoreType.DMA((count,)), pltpu.SemaphoreType.DMA((units,))],
        compiler_params=pltpu.CompilerParams(collective_id=2, has_side_effects=True, vmem_limit_bytes=56 << 20),
        name="reduce_gradients",
    )(part, small)


def sum_kernel(depth, own_ref, sum_ref, room, send, recv):
    place = Place(depth)
    place.barrier()
    sum_ref[...] = own_ref[...]
    sums = SumAll(place, Wire(send, recv), sum_ref, room)
    for stage in range(4):
        sums.start(stage)
        sums.finish(stage)


def sum_all(depth, own):
    vmem = pl.BlockSpec(memory_space=pltpu.VMEM)
    return pl.pallas_call(
        functools.partial(sum_kernel, depth),
        out_shape=jax.ShapeDtypeStruct(own.shape, jnp.float32),
        in_specs=[vmem],
        out_specs=vmem,
        scratch_shapes=[pltpu.VMEM((3 + depth,) + own.shape, jnp.float32), pltpu.SemaphoreType.DMA((3 + depth - 1,)), pltpu.SemaphoreType.DMA((3 + depth - 1,))],
        compiler_params=pltpu.CompilerParams(collective_id=3, has_side_effects=True),
        name="sum_squares",
    )(own)


def body_near(depth, *arrays):
    (
        tokens, segment, pairing, images,
        qkv_weight, qkv_first, qkv_second, out_weight, out_first, out_second,
        up_weight, up_first, up_second, down_weight, down_first, down_second,
        affine, affine_first, affine_second, head_bias, head_first, head_second,
        inner_bias, inner_first, inner_second,
    ) = arrays
    bf16 = jnp.bfloat16
    mp = lax.axis_index("mp")
    dp = lax.axis_index("dp")
    packs, length, width = tokens.shape
    mine = packs // 2
    rows = mine * length
    share, half = qkv_weight.shape[1:]
    blocks = up_weight.shape[1] // half
    dp_size = 4 * depth

    def cut(weight):
        return weight.reshape(share, blocks, half).transpose(1, 0, 2)

    own = jnp.concatenate([qkv_weight, out_weight[None], cut(up_weight), cut(down_weight)]).astype(bf16)
    image = lax.dynamic_slice_in_dim(images, mp * (images.shape[0] // 2), images.shape[0] // 2).astype(jnp.float32)
    image = normalize(image).astype(bf16)[None]
    small = jnp.concatenate([affine.reshape(-1), head_bias.reshape(-1), inner_bias])
    small = jnp.pad(small, (0, 1024 - small.shape[0])).reshape(1, 8, 128)
    full, images_full, smalls = gather_all(depth, own, image, small)
    full = full.reshape(2, 4 + 2 * blocks, dp_size * share, half)
    images_full = images_full.reshape(-1, width)
    smalls = smalls.reshape(2, dp_size, 1024)
    n_affine, n_head = affine.size, head_bias.size

    def rounded(a):
        return a.astype(bf16).astype(jnp.float32)

    affine_wide = rounded(smalls[0, :, :n_affine].reshape(dp_size, 6, -1).transpose(1, 0, 2).reshape(6, width))
    head_wide = rounded(smalls[:, :, n_affine : n_affine + n_head].reshape(2, dp_size, 2, -1).transpose(2, 0, 1, 3).reshape(2, width))
    inner_wide = rounded(smalls[:, :, n_affine + n_head : n_affine + n_head + inner_bias.size].reshape(-1))

    def whole(u, n):
        return full[:, u : u + n].transpose(2, 0, 1, 3).reshape(width, -1)

    qkv_full = jnp.stack([whole(0, 1), whole(1, 1), whole(2, 1)])
    out_full, up_full, down_full = whole(3, 1), whole(4, blocks), whole(4 + blocks, blocks)
    tokens = lax.dynamic_slice_in_dim(tokens, mp * mine, mine)
    segment = lax.dynamic_slice_in_dim(segment, mp * mine, mine)
    pairing = lax.dynamic_slice_in_dim(pairing, mp * mine, mine)
    heads = width // HD
    shape4 = (mine, length, heads, HD)
    root_scale = HD ** (-0.5)
    inputs = tokens.reshape(rows, width).astype(jnp.float32)
    normed_one = layer_norm(inputs, affine_wide[0], affine_wide[1]).astype(bf16)
    projected = jnp.einsum("td,kde->kte", normed_one, qkv_full, preferred_element_type=jnp.float32)
    query = (projected[0] + head_wide[0]).astype(bf16).reshape(shape4)
    keys = projected[1].astype(bf16).reshape(shape4)
    values = (projected[2] + head_wide[1]).astype(bf16).reshape(shape4)
    same = segment[:, None, :, None] == segment[:, None, None, :]
    raw = jnp.einsum("pqhe,pkhe->phqk", query, keys, preferred_element_type=jnp.float32) * root_scale
    scores = jnp.where(same, raw, mask_value)
    top = jnp.max(scores, -1, keepdims=True)
    log_total = top + jnp.log(jnp.sum(jnp.exp(scores - top), -1, keepdims=True))
    probs_wide = jnp.exp(scores - log_total)
    probs = probs_wide.astype(bf16)
    mixed = jnp.einsum("phqk,pkhe->pqhe", probs, values, preferred_element_type=jnp.float32)
    mixed = mixed.reshape(rows, width).astype(bf16)
    resid = inputs + summation_axes_spec(mixed, out_full, 1, 1) + affine_wide[4]
    normed_two = layer_norm(resid, affine_wide[2], affine_wide[3]).astype(bf16)
    upper = jnp.dot(normed_two, up_full, preferred_element_type=jnp.float32) + inner_wide
    activated, gelu_back = jax.vjp(jax.nn.gelu, upper)
    hidden = activated.astype(bf16)
    output = resid + summation_axes_spec(hidden, down_full, 1, 1) + affine_wide[5]
    slots = pairing.shape[1]
    onehot = (segment[:, None, :] == jnp.arange(slots, dtype=jnp.int32)[None, :, None]).astype(jnp.float32)
    counts = jnp.sum(onehot, -1)
    divisor = jnp.maximum(counts, 1.0)[..., None]
    pooled = jnp.einsum("pcl,pld->pcd", onehot, output.reshape(mine, length, width), precision=exact_arithmetic_mode) / divisor
    flat = pooled.reshape(mine * slots, width)
    caption_wide, normalize_back = jax.vjp(normalize, flat)
    caption = caption_wide.astype(bf16)
    live = (counts > 0).reshape(-1).astype(jnp.float32)
    target = pairing.reshape(-1)
    similarity = sharpness_divisor * summation_axes_spec(caption, images_full, 1, 1)
    best = jnp.max(similarity, 1)
    log_sum = best + jnp.log(jnp.sum(jnp.exp(similarity - best[:, None]), 1))
    place = jnp.arange(similarity.shape[1], dtype=jnp.int32)
    per = images.shape[0] // 2
    owner = place // per
    column = (owner % dp_size) * (2 * per) + (owner // dp_size) * per + place % per
    hit = (target[:, None] == column[None, :]).astype(jnp.float32)
    positive = jnp.sum(hit * similarity, 1)
    logit_gradient = (loss_scale * live[:, None] * (jnp.exp(similarity - log_sum[:, None]) - hit)).astype(bf16)
    caption_grad = sharpness_divisor * jnp.dot(logit_gradient, images_full, preferred_element_type=jnp.float32)
    loss_local = jnp.sum(live * (log_sum - positive))
    (grad_flat,) = normalize_back(caption_grad)
    grad_pooled = grad_flat.reshape(mine, slots, width) / divisor
    grad_output = jnp.einsum("pcl,pcd->pld", onehot, grad_pooled, precision=exact_arithmetic_mode).reshape(rows, width)
    grad_output_low = grad_output.astype(bf16)
    down_grad = summation_axes_spec(grad_output_low, hidden, 0, 0).astype(bf16)
    grad_hidden = jnp.dot(grad_output_low, down_full, preferred_element_type=jnp.float32)
    (grad_upper,) = gelu_back(grad_hidden)
    grad_upper = grad_upper.astype(bf16)
    inner_grad = jnp.sum(grad_upper.astype(jnp.float32), 0)
    up_grad = summation_axes_spec(normed_two, grad_upper, 0, 0).astype(bf16)
    grad_two = summation_axes_spec(grad_upper, up_full, 1, 1)
    _, norm_two_back = jax.vjp(layer_norm, resid, affine_wide[2], affine_wide[3])
    grad_resid_norm, gain_two_grad, shift_two_grad = norm_two_back(grad_two)
    grad_resid = grad_output + grad_resid_norm
    grad_resid_low = grad_resid.astype(bf16)
    out_grad = summation_axes_spec(grad_resid_low, mixed, 0, 0).astype(bf16)
    grad_mixed = jnp.dot(grad_resid_low, out_full, preferred_element_type=jnp.float32)
    grad_mixed = grad_mixed.astype(bf16).reshape(shape4)
    grad_value = jnp.einsum("phqk,pqhe->pkhe", probs, grad_mixed, preferred_element_type=jnp.float32)
    grad_probs = jnp.einsum("pqhe,pkhe->phqk", grad_mixed, values, preferred_element_type=jnp.float32)
    grad_scores = probs_wide * (grad_probs - jnp.sum(probs_wide * grad_probs, -1, keepdims=True))
    grad_scores = grad_scores.astype(bf16)
    grad_query = jnp.einsum("phqk,pkhe->pqhe", grad_scores, keys, preferred_element_type=jnp.float32) * root_scale
    grad_key = jnp.einsum("phqk,pqhe->pkhe", grad_scores, query, preferred_element_type=jnp.float32) * root_scale
    grad_qkv = jnp.stack([grad_query, grad_key, grad_value]).reshape(3, rows, width).astype(bf16)
    head_grad = jnp.stack([jnp.sum(grad_qkv[0].astype(jnp.float32), 0), jnp.sum(grad_qkv[2].astype(jnp.float32), 0)])
    qkv_grad = jnp.einsum("td,kte->kde", normed_one, grad_qkv, preferred_element_type=jnp.float32).astype(bf16)
    grad_one = jnp.einsum("kte,kde->td", grad_qkv, qkv_full, preferred_element_type=jnp.float32)
    _, norm_one_back = jax.vjp(layer_norm, inputs, affine_wide[0], affine_wide[1])
    grad_input_norm, gain_one_grad, shift_one_grad = norm_one_back(grad_one)
    grad_input = (grad_resid + grad_input_norm).reshape(mine, length, width).astype(bf16)
    grad_input = lax.all_gather(grad_input, "mp", axis=0, tiled=True).astype(jnp.float32)
    affine_grad = jnp.stack([gain_one_grad, shift_one_grad, gain_two_grad, shift_two_grad, jnp.sum(grad_resid, 0), jnp.sum(grad_output, 0)])
    loss_row = jnp.zeros((1, width), jnp.float32).at[0, 0].set(loss_local)
    small_grad = jnp.concatenate([affine_grad, head_grad, inner_grad.reshape(-1, width), loss_row, jnp.zeros((3, width), jnp.float32)])

    def parts(grad, n):
        return grad.reshape(dp_size, share, 2, n, half).transpose(2, 3, 0, 1, 4)

    part = jnp.concatenate([parts(qkv_grad[0], 1), parts(qkv_grad[1], 1), parts(qkv_grad[2], 1), parts(out_grad, 1), parts(up_grad, blocks), parts(down_grad, blocks)], 1)
    part = part.reshape(2, 4 + 2 * blocks, depth, 2, 2, share, half)
    total, small_sum = reduce_all(depth, part, small_grad)

    def uncut(a):
        return a.transpose(1, 0, 2).reshape(share, -1)

    def lane(a, n):
        return lax.dynamic_slice_in_dim(a, dp * n, n, a.ndim - 1)

    inner_sum = small_sum[8 : 8 + inner_grad.shape[0] // width].reshape(-1)
    head_step, inner_step = head_bias.shape[1], inner_bias.shape[0]
    grads = (
        total[0:3], total[3], uncut(total[4 : 4 + blocks]), uncut(total[4 + blocks :]),
        lane(small_sum[0:6], affine.shape[1]),
        lax.dynamic_slice_in_dim(small_sum[6:8], (mp * dp_size + dp) * head_step, head_step, 1),
        lax.dynamic_slice_in_dim(inner_sum, (mp * dp_size + dp) * inner_step, inner_step, 0),
    )
    mean_loss = small_sum[8 + inner_grad.shape[0] // width, 0] / float(packs * slots * dp_size)
    weights = (qkv_weight, out_weight, up_weight, down_weight, affine, head_bias, inner_bias)
    firsts = (qkv_first, out_first, up_first, down_first, affine_first, head_first, inner_first)
    seconds = (qkv_second, out_second, up_second, down_second, affine_second, head_second, inner_second)
    decays = (weight_decay, weight_decay, weight_decay, weight_decay, 0.0, 0.0, 0.0)
    steps = [moments(weights[i], firsts[i], seconds[i], grads[i], decays[i]) for i in range(7)]
    updates = [s[2] for s in steps]
    squares = jnp.stack([tensor_squares(*weights, 2.0), tensor_squares(*updates, 2.0)])
    squares = sum_all(depth, jnp.pad(squares, ((0, 6), (0, 113))))
    norms = jnp.sqrt(squares[0:2, 0:15])
    weight_split, update_split = split_norms(norms[0]), split_norms(norms[1])
    results = [mean_loss, grad_input]
    for i in range(7):
        results += [scaled_step(weights[i], updates[i], weight_split[i], update_split[i]), steps[i][0], steps[i][1]]
    return (*results, norms)


def body(
    tokens,
    segment,
    pairing,
    images,
    qkv_weight,
    qkv_first,
    qkv_second,
    out_weight,
    out_first,
    out_second,
    up_weight,
    up_first,
    up_second,
    down_weight,
    down_first,
    down_second,
    affine,
    affine_first,
    affine_second,
    head_bias,
    head_first,
    head_second,
    inner_bias,
    inner_first,
    inner_second,
):
    model_size = lax.axis_size("mp")
    packs, length, width = tokens.shape
    rows = packs * length
    qkv_full, out_full, up_full, down_full, affine_full, head_full, inner_full = (
        lax.all_gather(qkv_weight.astype(jnp.bfloat16), "dp", axis=1, tiled=True),
        lax.all_gather(out_weight.astype(jnp.bfloat16), "dp", axis=0, tiled=True),
        lax.all_gather(up_weight.astype(jnp.bfloat16), "dp", axis=0, tiled=True),
        lax.all_gather(down_weight.astype(jnp.bfloat16), "dp", axis=0, tiled=True),
        lax.all_gather(affine.astype(jnp.bfloat16), "dp", axis=1, tiled=True),
        lax.all_gather(head_bias.astype(jnp.bfloat16), "dp", axis=1, tiled=True),
        lax.all_gather(inner_bias.astype(jnp.bfloat16), "dp", axis=0, tiled=True),
    )
    affine_wide = affine_full.astype(jnp.float32)
    head_wide = head_full.astype(jnp.float32)
    inner_wide = inner_full.astype(jnp.float32)
    half = qkv_full.shape[2]
    local_heads = half // HD
    shape4 = (packs, length, local_heads, HD)
    root_scale = HD ** (-0.5)
    inputs = tokens.reshape(rows, width).astype(jnp.float32)
    normed_one = layer_norm(inputs, affine_wide[0], affine_wide[1]).astype(jnp.bfloat16)
    projected = jnp.einsum("td,kde->kte", normed_one, qkv_full, preferred_element_type=jnp.float32)
    query = (projected[0] + head_wide[0]).astype(jnp.bfloat16).reshape(shape4)
    keys = projected[1].astype(jnp.bfloat16).reshape(shape4)
    values = (projected[2] + head_wide[1]).astype(jnp.bfloat16).reshape(shape4)
    same = segment[:, None, :, None] == segment[:, None, None, :]

    def masked_scores():
        raw = (
            jnp.einsum("pqhe,pkhe->phqk", query, keys, preferred_element_type=jnp.float32)
            * root_scale
        )
        return jnp.where(same, raw, mask_value)

    scores = masked_scores()
    top = jnp.max(scores, -1, keepdims=True)
    log_total = top + jnp.log(jnp.sum(jnp.exp(scores - top), -1, keepdims=True))
    probs = jnp.exp(scores - log_total).astype(jnp.bfloat16)
    mixed = jnp.einsum("phqk,pkhe->pqhe", probs, values, preferred_element_type=jnp.float32)
    mixed = mixed.reshape(rows, half).astype(jnp.bfloat16)
    attended = lax.psum(summation_axes_spec(mixed, out_full, 1, 1), "mp")
    resid = inputs + attended + affine_wide[4]
    normed_two = layer_norm(resid, affine_wide[2], affine_wide[3]).astype(jnp.bfloat16)
    upper = jnp.dot(normed_two, up_full, preferred_element_type=jnp.float32) + inner_wide
    activated, gelu_back = jax.vjp(jax.nn.gelu, upper)
    hidden = activated.astype(jnp.bfloat16)
    lowered = lax.psum(
        summation_axes_spec(hidden, down_full, 1, 1).astype(jnp.bfloat16), "mp"
    ).astype(jnp.float32)
    output = resid + lowered + affine_wide[5]
    slots = pairing.shape[1]
    onehot = (segment[:, None, :] == jnp.arange(slots, dtype=jnp.int32)[None, :, None]).astype(
        jnp.float32
    )
    counts = jnp.sum(onehot, -1)
    divisor = jnp.maximum(counts, 1.0)[..., None]
    pooled = (
        jnp.einsum(
            "pcl,pld->pcd",
            onehot,
            output.reshape(packs, length, width),
            precision=exact_arithmetic_mode,
        )
        / divisor
    )
    flat = pooled.reshape(packs * slots, width)
    caption_wide, normalize_back = jax.vjp(normalize, flat)
    sentence_words = caption_wide.astype(jnp.bfloat16)
    live = (counts > 0).reshape(-1).astype(jnp.float32)
    target = pairing.reshape(-1)
    captions_count = flat.shape[0]
    slot_total = float(captions_count * lax.axis_size("dp"))
    picture_summed = normalize(images.astype(jnp.float32)).astype(jnp.bfloat16)

    def similarity(packed_sequence_slice):
        return sharpness_divisor * summation_axes_spec(sentence_words, packed_sequence_slice, 1, 1)

    score_packed_sequence_slice = lax.all_gather(picture_summed, "dp", axis=0, tiled=True)
    best = jnp.full((captions_count,), mask_value, jnp.float32)
    similarity_grid = similarity(score_packed_sequence_slice)
    new_best = jnp.maximum(best, jnp.max(similarity_grid, 1))
    total = jnp.sum(jnp.exp(similarity_grid - new_best[:, None]), 1)
    column = jnp.arange(score_packed_sequence_slice.shape[0], dtype=jnp.int32)
    hit = target[:, None] == column[None, :]
    positive = jnp.sum(jnp.where(hit, similarity_grid, 0.0), 1)
    best_all, total_all, positive = (new_best, total, positive)
    log_sum = best_all + jnp.log(total_all)
    grad_packed_sequence_slice = lax.all_gather(picture_summed, "dp", axis=0, tiled=True)
    similarity_grid = similarity(grad_packed_sequence_slice)
    column = jnp.arange(grad_packed_sequence_slice.shape[0], dtype=jnp.int32)
    hit = (target[:, None] == column[None, :]).astype(jnp.float32)
    logit_gradient = (
        loss_scale * live[:, None] * (jnp.exp(similarity_grid - log_sum[:, None]) - hit)
    ).astype(jnp.bfloat16)
    sentence_derivative = sharpness_divisor * jnp.dot(
        logit_gradient, grad_packed_sequence_slice, preferred_element_type=jnp.float32
    )
    cross = log_sum - positive
    loss_local = jnp.sum(live * cross)
    loss_total = lax.psum(loss_local, "dp")
    mean_loss = loss_total / slot_total
    (grad_flat,) = normalize_back(sentence_derivative)
    grad_pooled = grad_flat.reshape(packs, slots, width) / divisor
    grad_output = jnp.einsum(
        "pcl,pcd->pld", onehot, grad_pooled, precision=exact_arithmetic_mode
    ).reshape(rows, width)
    grad_output_low = grad_output.astype(jnp.bfloat16)
    down_grad = summation_axes_spec(grad_output_low, hidden, 0, 0)
    grad_hidden = jnp.dot(grad_output_low, down_full, preferred_element_type=jnp.float32)
    (grad_upper,) = gelu_back(grad_hidden)
    grad_upper = grad_upper.astype(jnp.bfloat16)
    inner_grad = jnp.sum(grad_upper.astype(jnp.float32), 0)
    up_grad = summation_axes_spec(normed_two, grad_upper, 0, 0)
    grad_two = lax.psum(
        summation_axes_spec(grad_upper, up_full, 1, 1).astype(jnp.bfloat16), "mp"
    ).astype(jnp.float32)
    _, norm_two_back = jax.vjp(layer_norm, resid, affine_wide[2], affine_wide[3])
    grad_resid_norm, gain_two_grad, shift_two_grad = norm_two_back(grad_two)
    grad_resid = grad_output + grad_resid_norm
    grad_resid_low = grad_resid.astype(jnp.bfloat16)
    out_grad = summation_axes_spec(grad_resid_low, mixed, 0, 0)
    grad_mixed = jnp.dot(grad_resid_low, out_full, preferred_element_type=jnp.float32)
    grad_mixed = grad_mixed.astype(jnp.bfloat16).reshape(shape4)
    probs_wide = jnp.exp(masked_scores() - log_total)
    probs_low = probs_wide.astype(jnp.bfloat16)
    grad_value = jnp.einsum(
        "phqk,pqhe->pkhe", probs_low, grad_mixed, preferred_element_type=jnp.float32
    )
    grad_probs = jnp.einsum(
        "pqhe,pkhe->phqk", grad_mixed, values, preferred_element_type=jnp.float32
    )
    grad_scores = probs_wide * (grad_probs - jnp.sum(probs_wide * grad_probs, -1, keepdims=True))
    grad_scores = grad_scores.astype(jnp.bfloat16)
    grad_query = (
        jnp.einsum("phqk,pkhe->pqhe", grad_scores, keys, preferred_element_type=jnp.float32)
        * root_scale
    )
    grad_key = (
        jnp.einsum("phqk,pqhe->pkhe", grad_scores, query, preferred_element_type=jnp.float32)
        * root_scale
    )
    grad_qkv = (
        jnp.stack([grad_query, grad_key, grad_value]).reshape(3, rows, half).astype(jnp.bfloat16)
    )
    head_grad = jnp.stack(
        [jnp.sum(grad_qkv[0].astype(jnp.float32), 0), jnp.sum(grad_qkv[2].astype(jnp.float32), 0)]
    )
    qkv_grad = jnp.einsum("td,kte->kde", normed_one, grad_qkv, preferred_element_type=jnp.float32)
    grad_one = lax.psum(
        jnp.einsum("kte,kde->td", grad_qkv, qkv_full, preferred_element_type=jnp.float32).astype(
            jnp.bfloat16
        ),
        "mp",
    ).astype(jnp.float32)
    _, norm_one_back = jax.vjp(layer_norm, inputs, affine_wide[0], affine_wide[1])
    grad_input_norm, gain_one_grad, shift_one_grad = norm_one_back(grad_one)
    grad_input = (grad_resid + grad_input_norm).reshape(packs, length, width)
    affine_grad = jnp.stack(
        [
            gain_one_grad,
            shift_one_grad,
            gain_two_grad,
            shift_two_grad,
            jnp.sum(grad_resid, 0),
            jnp.sum(grad_output, 0),
        ]
    )
    qkv_part, out_part, up_part, down_part, affine_part, head_part, inner_part = (
        lax.psum_scatter(qkv_grad, "dp", scatter_dimension=1, tiled=True),
        lax.psum_scatter(out_grad, "dp", scatter_dimension=0, tiled=True),
        lax.psum_scatter(up_grad, "dp", scatter_dimension=0, tiled=True),
        lax.psum_scatter(down_grad, "dp", scatter_dimension=0, tiled=True),
        lax.psum_scatter(affine_grad, "dp", scatter_dimension=1, tiled=True),
        lax.psum_scatter(head_grad, "dp", scatter_dimension=1, tiled=True),
        lax.psum_scatter(inner_grad, "dp", scatter_dimension=0, tiled=True),
    )
    weights = (qkv_weight, out_weight, up_weight, down_weight, affine, head_bias, inner_bias)
    firsts = (qkv_first, out_first, up_first, down_first, affine_first, head_first, inner_first)
    seconds = (
        qkv_second,
        out_second,
        up_second,
        down_second,
        affine_second,
        head_second,
        inner_second,
    )
    grads = (qkv_part, out_part, up_part, down_part, affine_part, head_part, inner_part)
    decays = (weight_decay, weight_decay, weight_decay, weight_decay, 0.0, 0.0, 0.0)
    parts = [
        moments(weights[index], firsts[index], seconds[index], grads[index], decays[index])
        for index in range(7)
    ]
    updates = [packed_sequence_slice[2] for packed_sequence_slice in parts]
    weight_squares = tensor_squares(*weights, float(model_size))
    update_squares = tensor_squares(*updates, float(model_size))
    weight_total, update_total = lax.psum((weight_squares, update_squares), ("dp", "mp"))
    weight_norm = jnp.sqrt(weight_total)
    update_norm = jnp.sqrt(update_total)
    weight_split = split_norms(weight_norm)
    update_split = split_norms(update_norm)
    news = [
        scaled_step(weights[index], updates[index], weight_split[index], update_split[index])
        for index in range(7)
    ]
    return (
        mean_loss,
        grad_input,
        news[0],
        parts[0][0],
        parts[0][1],
        news[1],
        parts[1][0],
        parts[1][1],
        news[2],
        parts[2][0],
        parts[2][1],
        news[3],
        parts[3][0],
        parts[3][1],
        news[4],
        parts[4][0],
        parts[4][1],
        news[5],
        parts[5][0],
        parts[5][1],
        news[6],
        parts[6][0],
        parts[6][1],
        jnp.stack([weight_norm, update_norm]),
    )


def solution(mesh):
    depth = mesh.shape["dp"] // 4
    fits = mesh.shape["mp"] == 2 and mesh.shape["dp"] % 8 == 0 and 768 // mesh.shape["dp"] % 16 == 0
    return jax.shard_map(
        functools.partial(body_near, depth) if fits else body,
        mesh=mesh,
        in_specs=(
            P("dp", None, None),
            P("dp", None),
            P("dp", None),
            P("dp", None),
            P(None, "dp", "mp"),
            P(None, "dp", "mp"),
            P(None, "dp", "mp"),
            P("dp", "mp"),
            P("dp", "mp"),
            P("dp", "mp"),
            P("dp", "mp"),
            P("dp", "mp"),
            P("dp", "mp"),
            P("dp", "mp"),
            P("dp", "mp"),
            P("dp", "mp"),
            P(None, "dp"),
            P(None, "dp"),
            P(None, "dp"),
            P(None, ("mp", "dp")),
            P(None, ("mp", "dp")),
            P(None, ("mp", "dp")),
            P(("mp", "dp")),
            P(("mp", "dp")),
            P(("mp", "dp")),
        ),
        out_specs=(
            P(),
            P("dp", None, None),
            P(None, "dp", "mp"),
            P(None, "dp", "mp"),
            P(None, "dp", "mp"),
            P("dp", "mp"),
            P("dp", "mp"),
            P("dp", "mp"),
            P("dp", "mp"),
            P("dp", "mp"),
            P("dp", "mp"),
            P("dp", "mp"),
            P("dp", "mp"),
            P("dp", "mp"),
            P(None, "dp"),
            P(None, "dp"),
            P(None, "dp"),
            P(None, ("mp", "dp")),
            P(None, ("mp", "dp")),
            P(None, ("mp", "dp")),
            P(("mp", "dp")),
            P(("mp", "dp")),
            P(("mp", "dp")),
            P(),
        ),
        check_vma=False,
    )
```

```python
import functools

import jax
import jax.numpy as jnp
from jax import lax
from jax.experimental import pallas as pl
from jax.experimental.pallas import tpu as pltpu
from jax.sharding import PartitionSpec as P

HD = 64
STEP = 10


norm_epsilon = 1e-06
mask_value = -1000000000.0
sharpness_divisor = 50.0
loss_scale = 128.0
beta_first = 0.9
beta_second = 0.999
adam_epsilon = 1e-06
weight_decay = 0.01
learning_rate = 0.5
exact_arithmetic_mode = lax.Precision.HIGHEST


def layer_norm(values, gain, shift):
    center = values - jnp.mean(values, -1, keepdims=True)
    spread = jnp.mean(center * center, -1, keepdims=True)
    return center * lax.rsqrt(spread + norm_epsilon) * gain + shift


def normalize(values):
    return values * lax.rsqrt(jnp.sum(values * values, -1, keepdims=True) + norm_epsilon)


def summation_axes_spec(left, right, left_dim, right_dim):
    return lax.dot_general(
        left, right, (((left_dim,), (right_dim,)), ((), ())), preferred_element_type=jnp.float32
    )


def moments(weight, first, second, grad, decay):
    first_new = beta_first * first + (1.0 - beta_first) * grad
    second_new = beta_second * second + (1.0 - beta_second) * grad * grad
    first_hat = first_new / (1.0 - beta_first**STEP)
    second_hat = second_new / (1.0 - beta_second**STEP)
    update = first_hat / (jnp.sqrt(second_hat) + adam_epsilon) + decay * weight
    return (first_new, second_new, update)


def tensor_squares(qkv, out, upper, lower, affine, head, inner, replicas):
    return jnp.concatenate(
        [
            jnp.sum(qkv * qkv, (1, 2)),
            jnp.sum(out * out)[None],
            jnp.sum(upper * upper)[None],
            jnp.sum(lower * lower)[None],
            jnp.sum(affine * affine, 1) / replicas,
            jnp.sum(head * head, 1),
            jnp.sum(inner * inner)[None],
        ]
    )


def split_norms(norms):
    return (
        norms[0:3].reshape(3, 1, 1),
        norms[3],
        norms[4],
        norms[5],
        norms[6:12].reshape(6, 1),
        norms[12:14].reshape(2, 1),
        norms[14],
    )


def scaled_step(weight, update, weight_norm, update_norm):
    return weight - learning_rate * weight_norm / update_norm * update


MESH = pl.DeviceIdType.MESH
f32 = jnp.float32
bf16 = jnp.bfloat16


class Place:
    def __init__(self, depth):
        self.depth = depth
        dp = lax.axis_index("dp")
        self.dp = dp
        self.x = lax.axis_index("mp")
        self.z, self.y, self.c = dp // 4, (dp // 2) % 2, dp % 2

    def at(self, z, y, c, x):
        return ((z * 2 + y) * 2 + c, x)

    def over_x(self):
        return self.at(self.z, self.y, self.c, 1 - self.x)

    def over_y(self):
        return self.at(self.z, 1 - self.y, self.c, self.x)

    def over_c(self):
        return self.at(self.z, self.y, 1 - self.c, self.x)

    def over_z(self, k):
        return self.at(lax.rem(self.z + k, self.depth), self.y, self.c, self.x)

    def barrier(self):
        sem = pltpu.get_barrier_semaphore()
        peers = [self.over_x(), self.over_y(), self.over_c()] + [self.over_z(k) for k in range(1, self.depth)]
        for peer in peers:
            pl.semaphore_signal(sem, inc=1, device_id=peer, device_id_type=MESH)
        pl.semaphore_wait(sem, len(peers))


class Wire:
    def __init__(self, send, recv):
        self.send, self.recv, self.used, self.open = send, recv, 0, []

    def start(self, src, dst, device):
        i = self.used
        self.used += 1
        copy = pltpu.make_async_remote_copy(
            src_ref=src, dst_ref=dst, send_sem=self.send.at[i], recv_sem=self.recv.at[i], device_id=device, device_id_type=MESH
        )
        copy.start()
        self.open.append(copy)
        return copy

    def close(self):
        for copy in self.open:
            copy.wait_send()
        self.open = []


def arrive(copies):
    for copy in copies:
        copy.wait_recv()


class Sheet:
    def __init__(self, full, u):
        self.full, self.u, self.half = full, u, full.shape[-1] // 2

    def part(self, z, y, c, x=None):
        lanes = pl.ds(0, 2 * self.half) if x is None else pl.ds(pl.multiple_of(x * self.half, 128), self.half)
        return self.full.at[self.u, z, y, c, :, lanes]


class Stack:
    def __init__(self, full):
        self.full = full

    def part(self, z, y, c, x=None):
        return self.full.at[z, y, c, slice(None) if x is None else x]


class Gather:
    def __init__(self, place, wire, items, ahead, lag):
        self.p, self.wire, self.items, self.ahead, self.lag = place, wire, items, ahead, lag
        self.flight = {}
        self.t = 0
        self.whole = -1
        for i in range(min(ahead, len(items))):
            self.far(i)

    def far(self, i):
        p, it = self.p, self.items[i]
        mine = it.part(p.z, p.y, p.c, p.x)
        self.flight["z", i] = [self.wire.start(mine, mine, p.over_z(k)) for k in range(1, p.depth)]

    def one(self, i):
        p, it, h = self.p, self.items[i], self.p.depth // 2
        arrive(self.flight["z", i])
        a = it.part(pl.ds(0, h), p.y, p.c, p.x)
        b = it.part(pl.ds(h, p.depth - h), p.y, p.c, p.x)
        self.flight["1", i] = [self.wire.start(a, a, p.over_x()), self.wire.start(b, b, p.over_y())]

    def two(self, i):
        p, it, h = self.p, self.items[i], self.p.depth // 2
        arrive(self.flight["1", i])
        a = it.part(pl.ds(0, h), p.y, p.c)
        b = it.part(pl.ds(h, p.depth - h), slice(None), p.c, p.x)
        self.flight["2", i] = [self.wire.start(a, a, p.over_y()), self.wire.start(b, b, p.over_x())]

    def core(self, i):
        p, it = self.p, self.items[i]
        arrive(self.flight["2", i])
        r = it.part(slice(None), slice(None), p.c)
        self.flight["c", i] = [self.wire.start(r, r, p.over_c())]

    def step(self):
        t, n, lag = self.t, len(self.items), self.lag
        if t < n:
            self.one(t)
            if t + self.ahead < n:
                self.far(t + self.ahead)
        if 0 <= t - lag < n:
            self.two(t - lag)
        if 0 <= t - 2 * lag < n:
            self.core(t - 2 * lag)
        if 0 <= t - 2 * lag - 1 < n:
            arrive(self.flight["c", t - 2 * lag - 1])
            self.whole = t - 2 * lag - 1
        self.t += 1

    def until(self, i):
        while self.whole < i:
            self.step()


def add_blocks(dst, src, count):
    def step(i, carry):
        (d, at), (s, of) = dst(i), src(i)
        d[at] = (d[at].astype(f32) + s[of].astype(f32)).astype(d.dtype)
        return carry

    lax.fori_loop(0, count, step, 0)


class Reduce:
    def __init__(self, place, wire, order, lag, free, part, from_core, one_a, one_b, two_a, two_b, from_z, total):
        self.p, self.wire, self.order, self.lag, self.free = place, wire, order, lag, free
        self.part, self.from_core, self.one_a, self.one_b = part, from_core, one_a, one_b
        self.two_a, self.two_b, self.from_z, self.total = two_a, two_b, from_z, total
        self.h = place.depth // 2
        self.half = part.shape[-1] // 2
        self.slots = from_core.shape[0]
        self.flight = {}
        self.t = 0

    def lanes(self, x):
        return pl.ds(pl.multiple_of(x * self.half, 128), self.half)

    def core(self, i):
        p, u = self.p, self.order[i]
        if i >= self.slots:
            pl.semaphore_wait(self.free, 1)
        self.flight["c", i] = [self.wire.start(self.part.at[u, :, :, 1 - p.c], self.from_core.at[i % self.slots], p.over_c())]

    def one(self, i):
        p, u, h, Z, part = self.p, self.order[i], self.h, self.p.depth, self.part
        arrive(self.flight["c", i])
        add_blocks(
            lambda j: (part, (u, j // 2, j % 2, p.c)),
            lambda j: (self.from_core, (i % self.slots, j // 2, j % 2)), 2 * Z,
        )
        if i + self.slots < len(self.order):
            pl.semaphore_signal(self.free, inc=1, device_id=p.over_c(), device_id_type=MESH)
        self.flight["1", i] = [
            self.wire.start(part.at[u, pl.ds(0, h), :, p.c, :, self.lanes(1 - p.x)], self.one_a.at[u], p.over_x()),
            self.wire.start(part.at[u, pl.ds(h, Z - h), 1 - p.y, p.c], self.one_b.at[u], p.over_y()),
        ]

    def two(self, i):
        p, u, h, Z, part = self.p, self.order[i], self.h, self.p.depth, self.part
        arrive(self.flight["1", i])
        mine = self.lanes(p.x)
        add_blocks(lambda j: (part, (u, j // 2, j % 2, p.c, slice(None), mine)), lambda j: (self.one_a, (u, j // 2, j % 2)), 2 * h)
        add_blocks(lambda j: (part, (u, h + j, p.y, p.c)), lambda j: (self.one_b, (u, j)), Z - h)
        self.flight["2", i] = [
            self.wire.start(part.at[u, pl.ds(0, h), 1 - p.y, p.c, :, mine], self.two_a.at[u], p.over_y()),
            self.wire.start(part.at[u, pl.ds(h, Z - h), p.y, p.c, :, self.lanes(1 - p.x)], self.two_b.at[u], p.over_x()),
        ]

    def far(self, i):
        p, u, h, Z, part = self.p, self.order[i], self.h, self.p.depth, self.part
        arrive(self.flight["2", i])
        mine = self.lanes(p.x)
        add_blocks(lambda j: (part, (u, j, p.y, p.c, slice(None), mine)), lambda j: (self.two_a, (u, j)), h)
        add_blocks(lambda j: (part, (u, h + j, p.y, p.c, slice(None), mine)), lambda j: (self.two_b, (u, j)), Z - h)
        self.flight["z", i] = [
            self.wire.start(part.at[u, lax.rem(p.z + k, Z), p.y, p.c, :, mine], self.from_z.at[k - 1, u], p.over_z(k))
            for k in range(1, Z)
        ]

    def last(self, i):
        p, u = self.p, self.order[i]
        arrive(self.flight["z", i])
        t = self.part[u, p.z, p.y, p.c, :, self.lanes(p.x)].astype(f32)
        for j in range(p.depth - 1):
            t = t + self.from_z[j, u].astype(f32)
        self.total[u] = t

    def step(self):
        t, n, lag = self.t, len(self.order), self.lag
        stages = ((self.core, 0), (self.one, 1), (self.two, 1 + lag), (self.far, 1 + 2 * lag), (self.last, 1 + 3 * lag))
        for stage, late in stages:
            if 0 <= t - late < n:
                stage(t - late)
        self.t += 1

    def finish(self):
        while self.t < len(self.order) + 1 + 3 * self.lag:
            self.step()


class SumAll:
    def __init__(self, place, wire, own, room):
        self.p, self.wire, self.own, self.room = place, wire, own, room
        self.stage = 0

    def start(self):
        p = self.p
        if self.stage < 3:
            device = (p.over_c, p.over_x, p.over_y)[self.stage]()
            self.flight = [self.wire.start(self.own, self.room.at[self.stage], device)]
        else:
            self.flight = [self.wire.start(self.own, self.room.at[3 + p.z], p.over_z(k)) for k in range(1, p.depth)]

    def finish(self):
        p = self.p
        arrive(self.flight)
        for copy in self.flight:
            copy.wait_send()
        self.wire.open = [c for c in self.wire.open if all(c is not f for f in self.flight)]
        if self.stage < 3:
            self.own[...] = self.own[...] + self.room[self.stage]
        else:
            self.room[3 + p.z] = self.own[...]
            t = self.room[3]
            for z in range(1, p.depth):
                t = t + self.room[3 + z]
            self.own[...] = t
        self.stage += 1

    def run(self):
        while self.stage < 4:
            self.start()
            self.finish()


def dot(a, b, left=1, right=0):
    return lax.dot_general(a, b, (((left,), (right,)), ((), ())), preferred_element_type=f32)


def row_loop(count, size, f):
    def step(i, carry):
        f(pl.ds(pl.multiple_of(i * size, size), size))
        return carry

    lax.fori_loop(0, count // size, step, 0)


def center_scale(x):
    center = x - jnp.mean(x, -1, keepdims=True)
    return center, lax.rsqrt(jnp.mean(center * center, -1, keepdims=True) + norm_epsilon)


def three(x):
    hi = x.astype(bf16)
    rest = x - hi.astype(f32)
    mid = rest.astype(bf16)
    return hi, mid, (rest - mid.astype(f32)).astype(bf16)


def fold(x):
    return jnp.sum(x.reshape(x.shape[0] // 8, 8, x.shape[1]), 0)


def block_kernel(
    depth,
    tokens, segment, pairing, images, qkv_weight, out_weight, up_weight, down_weight, affine, head_bias, inner_bias,
    total, sums, grad_input,
    full, pictures, part, from_core, one_a, one_b, two_a, two_b, from_z,
    tok, normed_one, qkv, mixed, resid, normed_two, hidden, slope, stream, grad_mixed, acc, low,
    probs, same, wide, room, room2, folds, cap, key_acc, value_acc, grad_near, grad_far,
    send, recv, free, local,
):
    place = Place(depth)
    x, dp = place.x, place.dp
    rows, width = tok.shape
    packs, length = 2, rows // 2
    half = qkv_weight.shape[2]
    units = full.shape[0]
    blocks = up_weight.shape[1] // half
    share = full.shape[4]
    up0, down0 = 4, 4 + blocks

    token_copies = [
        pltpu.make_async_copy(tokens.at[packs * x + p], tok.at[pl.ds(p * length, length)], local.at[p]) for p in range(packs)
    ]
    for copy in token_copies:
        copy.start()

    def keep(u, value):
        full[u, place.z, place.y, place.c, :, pl.ds(pl.multiple_of(x * half, 128), half)] = value.astype(bf16)

    for k in range(3):
        keep(k, qkv_weight[k])
    keep(3, out_weight[...])
    for j in range(blocks):
        keep(up0 + j, up_weight[:, j * half : (j + 1) * half])
        keep(down0 + j, down_weight[:, j * half : (j + 1) * half])
    few = pictures.shape[4]
    picture = images[pl.ds(pl.multiple_of(x * few, few), few)].astype(f32)
    pictures[place.z, place.y, place.c, x] = normalize(picture).astype(bf16)

    place.barrier()
    wire = Wire(send, recv)
    items = [Sheet(full, u) for u in range(units)]
    items.insert(units - 1, Stack(pictures))
    image_at = units - 1
    gather = Gather(place, wire, items, 3, 2)

    def ready(u):
        gather.until(u if u < image_at else u + 1)

    def placed(a, at, lanes):
        a = a.astype(bf16)
        n = a.shape[1]
        spot = lax.broadcasted_iota(jnp.int32, (n, lanes), 1) == lax.broadcasted_iota(jnp.int32, (n, lanes), 0) + at
        return dot(a, jnp.where(spot, 1.0, 0.0).astype(bf16))

    owner = x * (4 * depth) + dp
    n_affine, n_head, n_inner = affine.shape[1], head_bias.shape[1], inner_bias.shape[1]
    wide[...] = jnp.zeros_like(wide)
    first = jnp.where(x == 0, 1.0, 0.0)
    wide[0:6] = placed(affine[...], dp * n_affine, width) * first
    wide[6:8] = placed(head_bias[...], owner * n_head, width)
    inner_row = placed(inner_bias[...], (owner * n_inner) % width, width)
    inner_rows = 2 * blocks * half // width
    at_row = lax.broadcasted_iota(jnp.int32, (inner_rows, width), 0) == (owner * n_inner) // width
    wide[8 : 8 + inner_rows] = jnp.where(at_row, jnp.broadcast_to(inner_row, (inner_rows, width)), 0.0)
    spread = SumAll(place, wire, wide, room)
    while spread.stage < 4:
        spread.start()
        if gather.t < 1:
            gather.step()
        spread.finish()

    for copy in token_copies:
        copy.wait()

    slots = pairing.shape[2]
    tile, window = 64, 128
    starts = [min(max(t * tile - (window - tile) // 2, 0), length - window) for t in range(length // tile)]
    onehots, columns = [], []
    for p in range(packs):
        seg = jnp.broadcast_to(segment[packs * x + p], (slots, length))
        onehot = jnp.where(seg == lax.broadcasted_iota(jnp.int32, (slots, length), 0), 1.0, 0.0)
        onehots.append(onehot)
        low_hot = onehot.astype(bf16)
        both = dot(low_hot, low_hot, 0, 0)
        folds_at = acc.at[pl.ds(0, length), pl.ds(0, length)]
        folds_at[...] = both
        eye = lax.broadcasted_iota(jnp.int32, (window, window), 0) == lax.broadcasted_iota(jnp.int32, (window, window), 1)
        for t, w in enumerate(starts):
            pick = lax.broadcasted_iota(jnp.int32, (length, window), 0) == lax.broadcasted_iota(jnp.int32, (length, window), 1) + w
            shared = dot(folds_at[pl.ds(t * tile, tile)].astype(bf16), jnp.where(pick, 1.0, 0.0).astype(bf16))
            same[p, t, 0:tile] = shared
            same[p, t, tile : 2 * tile] = shared

    gather.step()

    def norm_one(r):
        center, scale = center_scale(tok[r].astype(f32))
        normed_one[r] = (center * scale * wide[0:1] + wide[1:2]).astype(bf16)

    row_loop(rows, 32, norm_one)
    gather.step()

    def unit(u):
        return full[u].reshape(width, width)

    chunk = 256

    def unit_lanes(u, j):
        return full[u, :, :, :, :, pl.ds(j * chunk, chunk)].reshape(width, chunk)

    for k in range(3):
        ready(k)
        for j in range(width // chunk):
            lanes = pl.ds(j * chunk, chunk)
            value = dot(normed_one[...], unit_lanes(k, j))
            if k != 1:
                row = 6 if k == 0 else 7
                value = value + wide[row : row + 1, lanes]
            qkv[k, :, lanes] = value.astype(bf16)

    root_scale = HD**-0.5
    pair = 2 * HD
    pairs = width // pair
    lower = lax.broadcasted_iota(jnp.int32, (tile, pair), 1) < HD

    def doubled(a):
        zero = jnp.zeros_like(a)
        return jnp.concatenate([jnp.where(lower, a, zero), jnp.where(lower, zero, a)], 0)

    def joined(a):
        return jnp.where(lower, a[:tile], a[tile:])

    def attend(p):
        def step(g, carry):
            lanes = pl.ds(pl.multiple_of(g * pair, pair), pair)
            for t, w in enumerate(starts):
                near = pl.ds(p * length + t * tile, tile)
                reach = pl.ds(p * length + w, window)
                query = doubled(qkv[0, near, lanes])
                scores = dot(query, qkv[1, reach, lanes], 1, 1) * root_scale
                scores = jnp.where(same[p, t] > 0.5, scores, mask_value)
                e = jnp.exp(scores - jnp.max(scores, -1, keepdims=True))
                prob = (e * (1.0 / jnp.sum(e, -1, keepdims=True))).astype(bf16)
                probs[p, g, t] = prob
                mixed[near, lanes] = joined(dot(prob, qkv[2, reach, lanes])).astype(bf16)
            return carry

        lax.fori_loop(0, pairs, step, 0)

    for p in range(packs):
        attend(p)
        gather.step()

    ready(3)
    acc[...] = dot(mixed[...], unit(3), 1, 1)

    def norm_two(r):
        value = tok[r].astype(f32) + acc[r] + wide[4:5]
        resid[r] = value
        center, scale = center_scale(value)
        normed_two[r] = (center * scale * wide[2:3] + wide[3:4]).astype(bf16)
        stream[r] = value + wide[5:6]

    row_loop(rows, 32, norm_two)

    curve = (2.0 / jnp.pi) ** 0.5
    for j in range(blocks):
        ready(up0 + j)
        at = j * half
        row, lane = at // width, at % width
        rows_per = blocks * half // width
        bias = jnp.concatenate(
            [wide[8 + row : 9 + row, lane : lane + half], wide[8 + rows_per + row : 9 + rows_per + row, lane : lane + half]], 1
        )
        for k in range(width // chunk):
            lanes = pl.ds(k * chunk, chunk)
            acc[:, lanes] = dot(normed_two[...], unit_lanes(up0 + j, k))

        def activate(r, j=j, bias=bias):
            u = acc[r] + bias
            square = u * u
            t = jnp.tanh(curve * (u + 0.044715 * (square * u)))
            hidden[j, r] = (0.5 * u * (1.0 + t)).astype(bf16)
            slope[j, r] = (0.5 * (1.0 + t) + 0.5 * u * (1.0 - t * t) * (curve * (1.0 + 3.0 * 0.044715 * square))).astype(bf16)

        row_loop(rows, 16, activate)

    for j in range(blocks):
        ready(down0 + j)
        stream[...] += dot(hidden[j], unit(down0 + j), 1, 1)

    live_rows, count_rows, target_rows = [], [], []
    for p in range(packs):
        count = jnp.sum(onehots[p], 1, keepdims=True)
        hot = onehots[p].astype(bf16)
        hi, mid, lo = three(stream[pl.ds(p * length, length)])
        pooled = dot(hot, hi) + dot(hot, mid) + dot(hot, lo)
        cap[pl.ds(p * slots, slots)] = pooled / jnp.maximum(count, 1.0)
        count_rows.append(count)
        names = jnp.broadcast_to(pairing[packs * x + p], (slots, slots)).astype(f32)
        diagonal = lax.broadcasted_iota(jnp.int32, (slots, slots), 0) == lax.broadcasted_iota(jnp.int32, (slots, slots), 1)
        target_rows.append(jnp.sum(jnp.where(diagonal, names, 0.0), 1, keepdims=True))
    counts = jnp.concatenate(count_rows, 0)
    target = jnp.concatenate(target_rows, 0)
    live = jnp.where(counts > 0.0, 1.0, 0.0)
    pooled = cap[...]
    radius = lax.rsqrt(jnp.sum(pooled * pooled, -1, keepdims=True) + norm_epsilon)
    caption = (pooled * radius).astype(bf16)
    all_images = pictures[...].reshape(-1, width)
    count = all_images.shape[0]
    logits = sharpness_divisor * dot(caption, all_images, 1, 1)
    hit = lax.broadcasted_iota(jnp.int32, logits.shape, 1).astype(f32) == target
    best = jnp.max(logits, -1, keepdims=True)
    e = jnp.exp(logits - best)
    sum_e = jnp.sum(e, -1, keepdims=True)
    positive = jnp.sum(jnp.where(hit, logits, 0.0), -1, keepdims=True)
    cross = best + jnp.log(sum_e) - positive
    loss = jnp.sum(live * cross, 0, keepdims=True)
    scaled = loss_scale * live
    grad_logits = (scaled * (e * (1.0 / sum_e) - jnp.where(hit, 1.0, 0.0))).astype(bf16)
    grad_caption = sharpness_divisor * dot(grad_logits, all_images)
    inner = jnp.sum(pooled * grad_caption, -1, keepdims=True)
    grad_pooled = radius * grad_caption - (radius * radius * radius) * inner * pooled
    grad_pooled = grad_pooled / jnp.maximum(counts, 1.0)
    folds[...] = jnp.zeros_like(folds)
    for p in range(packs):
        hot = onehots[p].astype(bf16)
        hi, mid, lo = three(grad_pooled[p * slots : (p + 1) * slots])
        stream[pl.ds(p * length, length)] = dot(hot, hi, 0, 0) + dot(hot, mid, 0, 0) + dot(hot, lo, 0, 0)

    def lower_stream(r):
        value = stream[r]
        low[r] = value.astype(bf16)
        folds[5] += fold(value)

    row_loop(rows, 32, lower_stream)

    order = [down0 + j for j in range(blocks)] + [up0 + j for j in range(blocks)] + [3, 0, 1, 2]
    reduce = Reduce(place, wire, order, 2, free, part, from_core, one_a, one_b, two_a, two_b, from_z, total)

    def weight_grad(u, left, right):
        for j in range(width // chunk):
            lanes = pl.ds(j * chunk, chunk)
            value = dot(left, right(lanes), 0, 0).astype(bf16)
            part[u, :, :, :, :, lanes] = value.reshape(depth, 2, 2, share, chunk)
        reduce.step()

    sums[...] = jnp.zeros_like(sums)
    for j in range(blocks):
        weight_grad(down0 + j, low[...], lambda lanes, j=j: hidden[j, :, lanes])
        for k in range(width // chunk):
            lanes = pl.ds(k * chunk, chunk)
            acc[:, lanes] = dot(low[...], unit_lanes(down0 + j, k))

        def upper_back(r, j=j):
            value = (acc[r] * slope[j, r].astype(f32)).astype(bf16)
            hidden[j, r] = value
            folds[6] += fold(value.astype(f32))

        folds[6] = jnp.zeros_like(folds[6])
        row_loop(rows, 32, upper_back)
        inner_sum = jnp.sum(folds[6], 0, keepdims=True)
        at = j * half
        row, lane = at // width, at % width
        rows_per = blocks * half // width
        sums[8 + row : 9 + row, lane : lane + half] = inner_sum[:, :half]
        sums[8 + rows_per + row : 9 + rows_per + row, lane : lane + half] = inner_sum[:, half:]

    for j in range(blocks):
        weight_grad(up0 + j, normed_two[...], lambda lanes, j=j: hidden[j, :, lanes])
        value = dot(hidden[j], unit(up0 + j), 1, 1)
        if j == 0:
            acc[...] = value
        else:
            acc[...] += value

    def norm_two_back(r):
        center, scale = center_scale(resid[r])
        hat = center * scale
        grad = acc[r]
        weighted = grad * wide[2:3]
        value = stream[r] + scale * (
            weighted - jnp.mean(weighted, -1, keepdims=True) - hat * jnp.mean(weighted * hat, -1, keepdims=True)
        )
        stream[r] = value
        low[r] = value.astype(bf16)
        folds[2] += fold(grad * hat)
        folds[3] += fold(grad)
        folds[4] += fold(value)

    row_loop(rows, 32, norm_two_back)
    weight_grad(3, low[...], lambda lanes: mixed[:, lanes])
    for k in range(width // chunk):
        lanes = pl.ds(k * chunk, chunk)
        grad_mixed[:, lanes] = dot(low[...], unit_lanes(3, k)).astype(bf16)

    def attend_back(p):
        def step(g, carry):
            lanes = pl.ds(pl.multiple_of(g * pair, pair), pair)
            key_acc[...] = jnp.zeros_like(key_acc)
            value_acc[...] = jnp.zeros_like(value_acc)
            for t, w in enumerate(starts):
                near = pl.ds(p * length + t * tile, tile)
                reach = pl.ds(p * length + w, window)
                query = doubled(qkv[0, near, lanes])
                grad = doubled(grad_mixed[near, lanes])
                prob = probs[p, g, t]
                prob_wide = prob.astype(f32)
                grad_prob = dot(grad, qkv[2, reach, lanes], 1, 1)
                grad_score = prob_wide * (grad_prob - jnp.sum(prob_wide * grad_prob, -1, keepdims=True))
                grad_score = grad_score.astype(bf16)
                key_acc[pl.ds(w, window)] += dot(grad_score, query, 0, 0)
                value_acc[pl.ds(w, window)] += dot(prob, grad, 0, 0)
                qkv[0, near, lanes] = (joined(dot(grad_score, qkv[1, reach, lanes])) * root_scale).astype(bf16)
            span = pl.ds(p * length, length)
            qkv[1, span, lanes] = (key_acc[...] * root_scale).astype(bf16)
            qkv[2, span, lanes] = value_acc[...].astype(bf16)
            return carry

        lax.fori_loop(0, pairs, step, 0)

    for p in range(packs):
        attend_back(p)

    for k in range(3):
        weight_grad(k, normed_one[...], lambda lanes, k=k: qkv[k, :, lanes])
        value = dot(qkv[k], unit(k), 1, 1)
        if k == 0:
            acc[...] = value
        else:
            acc[...] += value

    def head_sums(r):
        folds[7] += fold(qkv[0, r].astype(f32))
        folds[8] += fold(qkv[2, r].astype(f32))

    row_loop(rows, 32, head_sums)

    def norm_one_back(r):
        center, scale = center_scale(tok[r].astype(f32))
        hat = center * scale
        grad = acc[r]
        weighted = grad * wide[0:1]
        value = stream[r] + scale * (
            weighted - jnp.mean(weighted, -1, keepdims=True) - hat * jnp.mean(weighted * hat, -1, keepdims=True)
        )
        grad_near[r] = value.astype(bf16)
        folds[0] += fold(grad * hat)
        folds[1] += fold(grad)

    row_loop(rows, 32, norm_one_back)
    swap = wire.start(grad_near, grad_far, place.over_x())

    for k, row in ((0, 0), (1, 1), (2, 2), (3, 3), (4, 4), (5, 5), (7, 6), (8, 7)):
        sums[row : row + 1] = jnp.sum(folds[k], 0, keepdims=True)
    last_row = 8 + inner_rows
    sums[last_row : last_row + 1] = jnp.broadcast_to(loss, (1, width))
    SumAll(place, wire, sums, room2).run()

    def widen(source, target):
        def f(r):
            target[r] = source[r].astype(f32)

        row_loop(rows, 32, f)

    widen(grad_near, acc)
    outs = [
        pltpu.make_async_copy(acc.at[pl.ds(p * length, length)], grad_input.at[packs * x + p], local.at[p]) for p in range(packs)
    ]
    for copy in outs:
        copy.start()
    reduce.finish()
    swap.wait_recv()
    widen(grad_far, stream)
    outs += [
        pltpu.make_async_copy(stream.at[pl.ds(p * length, length)], grad_input.at[packs * (1 - x) + p], local.at[packs + p])
        for p in range(packs)
    ]
    for copy in outs[packs:]:
        copy.start()
    for copy in outs:
        copy.wait()
    wire.close()


def block_step(depth, tokens, segment, pairing, images, qkv_weight, out_weight, up_weight, down_weight, affine, head_bias, inner_bias):
    packs, length, width = tokens.shape
    rows = packs // 2 * length
    share, half = qkv_weight.shape[1:]
    blocks = up_weight.shape[1] // half
    units = 4 + 2 * blocks
    slots = pairing.shape[1]
    h = depth // 2
    few = images.shape[0] // 2
    ring = 4
    small = (16, width)
    low = lambda *shape: pltpu.VMEM(shape, bf16)
    wide = lambda *shape: pltpu.VMEM(shape, f32)
    count = (units + 1) * (depth - 1 + 5) + units * (5 + depth - 1) + 2 * (3 + depth - 1) + 1
    vmem = pl.BlockSpec(memory_space=pltpu.VMEM)
    hbm = pl.BlockSpec(memory_space=pl.ANY)
    return pl.pallas_call(
        functools.partial(block_kernel, depth),
        out_shape=(
            jax.ShapeDtypeStruct((units, share, half), f32),
            jax.ShapeDtypeStruct(small, f32),
            jax.ShapeDtypeStruct(tokens.shape, f32),
        ),
        in_specs=[hbm] + [vmem] * 10,
        out_specs=[vmem, vmem, hbm],
        scratch_shapes=[
            low(units, depth, 2, 2, share, width), low(depth, 2, 2, 2, few, width),
            low(units, depth, 2, 2, share, width), low(ring, depth, 2, share, width), low(units, h, 2, share, half),
            low(units, depth - h, share, width), low(units, h, share, half), low(units, depth - h, share, half),
            low(depth - 1, units, share, half),
            low(rows, width), low(rows, width), low(3, rows, width), low(rows, width), wide(rows, width), low(rows, width),
            low(blocks, rows, width), low(blocks, rows, width), wide(rows, width), low(rows, width), wide(rows, width), low(rows, width),
            low(2, width // (2 * HD), length // 64, 128, 128), wide(2, length // 64, 128, 128), wide(*small),
            wide(3 + depth, *small), wide(3 + depth, *small), wide(9, 8, width), wide(2 * slots, width), wide(length, 2 * HD), wide(length, 2 * HD),
            low(rows, width), low(rows, width),
            pltpu.SemaphoreType.DMA((count,)), pltpu.SemaphoreType.DMA((count,)), pltpu.SemaphoreType.REGULAR, pltpu.SemaphoreType.DMA((4,)),
        ],
        compiler_params=pltpu.CompilerParams(collective_id=1, has_side_effects=True, vmem_limit_bytes=64 << 20),
        name="train_block",
    )(
        tokens, segment.reshape(packs, 1, length), pairing.reshape(packs, 1, slots), images,
        qkv_weight, out_weight, up_weight, down_weight, affine, head_bias, inner_bias.reshape(1, -1),
    )


def sum_kernel(depth, own_ref, sum_ref, room, send, recv):
    place = Place(depth)
    place.barrier()
    sum_ref[...] = own_ref[...]
    SumAll(place, Wire(send, recv), sum_ref, room).run()


def sum_all(depth, own):
    vmem = pl.BlockSpec(memory_space=pltpu.VMEM)
    return pl.pallas_call(
        functools.partial(sum_kernel, depth),
        out_shape=jax.ShapeDtypeStruct(own.shape, f32),
        in_specs=[vmem],
        out_specs=vmem,
        scratch_shapes=[
            pltpu.VMEM((3 + depth,) + own.shape, f32),
            pltpu.SemaphoreType.DMA((3 + depth - 1,)), pltpu.SemaphoreType.DMA((3 + depth - 1,)),
        ],
        compiler_params=pltpu.CompilerParams(collective_id=2, has_side_effects=True),
        name="sum_squares",
    )(own)


def body_near(depth, *arrays):
    (
        tokens, segment, pairing, images,
        qkv_weight, qkv_first, qkv_second, out_weight, out_first, out_second,
        up_weight, up_first, up_second, down_weight, down_first, down_second,
        affine, affine_first, affine_second, head_bias, head_first, head_second,
        inner_bias, inner_first, inner_second,
    ) = arrays
    mp = lax.axis_index("mp")
    dp = lax.axis_index("dp")
    width = tokens.shape[-1]
    share, half = qkv_weight.shape[1:]
    blocks = up_weight.shape[1] // half
    dp_size = 4 * depth
    total, sums, grad_input = block_step(
        depth, tokens, segment, pairing, images, qkv_weight, out_weight, up_weight, down_weight, affine, head_bias, inner_bias
    )

    def uncut(a):
        return a.transpose(1, 0, 2).reshape(share, -1)

    def lane(a, at, n):
        return lax.dynamic_slice_in_dim(a, at * n, n, a.ndim - 1)

    inner_rows = 2 * blocks * half // width
    owner = mp * dp_size + dp
    grads = (
        total[0:3], total[3], uncut(total[4 : 4 + blocks]), uncut(total[4 + blocks :]),
        lane(sums[0:6], dp, affine.shape[1]),
        lane(sums[6:8], owner, head_bias.shape[1]),
        lane(sums[8 : 8 + inner_rows].reshape(-1), owner, inner_bias.shape[0]),
    )
    mean_loss = sums[8 + inner_rows, 0] / float(pairing.size * dp_size)
    weights = (qkv_weight, out_weight, up_weight, down_weight, affine, head_bias, inner_bias)
    firsts = (qkv_first, out_first, up_first, down_first, affine_first, head_first, inner_first)
    seconds = (qkv_second, out_second, up_second, down_second, affine_second, head_second, inner_second)
    decays = (weight_decay, weight_decay, weight_decay, weight_decay, 0.0, 0.0, 0.0)
    steps = [moments(weights[i], firsts[i], seconds[i], grads[i], decays[i]) for i in range(7)]
    updates = [s[2] for s in steps]
    squares = jnp.stack([tensor_squares(*weights, 2.0), tensor_squares(*updates, 2.0)])
    squares = sum_all(depth, jnp.pad(squares, ((0, 6), (0, 113))))
    norms = jnp.sqrt(squares[0:2, 0:15])
    weight_split, update_split = split_norms(norms[0]), split_norms(norms[1])
    results = [mean_loss, grad_input]
    for i in range(7):
        results += [scaled_step(weights[i], updates[i], weight_split[i], update_split[i]), steps[i][0], steps[i][1]]
    return (*results, norms)


def body(
    tokens,
    segment,
    pairing,
    images,
    qkv_weight,
    qkv_first,
    qkv_second,
    out_weight,
    out_first,
    out_second,
    up_weight,
    up_first,
    up_second,
    down_weight,
    down_first,
    down_second,
    affine,
    affine_first,
    affine_second,
    head_bias,
    head_first,
    head_second,
    inner_bias,
    inner_first,
    inner_second,
):
    model_size = lax.axis_size("mp")
    packs, length, width = tokens.shape
    rows = packs * length
    qkv_full, out_full, up_full, down_full, affine_full, head_full, inner_full = (
        lax.all_gather(qkv_weight.astype(jnp.bfloat16), "dp", axis=1, tiled=True),
        lax.all_gather(out_weight.astype(jnp.bfloat16), "dp", axis=0, tiled=True),
        lax.all_gather(up_weight.astype(jnp.bfloat16), "dp", axis=0, tiled=True),
        lax.all_gather(down_weight.astype(jnp.bfloat16), "dp", axis=0, tiled=True),
        lax.all_gather(affine.astype(jnp.bfloat16), "dp", axis=1, tiled=True),
        lax.all_gather(head_bias.astype(jnp.bfloat16), "dp", axis=1, tiled=True),
        lax.all_gather(inner_bias.astype(jnp.bfloat16), "dp", axis=0, tiled=True),
    )
    affine_wide = affine_full.astype(jnp.float32)
    head_wide = head_full.astype(jnp.float32)
    inner_wide = inner_full.astype(jnp.float32)
    half = qkv_full.shape[2]
    local_heads = half // HD
    shape4 = (packs, length, local_heads, HD)
    root_scale = HD ** (-0.5)
    inputs = tokens.reshape(rows, width).astype(jnp.float32)
    normed_one = layer_norm(inputs, affine_wide[0], affine_wide[1]).astype(jnp.bfloat16)
    projected = jnp.einsum("td,kde->kte", normed_one, qkv_full, preferred_element_type=jnp.float32)
    query = (projected[0] + head_wide[0]).astype(jnp.bfloat16).reshape(shape4)
    keys = projected[1].astype(jnp.bfloat16).reshape(shape4)
    values = (projected[2] + head_wide[1]).astype(jnp.bfloat16).reshape(shape4)
    same = segment[:, None, :, None] == segment[:, None, None, :]

    def masked_scores():
        raw = (
            jnp.einsum("pqhe,pkhe->phqk", query, keys, preferred_element_type=jnp.float32)
            * root_scale
        )
        return jnp.where(same, raw, mask_value)

    scores = masked_scores()
    top = jnp.max(scores, -1, keepdims=True)
    log_total = top + jnp.log(jnp.sum(jnp.exp(scores - top), -1, keepdims=True))
    probs = jnp.exp(scores - log_total).astype(jnp.bfloat16)
    mixed = jnp.einsum("phqk,pkhe->pqhe", probs, values, preferred_element_type=jnp.float32)
    mixed = mixed.reshape(rows, half).astype(jnp.bfloat16)
    attended = lax.psum(summation_axes_spec(mixed, out_full, 1, 1), "mp")
    resid = inputs + attended + affine_wide[4]
    normed_two = layer_norm(resid, affine_wide[2], affine_wide[3]).astype(jnp.bfloat16)
    upper = jnp.dot(normed_two, up_full, preferred_element_type=jnp.float32) + inner_wide
    activated, gelu_back = jax.vjp(jax.nn.gelu, upper)
    hidden = activated.astype(jnp.bfloat16)
    lowered = lax.psum(
        summation_axes_spec(hidden, down_full, 1, 1).astype(jnp.bfloat16), "mp"
    ).astype(jnp.float32)
    output = resid + lowered + affine_wide[5]
    slots = pairing.shape[1]
    onehot = (segment[:, None, :] == jnp.arange(slots, dtype=jnp.int32)[None, :, None]).astype(
        jnp.float32
    )
    counts = jnp.sum(onehot, -1)
    divisor = jnp.maximum(counts, 1.0)[..., None]
    pooled = (
        jnp.einsum(
            "pcl,pld->pcd",
            onehot,
            output.reshape(packs, length, width),
            precision=exact_arithmetic_mode,
        )
        / divisor
    )
    flat = pooled.reshape(packs * slots, width)
    caption_wide, normalize_back = jax.vjp(normalize, flat)
    sentence_words = caption_wide.astype(jnp.bfloat16)
    live = (counts > 0).reshape(-1).astype(jnp.float32)
    target = pairing.reshape(-1)
    captions_count = flat.shape[0]
    slot_total = float(captions_count * lax.axis_size("dp"))
    picture_summed = normalize(images.astype(jnp.float32)).astype(jnp.bfloat16)

    def similarity(packed_sequence_slice):
        return sharpness_divisor * summation_axes_spec(sentence_words, packed_sequence_slice, 1, 1)

    score_packed_sequence_slice = lax.all_gather(picture_summed, "dp", axis=0, tiled=True)
    best = jnp.full((captions_count,), mask_value, jnp.float32)
    similarity_grid = similarity(score_packed_sequence_slice)
    new_best = jnp.maximum(best, jnp.max(similarity_grid, 1))
    total = jnp.sum(jnp.exp(similarity_grid - new_best[:, None]), 1)
    column = jnp.arange(score_packed_sequence_slice.shape[0], dtype=jnp.int32)
    hit = target[:, None] == column[None, :]
    positive = jnp.sum(jnp.where(hit, similarity_grid, 0.0), 1)
    best_all, total_all, positive = (new_best, total, positive)
    log_sum = best_all + jnp.log(total_all)
    grad_packed_sequence_slice = lax.all_gather(picture_summed, "dp", axis=0, tiled=True)
    similarity_grid = similarity(grad_packed_sequence_slice)
    column = jnp.arange(grad_packed_sequence_slice.shape[0], dtype=jnp.int32)
    hit = (target[:, None] == column[None, :]).astype(jnp.float32)
    logit_gradient = (
        loss_scale * live[:, None] * (jnp.exp(similarity_grid - log_sum[:, None]) - hit)
    ).astype(jnp.bfloat16)
    sentence_derivative = sharpness_divisor * jnp.dot(
        logit_gradient, grad_packed_sequence_slice, preferred_element_type=jnp.float32
    )
    cross = log_sum - positive
    loss_local = jnp.sum(live * cross)
    loss_total = lax.psum(loss_local, "dp")
    mean_loss = loss_total / slot_total
    (grad_flat,) = normalize_back(sentence_derivative)
    grad_pooled = grad_flat.reshape(packs, slots, width) / divisor
    grad_output = jnp.einsum(
        "pcl,pcd->pld", onehot, grad_pooled, precision=exact_arithmetic_mode
    ).reshape(rows, width)
    grad_output_low = grad_output.astype(jnp.bfloat16)
    down_grad = summation_axes_spec(grad_output_low, hidden, 0, 0)
    grad_hidden = jnp.dot(grad_output_low, down_full, preferred_element_type=jnp.float32)
    (grad_upper,) = gelu_back(grad_hidden)
    grad_upper = grad_upper.astype(jnp.bfloat16)
    inner_grad = jnp.sum(grad_upper.astype(jnp.float32), 0)
    up_grad = summation_axes_spec(normed_two, grad_upper, 0, 0)
    grad_two = lax.psum(
        summation_axes_spec(grad_upper, up_full, 1, 1).astype(jnp.bfloat16), "mp"
    ).astype(jnp.float32)
    _, norm_two_back = jax.vjp(layer_norm, resid, affine_wide[2], affine_wide[3])
    grad_resid_norm, gain_two_grad, shift_two_grad = norm_two_back(grad_two)
    grad_resid = grad_output + grad_resid_norm
    grad_resid_low = grad_resid.astype(jnp.bfloat16)
    out_grad = summation_axes_spec(grad_resid_low, mixed, 0, 0)
    grad_mixed = jnp.dot(grad_resid_low, out_full, preferred_element_type=jnp.float32)
    grad_mixed = grad_mixed.astype(jnp.bfloat16).reshape(shape4)
    probs_wide = jnp.exp(masked_scores() - log_total)
    probs_low = probs_wide.astype(jnp.bfloat16)
    grad_value = jnp.einsum(
        "phqk,pqhe->pkhe", probs_low, grad_mixed, preferred_element_type=jnp.float32
    )
    grad_probs = jnp.einsum(
        "pqhe,pkhe->phqk", grad_mixed, values, preferred_element_type=jnp.float32
    )
    grad_scores = probs_wide * (grad_probs - jnp.sum(probs_wide * grad_probs, -1, keepdims=True))
    grad_scores = grad_scores.astype(jnp.bfloat16)
    grad_query = (
        jnp.einsum("phqk,pkhe->pqhe", grad_scores, keys, preferred_element_type=jnp.float32)
        * root_scale
    )
    grad_key = (
        jnp.einsum("phqk,pqhe->pkhe", grad_scores, query, preferred_element_type=jnp.float32)
        * root_scale
    )
    grad_qkv = (
        jnp.stack([grad_query, grad_key, grad_value]).reshape(3, rows, half).astype(jnp.bfloat16)
    )
    head_grad = jnp.stack(
        [jnp.sum(grad_qkv[0].astype(jnp.float32), 0), jnp.sum(grad_qkv[2].astype(jnp.float32), 0)]
    )
    qkv_grad = jnp.einsum("td,kte->kde", normed_one, grad_qkv, preferred_element_type=jnp.float32)
    grad_one = lax.psum(
        jnp.einsum("kte,kde->td", grad_qkv, qkv_full, preferred_element_type=jnp.float32).astype(
            jnp.bfloat16
        ),
        "mp",
    ).astype(jnp.float32)
    _, norm_one_back = jax.vjp(layer_norm, inputs, affine_wide[0], affine_wide[1])
    grad_input_norm, gain_one_grad, shift_one_grad = norm_one_back(grad_one)
    grad_input = (grad_resid + grad_input_norm).reshape(packs, length, width)
    affine_grad = jnp.stack(
        [
            gain_one_grad,
            shift_one_grad,
            gain_two_grad,
            shift_two_grad,
            jnp.sum(grad_resid, 0),
            jnp.sum(grad_output, 0),
        ]
    )
    qkv_part, out_part, up_part, down_part, affine_part, head_part, inner_part = (
        lax.psum_scatter(qkv_grad, "dp", scatter_dimension=1, tiled=True),
        lax.psum_scatter(out_grad, "dp", scatter_dimension=0, tiled=True),
        lax.psum_scatter(up_grad, "dp", scatter_dimension=0, tiled=True),
        lax.psum_scatter(down_grad, "dp", scatter_dimension=0, tiled=True),
        lax.psum_scatter(affine_grad, "dp", scatter_dimension=1, tiled=True),
        lax.psum_scatter(head_grad, "dp", scatter_dimension=1, tiled=True),
        lax.psum_scatter(inner_grad, "dp", scatter_dimension=0, tiled=True),
    )
    weights = (qkv_weight, out_weight, up_weight, down_weight, affine, head_bias, inner_bias)
    firsts = (qkv_first, out_first, up_first, down_first, affine_first, head_first, inner_first)
    seconds = (
        qkv_second,
        out_second,
        up_second,
        down_second,
        affine_second,
        head_second,
        inner_second,
    )
    grads = (qkv_part, out_part, up_part, down_part, affine_part, head_part, inner_part)
    decays = (weight_decay, weight_decay, weight_decay, weight_decay, 0.0, 0.0, 0.0)
    parts = [
        moments(weights[index], firsts[index], seconds[index], grads[index], decays[index])
        for index in range(7)
    ]
    updates = [packed_sequence_slice[2] for packed_sequence_slice in parts]
    weight_squares = tensor_squares(*weights, float(model_size))
    update_squares = tensor_squares(*updates, float(model_size))
    weight_total, update_total = lax.psum((weight_squares, update_squares), ("dp", "mp"))
    weight_norm = jnp.sqrt(weight_total)
    update_norm = jnp.sqrt(update_total)
    weight_split = split_norms(weight_norm)
    update_split = split_norms(update_norm)
    news = [
        scaled_step(weights[index], updates[index], weight_split[index], update_split[index])
        for index in range(7)
    ]
    return (
        mean_loss,
        grad_input,
        news[0],
        parts[0][0],
        parts[0][1],
        news[1],
        parts[1][0],
        parts[1][1],
        news[2],
        parts[2][0],
        parts[2][1],
        news[3],
        parts[3][0],
        parts[3][1],
        news[4],
        parts[4][0],
        parts[4][1],
        news[5],
        parts[5][0],
        parts[5][1],
        news[6],
        parts[6][0],
        parts[6][1],
        jnp.stack([weight_norm, update_norm]),
    )


def solution(mesh):
    depth = mesh.shape["dp"] // 4
    fits = mesh.shape["mp"] == 2 and mesh.shape["dp"] % 8 == 0 and 768 // mesh.shape["dp"] % 16 == 0
    return jax.shard_map(
        functools.partial(body_near, depth) if fits else body,
        mesh=mesh,
        in_specs=(
            P("dp", None, None),
            P("dp", None),
            P("dp", None),
            P("dp", None),
            P(None, "dp", "mp"),
            P(None, "dp", "mp"),
            P(None, "dp", "mp"),
            P("dp", "mp"),
            P("dp", "mp"),
            P("dp", "mp"),
            P("dp", "mp"),
            P("dp", "mp"),
            P("dp", "mp"),
            P("dp", "mp"),
            P("dp", "mp"),
            P("dp", "mp"),
            P(None, "dp"),
            P(None, "dp"),
            P(None, "dp"),
            P(None, ("mp", "dp")),
            P(None, ("mp", "dp")),
            P(None, ("mp", "dp")),
            P(("mp", "dp")),
            P(("mp", "dp")),
            P(("mp", "dp")),
        ),
        out_specs=(
            P(),
            P("dp", None, None),
            P(None, "dp", "mp"),
            P(None, "dp", "mp"),
            P(None, "dp", "mp"),
            P("dp", "mp"),
            P("dp", "mp"),
            P("dp", "mp"),
            P("dp", "mp"),
            P("dp", "mp"),
            P("dp", "mp"),
            P("dp", "mp"),
            P("dp", "mp"),
            P("dp", "mp"),
            P(None, "dp"),
            P(None, "dp"),
            P(None, "dp"),
            P(None, ("mp", "dp")),
            P(None, ("mp", "dp")),
            P(None, ("mp", "dp")),
            P(("mp", "dp")),
            P(("mp", "dp")),
            P(("mp", "dp")),
            P(),
        ),
        check_vma=False,
    )
```

```python
import functools

import jax
import jax.numpy as jnp
from jax import lax
from jax.experimental import pallas as pl
from jax.experimental.pallas import tpu as pltpu
from jax.sharding import PartitionSpec as P

HD = 64
STEP = 10


norm_epsilon = 1e-06
mask_value = -1000000000.0
sharpness_divisor = 50.0
loss_scale = 128.0
beta_first = 0.9
beta_second = 0.999
adam_epsilon = 1e-06
weight_decay = 0.01
learning_rate = 0.5
exact_arithmetic_mode = lax.Precision.HIGHEST


def layer_norm(values, gain, shift):
    center = values - jnp.mean(values, -1, keepdims=True)
    spread = jnp.mean(center * center, -1, keepdims=True)
    return center * lax.rsqrt(spread + norm_epsilon) * gain + shift


def normalize(values):
    return values * lax.rsqrt(jnp.sum(values * values, -1, keepdims=True) + norm_epsilon)


def summation_axes_spec(left, right, left_dim, right_dim):
    return lax.dot_general(
        left, right, (((left_dim,), (right_dim,)), ((), ())), preferred_element_type=jnp.float32
    )


def moments(weight, first, second, grad, decay):
    first_new = beta_first * first + (1.0 - beta_first) * grad
    second_new = beta_second * second + (1.0 - beta_second) * grad * grad
    first_hat = first_new / (1.0 - beta_first**STEP)
    second_hat = second_new / (1.0 - beta_second**STEP)
    update = first_hat / (jnp.sqrt(second_hat) + adam_epsilon) + decay * weight
    return (first_new, second_new, update)


def tensor_squares(qkv, out, upper, lower, affine, head, inner, replicas):
    return jnp.concatenate(
        [
            jnp.sum(qkv * qkv, (1, 2)),
            jnp.sum(out * out)[None],
            jnp.sum(upper * upper)[None],
            jnp.sum(lower * lower)[None],
            jnp.sum(affine * affine, 1) / replicas,
            jnp.sum(head * head, 1),
            jnp.sum(inner * inner)[None],
        ]
    )


def split_norms(norms):
    return (
        norms[0:3].reshape(3, 1, 1),
        norms[3],
        norms[4],
        norms[5],
        norms[6:12].reshape(6, 1),
        norms[12:14].reshape(2, 1),
        norms[14],
    )


def scaled_step(weight, update, weight_norm, update_norm):
    return weight - learning_rate * weight_norm / update_norm * update


MESH = pl.DeviceIdType.MESH
f32 = jnp.float32
bf16 = jnp.bfloat16
AHEAD, GLAG, RLAG, NROWS = 3, 1, 1, 32


class Place:
    def __init__(self, depth):
        self.depth = depth
        dp = lax.axis_index("dp")
        self.dp = dp
        self.x = lax.axis_index("mp")
        self.z, self.y, self.c = dp // 4, (dp // 2) % 2, dp % 2

    def at(self, z, y, c, x):
        return ((z * 2 + y) * 2 + c, x)

    def over_x(self):
        return self.at(self.z, self.y, self.c, 1 - self.x)

    def over_y(self):
        return self.at(self.z, 1 - self.y, self.c, self.x)

    def over_c(self):
        return self.at(self.z, self.y, 1 - self.c, self.x)

    def over_z(self, k):
        return self.at(lax.rem(self.z + k, self.depth), self.y, self.c, self.x)

    def in_plane(self, d):
        return self.at(self.z, 1 - self.y if d & 4 else self.y, 1 - self.c if d & 2 else self.c, 1 - self.x if d & 1 else self.x)

    def greet(self):
        sem = pltpu.get_barrier_semaphore()
        for peer in [self.in_plane(d) for d in range(1, 8)] + [self.over_z(k) for k in range(1, self.depth)]:
            pl.semaphore_signal(sem, inc=1, device_id=peer, device_id_type=MESH)

    def meet(self):
        pl.semaphore_wait(pltpu.get_barrier_semaphore(), 7 + self.depth - 1)


class Wire:
    def __init__(self, send, recv):
        self.send, self.recv, self.used, self.open = send, recv, 0, []

    def start(self, src, dst, device):
        i = self.used
        self.used += 1
        copy = pltpu.make_async_remote_copy(
            src_ref=src, dst_ref=dst, send_sem=self.send.at[i], recv_sem=self.recv.at[i], device_id=device, device_id_type=MESH
        )
        copy.start()
        self.open.append(copy)
        return copy

    def close(self):
        for copy in self.open:
            copy.wait_send()
        self.open = []


def arrive(copies):
    for copy in copies:
        copy.wait_recv()


class Flow:
    def __init__(self, stages, lags):
        self.stages, self.lags, self.done = stages, lags, [0] * len(stages)

    def run(self, s):
        self.stages[s](self.done[s])
        self.done[s] += 1

    def pump(self, lags=None):
        moved = False
        for s in range(len(self.stages) - 1, 0, -1):
            if self.done[s] < self.done[s - 1] - (self.lags if lags is None else lags)[s]:
                self.run(s)
                moved = True
        return moved

    def drain(self):
        while self.pump([0] * len(self.stages)):
            pass


class Sheet:
    def __init__(self, full, u):
        self.full, self.u, self.half = full, u, full.shape[-1] // 2

    def part(self, z, y, c, x=None):
        lanes = pl.ds(0, 2 * self.half) if x is None else pl.ds(pl.multiple_of(x * self.half, 128), self.half)
        return self.full.at[self.u, z, y, c, :, lanes]


class Gather:
    def __init__(self, place, wire, items, ahead, lag):
        self.p, self.wire, self.items, self.ahead = place, wire, items, ahead
        self.flight = {}
        self.flow = Flow([self.far, self.one, self.two, self.core, self.whole], [0, 0, lag, lag, 1])

    def far(self, i):
        p, it = self.p, self.items[i]
        mine = it.part(p.z, p.y, p.c, p.x)
        self.flight["z", i] = [self.wire.start(mine, mine, p.over_z(k)) for k in range(1, p.depth)]

    def one(self, i):
        p, it, h = self.p, self.items[i], self.p.depth // 2
        arrive(self.flight["z", i])
        a = it.part(pl.ds(0, h), p.y, p.c, p.x)
        b = it.part(pl.ds(h, p.depth - h), p.y, p.c, p.x)
        self.flight["1", i] = [self.wire.start(a, a, p.over_x()), self.wire.start(b, b, p.over_y())]

    def two(self, i):
        p, it, h = self.p, self.items[i], self.p.depth // 2
        arrive(self.flight["1", i])
        a = it.part(pl.ds(0, h), p.y, p.c)
        b = it.part(pl.ds(h, p.depth - h), slice(None), p.c, p.x)
        self.flight["2", i] = [self.wire.start(a, a, p.over_y()), self.wire.start(b, b, p.over_x())]

    def core(self, i):
        p, it = self.p, self.items[i]
        arrive(self.flight["2", i])
        r = it.part(slice(None), slice(None), p.c)
        self.flight["c", i] = [self.wire.start(r, r, p.over_c())]

    def whole(self, i):
        arrive(self.flight["c", i])

    def begin(self):
        flow, n = self.flow, len(self.items)
        while flow.done[0] < min(flow.done[1] + self.ahead, n):
            flow.run(0)

    def step(self):
        flow, n = self.flow, len(self.items)
        while flow.done[0] < min(flow.done[1] + self.ahead, n):
            flow.run(0)
        moved = flow.pump([0] * 5 if flow.done[1] == n else None)
        while flow.done[0] < min(flow.done[1] + self.ahead, n):
            flow.run(0)
        return moved

    def until(self, i):
        while self.flow.done[4] <= i:
            self.step()


def add_blocks(dst, src, count):
    def step(i, carry):
        (d, at), (s, of) = dst(i), src(i)
        d[at] = (d[at].astype(f32) + s[of].astype(f32)).astype(d.dtype)
        return carry

    lax.fori_loop(0, count, step, 0)


class Reduce:
    def __init__(self, place, wire, order, lag, free, part, from_core, one_a, one_b, two_a, two_b, from_z, total, use):
        self.p, self.wire, self.order, self.free, self.use = place, wire, order, free, use
        self.part, self.from_core, self.one_a, self.one_b = part, from_core, one_a, one_b
        self.two_a, self.two_b, self.from_z, self.total = two_a, two_b, from_z, total
        self.h = place.depth // 2
        self.half = part.shape[-1] // 2
        self.slots = from_core.shape[0]
        self.flight = {}
        self.flow = Flow([self.core, self.one, self.two, self.far, self.last], [0, 1, lag, lag, lag])

    def lanes(self, x):
        return pl.ds(pl.multiple_of(x * self.half, 128), self.half)

    def core(self, i):
        p, u = self.p, self.order[i]
        if i >= self.slots:
            pl.semaphore_wait(self.free, 1)
        self.flight["c", i] = [self.wire.start(self.part.at[u, :, :, 1 - p.c], self.from_core.at[i % self.slots], p.over_c())]

    def one(self, i):
        p, u, h, Z, part = self.p, self.order[i], self.h, self.p.depth, self.part
        arrive(self.flight["c", i])
        add_blocks(
            lambda j: (part, (u, j // 2, j % 2, p.c)),
            lambda j: (self.from_core, (i % self.slots, j // 2, j % 2)), 2 * Z,
        )
        if i + self.slots < len(self.order):
            pl.semaphore_signal(self.free, inc=1, device_id=p.over_c(), device_id_type=MESH)
        self.flight["1", i] = [
            self.wire.start(part.at[u, pl.ds(0, h), :, p.c, :, self.lanes(1 - p.x)], self.one_a.at[u], p.over_x()),
            self.wire.start(part.at[u, pl.ds(h, Z - h), 1 - p.y, p.c], self.one_b.at[u], p.over_y()),
        ]

    def two(self, i):
        p, u, h, Z, part = self.p, self.order[i], self.h, self.p.depth, self.part
        arrive(self.flight["1", i])
        mine = self.lanes(p.x)
        add_blocks(lambda j: (part, (u, j // 2, j % 2, p.c, slice(None), mine)), lambda j: (self.one_a, (u, j // 2, j % 2)), 2 * h)
        add_blocks(lambda j: (part, (u, h + j, p.y, p.c)), lambda j: (self.one_b, (u, j)), Z - h)
        self.flight["2", i] = [
            self.wire.start(part.at[u, pl.ds(0, h), 1 - p.y, p.c, :, mine], self.two_a.at[u], p.over_y()),
            self.wire.start(part.at[u, pl.ds(h, Z - h), p.y, p.c, :, self.lanes(1 - p.x)], self.two_b.at[u], p.over_x()),
        ]

    def far(self, i):
        p, u, h, Z, part = self.p, self.order[i], self.h, self.p.depth, self.part
        arrive(self.flight["2", i])
        mine = self.lanes(p.x)
        add_blocks(lambda j: (part, (u, j, p.y, p.c, slice(None), mine)), lambda j: (self.two_a, (u, j)), h)
        add_blocks(lambda j: (part, (u, h + j, p.y, p.c, slice(None), mine)), lambda j: (self.two_b, (u, j)), Z - h)
        self.flight["z", i] = [
            self.wire.start(part.at[u, lax.rem(p.z + k, Z), p.y, p.c, :, mine], self.from_z.at[k - 1, u], p.over_z(k))
            for k in range(1, Z)
        ]

    def last(self, i):
        p, u = self.p, self.order[i]
        arrive(self.flight["z", i])
        t = self.part[u, p.z, p.y, p.c, :, self.lanes(p.x)].astype(f32)
        for j in range(p.depth - 1):
            t = t + self.from_z[j, u].astype(f32)
        self.total[u] = t
        self.use(u, t)

    def step(self):
        self.flow.run(0)
        self.flow.pump()

    def pump(self):
        self.flow.pump()

    def finish(self):
        self.flow.drain()


class SumAll:
    def __init__(self, place, wire, own, room):
        self.p, self.wire, self.own, self.room = place, wire, own, room
        self.stage = 0

    def start(self):
        p = self.p
        if self.stage < 3:
            device = (p.over_c, p.over_x, p.over_y)[self.stage]()
            self.flight = [self.wire.start(self.own, self.room.at[self.stage], device)]
        else:
            self.flight = [self.wire.start(self.own, self.room.at[3 + p.z], p.over_z(k)) for k in range(1, p.depth)]

    def finish(self):
        p = self.p
        arrive(self.flight)
        for copy in self.flight:
            copy.wait_send()
        self.wire.open = [c for c in self.wire.open if all(c is not f for f in self.flight)]
        if self.stage < 3:
            self.own[...] = self.own[...] + self.room[self.stage]
        else:
            self.room[3 + p.z] = self.own[...]
            t = self.room[3]
            for z in range(1, p.depth):
                t = t + self.room[3 + z]
            self.own[...] = t
        self.stage += 1

    def run(self):
        while self.stage < 4:
            self.start()
            self.finish()


class SumSoon:
    def __init__(self, place, wire, own, plane, line):
        p = place
        slot = (p.y * 2 + p.c) * 2 + p.x
        plane[slot] = own[...]
        arrive([wire.start(own, plane.at[slot], p.in_plane(d)) for d in range(1, 8)])
        value = plane[0]
        for d in range(1, 8):
            value = value + plane[d]
        line[p.z] = value
        arrive([wire.start(line.at[p.z], line.at[p.z], p.over_z(k)) for k in range(1, p.depth)])
        value = line[0]
        for z in range(1, p.depth):
            value = value + line[z]
        self.value = value


class Pictures:
    def __init__(self, place, wire, full):
        self.p, self.wire, self.full = place, wire, full
        mine = full.at[place.z, place.y, place.c]
        self.flight = [wire.start(mine, mine, place.over_y())]
        self.sent = 0

    def far(self):
        p = self.p
        if self.sent == 0:
            arrive(self.flight)
            self.flight = []
        mine = self.full.at[p.z, :, p.c]
        self.sent += 1
        self.flight.append(self.wire.start(mine, mine, p.over_z(self.sent)))

    def core(self):
        p = self.p
        while self.sent < p.depth - 1:
            self.far()
        arrive(self.flight)
        r = self.full.at[:, :, p.c]
        self.flight = [self.wire.start(r, r, p.over_c())]

    def whole(self):
        arrive(self.flight)


def dot(a, b, left=1, right=0):
    return lax.dot_general(a, b, (((left,), (right,)), ((), ())), preferred_element_type=f32)


def row_loop(count, size, f, start=0):
    def step(i, carry):
        f(pl.ds(pl.multiple_of(start + i * size, size), size))
        return carry

    lax.fori_loop(0, count // size, step, 0)


def center_scale(x):
    center = x - jnp.mean(x, -1, keepdims=True)
    return center, lax.rsqrt(jnp.mean(center * center, -1, keepdims=True) + norm_epsilon)


def three(x):
    hi = x.astype(bf16)
    rest = x - hi.astype(f32)
    mid = rest.astype(bf16)
    return hi, mid, (rest - mid.astype(f32)).astype(bf16)


def fold(x):
    return jnp.sum(x.reshape(x.shape[0] // 8, 8, x.shape[1]), 0)


def placing(n, at, lanes):
    spot = lax.broadcasted_iota(jnp.int32, (n, lanes), 1) == lax.broadcasted_iota(jnp.int32, (n, lanes), 0) + at
    return jnp.where(spot, 1.0, 0.0).astype(bf16)


def picked(a, at, n):
    spot = placing(n, at, a.shape[1])
    return sum(dot(term, spot, 1, 1) for term in three(a))


def row_of(a, at):
    rows = lax.broadcasted_iota(jnp.int32, a.shape, 0) == at
    return jnp.sum(jnp.where(rows, a, jnp.zeros_like(a)), 0, keepdims=True)


def block_kernel(
    depth,
    tokens, segment, pairing, images, qkv_weight, out_weight, up_weight, down_weight, affine, head_bias, inner_bias,
    qkv_first, qkv_second, out_first, out_second, up_first, up_second, down_first, down_second,
    affine_first, affine_second, head_first, head_second, inner_first, inner_second,
    total, small_grad, norms, grad_low,
    full, pictures, part, from_core, one_a, one_b, two_a, two_b, from_z,
    tok, normed_one, qkv, mixed, resid, normed_two, hidden, slope, stream, grad_mixed, acc, low,
    probs, same, wide, sums, room, room2, folds, cap,
    old_qkv, old_out, old_up, old_down, squares, tile_sums, plane, line,
    send, recv, free, local, local_old,
):
    place = Place(depth)
    place.greet()
    x, dp = place.x, place.dp
    rows, width = tok.shape
    packs, length = 2, rows // 2
    half = qkv_weight.shape[2]
    units = full.shape[0]
    share = full.shape[4]
    blocks = up_weight.shape[1] // half
    up0, down0 = 4, 4 + blocks

    token_copies = [
        pltpu.make_async_copy(tokens.at[packs * x + p], tok.at[pl.ds(p * length, length)], local.at[p]) for p in range(packs)
    ]
    pairs_old = ((qkv_first, qkv_second, old_qkv), (out_first, out_second, old_out), (up_first, up_second, old_up), (down_first, down_second, old_down))
    old_copies = []
    for i, (one, two, kept) in enumerate(pairs_old):
        old_copies += [pltpu.make_async_copy(one, kept.at[0], local_old.at[2 * i]), pltpu.make_async_copy(two, kept.at[1], local_old.at[2 * i + 1])]
    for copy in token_copies + old_copies:
        copy.start()

    mine_lanes = pl.ds(pl.multiple_of(x * half, 128), half)

    def keep(u, value):
        full[u, place.z, place.y, place.c, :, mine_lanes] = value.astype(bf16)

    for k in range(3):
        keep(k, qkv_weight[k])
    keep(3, out_weight[...])
    for j in range(blocks):
        keep(up0 + j, up_weight[:, j * half : (j + 1) * half])
        keep(down0 + j, down_weight[:, j * half : (j + 1) * half])
    pictures[place.z, place.y, place.c] = normalize(images[...].astype(f32)).astype(bf16)

    place.meet()
    wire = Wire(send, recv)
    gather = Gather(place, wire, [Sheet(full, u) for u in range(units)], AHEAD, GLAG)
    ready = gather.until
    gather.begin()
    scenes = Pictures(place, wire, pictures)

    owner = x * (4 * depth) + dp
    n_affine, n_head, n_inner = affine.shape[1], head_bias.shape[1], inner_bias.shape[1]
    first = jnp.where(x == 0, 1.0, 0.0)
    inner_rows = 2 * blocks * half // width
    inner_at, inner_row = (owner * n_inner) % width, (owner * n_inner) // width
    wide[...] = jnp.zeros_like(wide)
    wide[0:6] = dot(affine[...].astype(bf16), placing(n_affine, dp * n_affine, width)) * first
    wide[6:8] = dot(head_bias[...].astype(bf16), placing(n_head, owner * n_head, width))
    inner_wide = dot(inner_bias[...].astype(bf16), placing(n_inner, inner_at, width))
    at_row = lax.broadcasted_iota(jnp.int32, (inner_rows, width), 0) == inner_row
    wide[8 : 8 + inner_rows] = jnp.where(at_row, jnp.broadcast_to(inner_wide, (inner_rows, width)), 0.0)
    spread = SumAll(place, wire, wide, room)
    spread.start()

    slots = pairing.shape[1]
    tile, window = 64, 128
    starts = [min(max(t * tile - (window - tile) // 2, 0), length - window) for t in range(length // tile)]
    onehots = []
    for p in range(packs):
        seg = jnp.broadcast_to(row_of(segment[...], packs * x + p), (slots, length))
        onehot = jnp.where(seg == lax.broadcasted_iota(jnp.int32, (slots, length), 0), 1.0, 0.0)
        onehots.append(onehot)
        low_hot = onehot.astype(bf16)
        both = acc.at[pl.ds(0, length), pl.ds(0, length)]
        both[...] = dot(low_hot, low_hot, 0, 0)
        for t, w in enumerate(starts):
            shared = dot(both[pl.ds(t * tile, tile)].astype(bf16), placing(window, w, length), 1, 1)
            same[p, t, 0:tile] = shared
            same[p, t, tile : 2 * tile] = shared
        if p == 0:
            spread.finish()
            spread.start()
    gather.step()
    spread.finish()
    spread.start()
    gather.step()
    spread.finish()
    spread.start()
    gather.step()
    scenes.far()
    spread.finish()

    for copy in token_copies:
        copy.wait()

    def norm_one(r):
        center, scale = center_scale(tok[r].astype(f32))
        normed_one[r] = (center * scale * wide[0:1] + wide[1:2]).astype(bf16)

    row_loop(rows, NROWS, norm_one)
    gather.step()

    def unit(u):
        return full[u].reshape(width, width)

    chunk = 256

    def unit_lanes(u, j):
        return full[u, :, :, :, :, pl.ds(j * chunk, chunk)].reshape(width, chunk)

    for k in range(3):
        ready(k)
        for j in range(width // chunk):
            lanes = pl.ds(j * chunk, chunk)
            value = dot(normed_one[...], unit_lanes(k, j))
            if k != 1:
                row = 6 if k == 0 else 7
                value = value + wide[row : row + 1, lanes]
            qkv[k, :, lanes] = value.astype(bf16)
    scenes.far()

    root_scale = HD**-0.5
    pair = 2 * HD
    pairs = width // pair
    lower = lax.broadcasted_iota(jnp.int32, (tile, pair), 1) < HD

    def doubled(a):
        zero = jnp.zeros_like(a)
        return jnp.concatenate([jnp.where(lower, a, zero), jnp.where(lower, zero, a)], 0)

    def joined(a):
        return jnp.where(lower, a[:tile], a[tile:])

    def attend(p, g):
        lanes = pl.ds(pl.multiple_of(g * pair, pair), pair)
        span = pl.ds(p * length, length)
        query, keys, values = qkv[0, span, lanes], qkv[1, span, lanes], qkv[2, span, lanes]
        found, weights = [], []
        for t, w in enumerate(starts):
            scores = dot(doubled(query[t * tile : (t + 1) * tile]), keys[w : w + window], 1, 1) * root_scale
            scores = jnp.where(same[p, t] > 0.5, scores, mask_value)
            e = jnp.exp(scores - jnp.max(scores, -1, keepdims=True))
            prob = (e * (1.0 / jnp.sum(e, -1, keepdims=True))).astype(bf16)
            weights.append(prob)
            found.append(joined(dot(prob, values[w : w + window])).astype(bf16))
        for t in range(len(starts)):
            probs[p, g, t] = weights[t]
        mixed[span, lanes] = jnp.concatenate(found, 0)

    def each_pair(f, p, some):
        def step(g, carry):
            f(p, g)
            return carry

        lax.fori_loop(some[0], some[1], step, 0)

    for p in range(packs):
        for some in ((0, pairs // 2), (pairs // 2, pairs)):
            each_pair(attend, p, some)
            gather.step()
    scenes.far()

    ready(3)
    acc[...] = dot(mixed[...], unit(3), 1, 1)
    gather.step()

    def norm_two(r):
        value = tok[r].astype(f32) + acc[r] + wide[4:5]
        resid[r] = value
        center, scale = center_scale(value)
        normed_two[r] = (center * scale * wide[2:3] + wide[3:4]).astype(bf16)
        stream[r] = value + wide[5:6]

    row_loop(rows, NROWS, norm_two)

    def inner_lanes(j):
        at = j * half
        return ((8 + at // width, at % width), (8 + (blocks * half + at) // width, (blocks * half + at) % width))

    curve = (2.0 / jnp.pi) ** 0.5
    for j in range(blocks):
        ready(up0 + j)
        bias = jnp.concatenate([wide[row : row + 1, lane : lane + half] for row, lane in inner_lanes(j)], 1)
        for k in range(width // chunk):
            lanes = pl.ds(k * chunk, chunk)
            acc[:, lanes] = dot(normed_two[...], unit_lanes(up0 + j, k))

        def activate(r, j=j, bias=bias):
            u = acc[r] + bias
            square = u * u
            t = jnp.tanh(curve * (u + 0.044715 * (square * u)))
            hidden[j, r] = (0.5 * u * (1.0 + t)).astype(bf16)
            slope[j, r] = (0.5 * (1.0 + t) + 0.5 * u * (1.0 - t * t) * (curve * (1.0 + 3.0 * 0.044715 * square))).astype(bf16)

        row_loop(rows, 16, activate)
        if j == 1:
            scenes.core()

    for j in range(blocks):
        ready(down0 + j)
        stream[...] += dot(hidden[j], unit(down0 + j), 1, 1)
    scenes.whole()

    count_rows, target_rows = [], []
    for p in range(packs):
        count = jnp.sum(onehots[p], 1, keepdims=True)
        hot = onehots[p].astype(bf16)
        hi, mid, lo = three(stream[pl.ds(p * length, length)])
        pooled = dot(hot, hi) + dot(hot, mid) + dot(hot, lo)
        cap[pl.ds(p * slots, slots)] = pooled / jnp.maximum(count, 1.0)
        count_rows.append(count)
        names = jnp.broadcast_to(row_of(pairing[...], packs * x + p), (slots, slots)).astype(f32)
        diagonal = lax.broadcasted_iota(jnp.int32, (slots, slots), 0) == lax.broadcasted_iota(jnp.int32, (slots, slots), 1)
        target_rows.append(jnp.sum(jnp.where(diagonal, names, 0.0), 1, keepdims=True))
    counts = jnp.concatenate(count_rows, 0)
    target = jnp.concatenate(target_rows, 0)
    live = jnp.where(counts > 0.0, 1.0, 0.0)
    pooled = cap[...]
    radius = lax.rsqrt(jnp.sum(pooled * pooled, -1, keepdims=True) + norm_epsilon)
    caption = (pooled * radius).astype(bf16)
    all_images = pictures[...].reshape(-1, width)
    logits = sharpness_divisor * dot(caption, all_images, 1, 1)
    hit = lax.broadcasted_iota(jnp.int32, logits.shape, 1).astype(f32) == target
    best = jnp.max(logits, -1, keepdims=True)
    e = jnp.exp(logits - best)
    sum_e = jnp.sum(e, -1, keepdims=True)
    positive = jnp.sum(jnp.where(hit, logits, 0.0), -1, keepdims=True)
    cross = best + jnp.log(sum_e) - positive
    loss = jnp.sum(live * cross, 0, keepdims=True)
    grad_logits = (loss_scale * live * (e * (1.0 / sum_e) - jnp.where(hit, 1.0, 0.0))).astype(bf16)
    grad_caption = sharpness_divisor * dot(grad_logits, all_images)
    inner = jnp.sum(pooled * grad_caption, -1, keepdims=True)
    grad_pooled = radius * grad_caption - (radius * radius * radius) * inner * pooled
    grad_pooled = grad_pooled / jnp.maximum(counts, 1.0)
    folds[...] = jnp.zeros_like(folds)
    for p in range(packs):
        hot = onehots[p].astype(bf16)
        hi, mid, lo = three(grad_pooled[p * slots : (p + 1) * slots])
        stream[pl.ds(p * length, length)] = dot(hot, hi, 0, 0) + dot(hot, mid, 0, 0) + dot(hot, lo, 0, 0)

    def lower_stream(r):
        value = stream[r]
        low[r] = value.astype(bf16)
        folds[5] += fold(value)

    row_loop(rows, 32, lower_stream)

    squares[...] = jnp.zeros_like(squares)
    for copy in old_copies:
        copy.wait()

    def lanes_folded(a):
        a = fold(a)
        return sum(a[:, i * 128 : (i + 1) * 128] for i in range(a.shape[1] // 128))

    def use(u, grad):
        if u < 3:
            weight, one, two, row = qkv_weight[u], old_qkv[0, u], old_qkv[1, u], u
        elif u == 3:
            weight, one, two, row = out_weight[...], old_out[0], old_out[1], 3
        else:
            row = 4 if u < down0 else 5
            at = (u - up0) % blocks * half
            weights, kept = (up_weight, old_up) if row == 4 else (down_weight, old_down)
            weight, one, two = weights[:, at : at + half], kept[0, :, at : at + half], kept[1, :, at : at + half]
        update = moments(weight, one, two, grad, weight_decay)[2]
        squares[0, row] += lanes_folded(weight * weight)
        squares[1, row] += lanes_folded(update * update)

    order = [down0 + j for j in range(blocks)] + [up0 + j for j in range(blocks)] + [3, 0, 1, 2]
    reduce = Reduce(place, wire, order, RLAG, free, part, from_core, one_a, one_b, two_a, two_b, from_z, total, use)

    def weight_grad(u, left, right):
        for j in range(width // chunk):
            lanes = pl.ds(j * chunk, chunk)
            value = dot(left, right(lanes), 0, 0).astype(bf16)
            part[u, :, :, :, :, lanes] = value.reshape(depth, 2, 2, share, chunk)
        reduce.step()

    sums[...] = jnp.zeros_like(sums)
    for j in range(blocks):
        weight_grad(down0 + j, low[...], lambda lanes, j=j: hidden[j, :, lanes])
        for k in range(width // chunk):
            lanes = pl.ds(k * chunk, chunk)
            acc[:, lanes] = dot(low[...], unit_lanes(down0 + j, k))

        def upper_back(r, j=j):
            value = (acc[r] * slope[j, r].astype(f32)).astype(bf16)
            hidden[j, r] = value
            folds[6] += fold(value.astype(f32))

        folds[6] = jnp.zeros_like(folds[6])
        row_loop(rows, 32, upper_back)
        inner_sum = jnp.sum(folds[6], 0, keepdims=True)
        for i, (row, lane) in enumerate(inner_lanes(j)):
            sums[row : row + 1, lane : lane + half] = inner_sum[:, i * half : (i + 1) * half]

    for j in range(blocks):
        weight_grad(up0 + j, normed_two[...], lambda lanes, j=j: hidden[j, :, lanes])
        value = dot(hidden[j], unit(up0 + j), 1, 1)
        if j == 0:
            acc[...] = value
        else:
            acc[...] += value

    def norm_two_back(r):
        center, scale = center_scale(resid[r])
        hat = center * scale
        grad = acc[r]
        weighted = grad * wide[2:3]
        value = stream[r] + scale * (
            weighted - jnp.mean(weighted, -1, keepdims=True) - hat * jnp.mean(weighted * hat, -1, keepdims=True)
        )
        stream[r] = value
        low[r] = value.astype(bf16)
        folds[2] += fold(grad * hat)
        folds[3] += fold(grad)
        folds[4] += fold(value)

    row_loop(rows, NROWS, norm_two_back)
    reduce.pump()
    weight_grad(3, low[...], lambda lanes: mixed[:, lanes])
    for k in range(width // chunk):
        lanes = pl.ds(k * chunk, chunk)
        grad_mixed[:, lanes] = dot(low[...], unit_lanes(3, k)).astype(bf16)
    reduce.pump()

    def overlaid(pieces):
        step = 32
        found = []
        for at in range(0, length, step):
            found.append(sum(piece[at - w : at - w + step] for w, piece in zip(starts, pieces) if w <= at < w + window))
        return jnp.concatenate(found, 0)

    def attend_back(p, g):
        lanes = pl.ds(pl.multiple_of(g * pair, pair), pair)
        span = pl.ds(p * length, length)
        query, keys, values, grads = qkv[0, span, lanes], qkv[1, span, lanes], qkv[2, span, lanes], grad_mixed[span, lanes]
        of_query, of_keys, of_values = [], [], []
        for t, w in enumerate(starts):
            some = doubled(query[t * tile : (t + 1) * tile])
            grad = doubled(grads[t * tile : (t + 1) * tile])
            prob = probs[p, g, t]
            prob_wide = prob.astype(f32)
            grad_prob = dot(grad, values[w : w + window], 1, 1)
            grad_score = prob_wide * (grad_prob - jnp.sum(prob_wide * grad_prob, -1, keepdims=True))
            grad_score = grad_score.astype(bf16)
            of_keys.append(dot(grad_score, some, 0, 0))
            of_values.append(dot(prob, grad, 0, 0))
            of_query.append((joined(dot(grad_score, keys[w : w + window])) * root_scale).astype(bf16))
        qkv[0, span, lanes] = jnp.concatenate(of_query, 0)
        qkv[1, span, lanes] = (overlaid(of_keys) * root_scale).astype(bf16)
        qkv[2, span, lanes] = overlaid(of_values).astype(bf16)

    for p in range(packs):
        for some in ((0, pairs // 2), (pairs // 2, pairs)):
            each_pair(attend_back, p, some)
            reduce.pump()

    for k in range(3):
        weight_grad(k, normed_one[...], lambda lanes, k=k: qkv[k, :, lanes])
        value = dot(qkv[k], unit(k), 1, 1)
        if k == 0:
            acc[...] = value
        else:
            acc[...] += value

    def norm_one_back(r):
        center, scale = center_scale(tok[r].astype(f32))
        hat = center * scale
        grad = acc[r]
        weighted = grad * wide[0:1]
        value = stream[r] + scale * (
            weighted - jnp.mean(weighted, -1, keepdims=True) - hat * jnp.mean(weighted * hat, -1, keepdims=True)
        )
        low[r] = value.astype(bf16)
        folds[0] += fold(grad * hat)
        folds[1] += fold(grad)

    swaps, outs = [], []
    for p in range(packs):
        row_loop(length, NROWS, norm_one_back, p * length)
        mine, there = low.at[pl.ds(p * length, length)], grad_low.at[packs * x + p]
        swaps.append(wire.start(mine, there, place.over_x()))
        outs.append(pltpu.make_async_copy(mine, there, local.at[p]))
        outs[-1].start()
        reduce.pump()

    def head_sums(r):
        folds[7] += fold(qkv[0, r].astype(f32))
        folds[8] += fold(qkv[2, r].astype(f32))

    row_loop(rows, 32, head_sums)
    for k, row in ((0, 0), (1, 1), (2, 2), (3, 3), (4, 4), (5, 5), (7, 6), (8, 7)):
        sums[row : row + 1] = jnp.sum(folds[k], 0, keepdims=True)
    last_row = 8 + inner_rows
    sums[last_row : last_row + 1] = jnp.broadcast_to(loss, (1, width))
    small_sum = SumAll(place, wire, sums, room2)
    while small_sum.stage < 4:
        small_sum.start()
        reduce.pump()
        small_sum.finish()

    small_grad[...] = jnp.zeros_like(small_grad)
    tile_sums[...] = jnp.zeros_like(tile_sums)
    of_affine = picked(sums[0:6], dp * n_affine, n_affine)
    of_head = picked(sums[6:8], owner * n_head, n_head)
    of_inner = picked(row_of(sums[8 : 8 + inner_rows], inner_row), inner_at, n_inner)
    small_grad[0:6, 0:n_affine] = of_affine
    small_grad[6:8, 0:n_head] = of_head
    small_grad[8:9, 0:n_inner] = of_inner
    small_grad[9:10] = sums[last_row : last_row + 1, 0:128]
    smalls = (
        (6, 6, n_affine, affine[...], affine_first[...], affine_second[...], of_affine, first),
        (12, 2, n_head, head_bias[...], head_first[...], head_second[...], of_head, 1.0),
        (14, 1, n_inner, inner_bias[...], inner_first[...], inner_second[...], of_inner, 1.0),
    )
    for row, n, lanes, weight, one, two, grad, share_of in smalls:
        update = moments(weight, one, two, grad, 0.0)[2]
        tile_sums[row : row + n, 0:lanes] = weight * weight * share_of
        tile_sums[16 + row : 16 + row + n, 0:lanes] = update * update * share_of

    reduce.finish()
    for k in range(2):
        for row in range(6):
            tile_sums[16 * k + row : 16 * k + row + 1] = jnp.sum(squares[k, row], 0, keepdims=True)
    every = SumSoon(place, wire, tile_sums, plane, line).value
    norms[...] = jnp.broadcast_to(jnp.sqrt(jnp.sum(every, -1, keepdims=True)), norms.shape)
    arrive(swaps)
    for copy in outs:
        copy.wait()
    wire.close()


def block_step(depth, *arrays):
    tokens, segment, pairing, images, qkv_weight, out_weight, up_weight, down_weight = arrays[:8]
    packs, length, width = tokens.shape
    rows = packs // 2 * length
    share, half = qkv_weight.shape[1:]
    blocks = up_weight.shape[1] // half
    units = 4 + 2 * blocks
    slots = pairing.shape[1]
    h = depth // 2
    few = images.shape[0]
    ring = 4
    small = (16, width)
    low = lambda *shape: pltpu.VMEM(shape, bf16)
    wide = lambda *shape: pltpu.VMEM(shape, f32)
    count = units * (depth - 1 + 5) + (depth - 1 + 2) + units * (5 + depth - 1) + 2 * (3 + depth - 1) + 2 + 7 + depth - 1
    vmem = pl.BlockSpec(memory_space=pltpu.VMEM)
    hbm = pl.BlockSpec(memory_space=pl.ANY)
    return pl.pallas_call(
        functools.partial(block_kernel, depth),
        out_shape=(
            jax.ShapeDtypeStruct((units, share, half), f32),
            jax.ShapeDtypeStruct((16, 128), f32),
            jax.ShapeDtypeStruct((32, 128), f32),
            jax.ShapeDtypeStruct(tokens.shape, bf16),
        ),
        in_specs=[hbm] + [vmem] * 10 + [hbm] * 8 + [vmem] * 6,
        out_specs=[vmem, vmem, vmem, hbm],
        scratch_shapes=[
            low(units, depth, 2, 2, share, width), low(depth, 2, 2, few, width),
            low(units, depth, 2, 2, share, width), low(ring, depth, 2, share, width), low(units, h, 2, share, half),
            low(units, depth - h, share, width), low(units, h, share, half), low(units, depth - h, share, half),
            low(depth - 1, units, share, half),
            low(rows, width), low(rows, width), low(3, rows, width), low(rows, width), wide(rows, width), low(rows, width),
            low(blocks, rows, width), low(blocks, rows, width), wide(rows, width), low(rows, width), wide(rows, width), low(rows, width),
            low(2, width // (2 * HD), length // 64, 128, 128), wide(2, length // 64, 128, 128), wide(*small), wide(*small),
            wide(3 + depth, *small), wide(3 + depth, *small), wide(9, 8, width), wide(2 * slots, width),
            wide(2, *qkv_weight.shape), wide(2, *out_weight.shape), wide(2, *up_weight.shape), wide(2, *down_weight.shape),
            wide(2, 6, 8, 128), wide(32, 128), wide(8, 32, 128), wide(depth, 32, 128),
            pltpu.SemaphoreType.DMA((count,)), pltpu.SemaphoreType.DMA((count,)), pltpu.SemaphoreType.REGULAR,
            pltpu.SemaphoreType.DMA((2,)), pltpu.SemaphoreType.DMA((8,)),
        ],
        compiler_params=pltpu.CompilerParams(collective_id=1, has_side_effects=True, vmem_limit_bytes=64 << 20),
        name="train_block",
    )(*arrays)


def finish_kernel(slot_total, total, small_grad, norms, grad_low, *refs):
    weights, firsts, seconds = refs[0:7], refs[7:14], refs[14:21]
    grad_input = refs[21]
    nexts, first_nexts, second_nexts = refs[22:29], refs[29:36], refs[36:43]
    mean_loss, tensor_norms, room, wide_room, sems = refs[43:48]
    packs = grad_low.shape[0]
    reads = [pltpu.make_async_copy(grad_low.at[p], room.at[p], sems.at[p]) for p in range(packs)]
    writes = [pltpu.make_async_copy(wide_room.at[p], grad_input.at[p], sems.at[packs + p]) for p in range(packs)]
    for copy in reads:
        copy.start()

    def update(i, at, grad, row, decay):
        weight, one, two = weights[i][at], firsts[i][at], seconds[i][at]
        first_new, second_new, change = moments(weight, one, two, grad, decay)
        first_nexts[i][at] = first_new
        second_nexts[i][at] = second_new
        count = 1 if isinstance(row, int) else row[1]
        row = row if isinstance(row, int) else row[0]
        weight_norm, update_norm = norms[row : row + count, 0:1], norms[16 + row : 16 + row + count, 0:1]
        nexts[i][at] = weight - learning_rate * weight_norm / update_norm * change

    every = slice(None)
    half = total.shape[2]
    blocks = weights[2].shape[1] // half
    for p in range(packs):
        reads[p].wait()

        def widen(r, p=p):
            wide_room[p, r] = room[p, r].astype(f32)

        row_loop(room.shape[1], 32, widen)
        writes[p].start()
    for k in range(3):
        update(0, (k,), total[k], k, weight_decay)
    update(1, (every,), total[3], 3, weight_decay)
    for i in range(2):
        for j in range(blocks):
            update(2 + i, (every, slice(j * half, (j + 1) * half)), total[4 + i * blocks + j], 4 + i, weight_decay)
    update(4, (every,), small_grad[0:6, 0 : weights[4].shape[1]], (6, 6), 0.0)
    update(5, (every,), small_grad[6:8, 0 : weights[5].shape[1]], (12, 2), 0.0)
    update(6, (every,), small_grad[8:9, 0 : weights[6].shape[1]], 14, 0.0)
    mean_loss[...] = small_grad[9:10, 0:1] / slot_total
    square = norms.shape[0] // 2
    diagonal = lax.broadcasted_iota(jnp.int32, (square, square), 0) == lax.broadcasted_iota(jnp.int32, (square, square), 1)
    for k in range(2):
        column = jnp.broadcast_to(norms[square * k : square * (k + 1), 0:1], (square, square))
        tensor_norms[k : k + 1] = jnp.sum(jnp.where(diagonal, column, 0.0), 0, keepdims=True)[:, 0:15]
    for copy in writes:
        copy.wait()


def finish_step(slot_total, total, small_grad, norms, grad_low, weights, firsts, seconds):
    vmem = pl.BlockSpec(memory_space=pltpu.VMEM)
    hbm = pl.BlockSpec(memory_space=pl.ANY)
    packs, length, width = grad_low.shape
    like = [jax.ShapeDtypeStruct(a.shape, f32) for a in weights]
    return pl.pallas_call(
        functools.partial(finish_kernel, slot_total),
        out_shape=(
            jax.ShapeDtypeStruct(grad_low.shape, f32), *like, *like, *like,
            jax.ShapeDtypeStruct((1, 1), f32), jax.ShapeDtypeStruct((2, 15), f32),
        ),
        in_specs=[vmem] * 3 + [hbm] + [vmem] * 21,
        out_specs=[hbm] + [vmem] * 23,
        scratch_shapes=[
            pltpu.VMEM((packs, length, width), bf16), pltpu.VMEM((packs, length, width), f32),
            pltpu.SemaphoreType.DMA((2 * packs,)),
        ],
        compiler_params=pltpu.CompilerParams(vmem_limit_bytes=64 << 20),
        name="optimizer",
    )(total, small_grad, norms, grad_low, *weights, *firsts, *seconds)


def body_near(depth, *arrays):
    (
        tokens, segment, pairing, images,
        qkv_weight, qkv_first, qkv_second, out_weight, out_first, out_second,
        up_weight, up_first, up_second, down_weight, down_first, down_second,
        affine, affine_first, affine_second, head_bias, head_first, head_second,
        inner_bias, inner_first, inner_second,
    ) = arrays
    inner_bias, inner_first, inner_second = (a.reshape(1, -1) for a in (inner_bias, inner_first, inner_second))
    total, small_grad, norms, grad_low = block_step(
        depth, tokens, segment, pairing, images, qkv_weight, out_weight, up_weight, down_weight, affine, head_bias, inner_bias,
        qkv_first, qkv_second, out_first, out_second, up_first, up_second, down_first, down_second,
        affine_first, affine_second, head_first, head_second, inner_first, inner_second,
    )
    weights = (qkv_weight, out_weight, up_weight, down_weight, affine, head_bias, inner_bias)
    firsts = (qkv_first, out_first, up_first, down_first, affine_first, head_first, inner_first)
    seconds = (qkv_second, out_second, up_second, down_second, affine_second, head_second, inner_second)
    slot_total = float(pairing.size * 4 * depth)
    grad_input, *news, mean_loss, tensor_norms = finish_step(slot_total, total, small_grad, norms, grad_low, weights, firsts, seconds)
    results = [mean_loss.reshape(()), grad_input]
    for i in range(7):
        triple = (news[i], news[7 + i], news[14 + i])
        results += [a.reshape(-1) for a in triple] if i == 6 else triple
    return (*results, tensor_norms)


def body(
    tokens,
    segment,
    pairing,
    images,
    qkv_weight,
    qkv_first,
    qkv_second,
    out_weight,
    out_first,
    out_second,
    up_weight,
    up_first,
    up_second,
    down_weight,
    down_first,
    down_second,
    affine,
    affine_first,
    affine_second,
    head_bias,
    head_first,
    head_second,
    inner_bias,
    inner_first,
    inner_second,
):
    model_size = lax.axis_size("mp")
    packs, length, width = tokens.shape
    rows = packs * length
    qkv_full, out_full, up_full, down_full, affine_full, head_full, inner_full = (
        lax.all_gather(qkv_weight.astype(jnp.bfloat16), "dp", axis=1, tiled=True),
        lax.all_gather(out_weight.astype(jnp.bfloat16), "dp", axis=0, tiled=True),
        lax.all_gather(up_weight.astype(jnp.bfloat16), "dp", axis=0, tiled=True),
        lax.all_gather(down_weight.astype(jnp.bfloat16), "dp", axis=0, tiled=True),
        lax.all_gather(affine.astype(jnp.bfloat16), "dp", axis=1, tiled=True),
        lax.all_gather(head_bias.astype(jnp.bfloat16), "dp", axis=1, tiled=True),
        lax.all_gather(inner_bias.astype(jnp.bfloat16), "dp", axis=0, tiled=True),
    )
    affine_wide = affine_full.astype(jnp.float32)
    head_wide = head_full.astype(jnp.float32)
    inner_wide = inner_full.astype(jnp.float32)
    half = qkv_full.shape[2]
    local_heads = half // HD
    shape4 = (packs, length, local_heads, HD)
    root_scale = HD ** (-0.5)
    inputs = tokens.reshape(rows, width).astype(jnp.float32)
    normed_one = layer_norm(inputs, affine_wide[0], affine_wide[1]).astype(jnp.bfloat16)
    projected = jnp.einsum("td,kde->kte", normed_one, qkv_full, preferred_element_type=jnp.float32)
    query = (projected[0] + head_wide[0]).astype(jnp.bfloat16).reshape(shape4)
    keys = projected[1].astype(jnp.bfloat16).reshape(shape4)
    values = (projected[2] + head_wide[1]).astype(jnp.bfloat16).reshape(shape4)
    same = segment[:, None, :, None] == segment[:, None, None, :]

    def masked_scores():
        raw = (
            jnp.einsum("pqhe,pkhe->phqk", query, keys, preferred_element_type=jnp.float32)
            * root_scale
        )
        return jnp.where(same, raw, mask_value)

    scores = masked_scores()
    top = jnp.max(scores, -1, keepdims=True)
    log_total = top + jnp.log(jnp.sum(jnp.exp(scores - top), -1, keepdims=True))
    probs = jnp.exp(scores - log_total).astype(jnp.bfloat16)
    mixed = jnp.einsum("phqk,pkhe->pqhe", probs, values, preferred_element_type=jnp.float32)
    mixed = mixed.reshape(rows, half).astype(jnp.bfloat16)
    attended = lax.psum(summation_axes_spec(mixed, out_full, 1, 1), "mp")
    resid = inputs + attended + affine_wide[4]
    normed_two = layer_norm(resid, affine_wide[2], affine_wide[3]).astype(jnp.bfloat16)
    upper = jnp.dot(normed_two, up_full, preferred_element_type=jnp.float32) + inner_wide
    activated, gelu_back = jax.vjp(jax.nn.gelu, upper)
    hidden = activated.astype(jnp.bfloat16)
    lowered = lax.psum(
        summation_axes_spec(hidden, down_full, 1, 1).astype(jnp.bfloat16), "mp"
    ).astype(jnp.float32)
    output = resid + lowered + affine_wide[5]
    slots = pairing.shape[1]
    onehot = (segment[:, None, :] == jnp.arange(slots, dtype=jnp.int32)[None, :, None]).astype(
        jnp.float32
    )
    counts = jnp.sum(onehot, -1)
    divisor = jnp.maximum(counts, 1.0)[..., None]
    pooled = (
        jnp.einsum(
            "pcl,pld->pcd",
            onehot,
            output.reshape(packs, length, width),
            precision=exact_arithmetic_mode,
        )
        / divisor
    )
    flat = pooled.reshape(packs * slots, width)
    caption_wide, normalize_back = jax.vjp(normalize, flat)
    sentence_words = caption_wide.astype(jnp.bfloat16)
    live = (counts > 0).reshape(-1).astype(jnp.float32)
    target = pairing.reshape(-1)
    captions_count = flat.shape[0]
    slot_total = float(captions_count * lax.axis_size("dp"))
    picture_summed = normalize(images.astype(jnp.float32)).astype(jnp.bfloat16)

    def similarity(packed_sequence_slice):
        return sharpness_divisor * summation_axes_spec(sentence_words, packed_sequence_slice, 1, 1)

    score_packed_sequence_slice = lax.all_gather(picture_summed, "dp", axis=0, tiled=True)
    best = jnp.full((captions_count,), mask_value, jnp.float32)
    similarity_grid = similarity(score_packed_sequence_slice)
    new_best = jnp.maximum(best, jnp.max(similarity_grid, 1))
    total = jnp.sum(jnp.exp(similarity_grid - new_best[:, None]), 1)
    column = jnp.arange(score_packed_sequence_slice.shape[0], dtype=jnp.int32)
    hit = target[:, None] == column[None, :]
    positive = jnp.sum(jnp.where(hit, similarity_grid, 0.0), 1)
    best_all, total_all, positive = (new_best, total, positive)
    log_sum = best_all + jnp.log(total_all)
    grad_packed_sequence_slice = lax.all_gather(picture_summed, "dp", axis=0, tiled=True)
    similarity_grid = similarity(grad_packed_sequence_slice)
    column = jnp.arange(grad_packed_sequence_slice.shape[0], dtype=jnp.int32)
    hit = (target[:, None] == column[None, :]).astype(jnp.float32)
    logit_gradient = (
        loss_scale * live[:, None] * (jnp.exp(similarity_grid - log_sum[:, None]) - hit)
    ).astype(jnp.bfloat16)
    sentence_derivative = sharpness_divisor * jnp.dot(
        logit_gradient, grad_packed_sequence_slice, preferred_element_type=jnp.float32
    )
    cross = log_sum - positive
    loss_local = jnp.sum(live * cross)
    loss_total = lax.psum(loss_local, "dp")
    mean_loss = loss_total / slot_total
    (grad_flat,) = normalize_back(sentence_derivative)
    grad_pooled = grad_flat.reshape(packs, slots, width) / divisor
    grad_output = jnp.einsum(
        "pcl,pcd->pld", onehot, grad_pooled, precision=exact_arithmetic_mode
    ).reshape(rows, width)
    grad_output_low = grad_output.astype(jnp.bfloat16)
    down_grad = summation_axes_spec(grad_output_low, hidden, 0, 0)
    grad_hidden = jnp.dot(grad_output_low, down_full, preferred_element_type=jnp.float32)
    (grad_upper,) = gelu_back(grad_hidden)
    grad_upper = grad_upper.astype(jnp.bfloat16)
    inner_grad = jnp.sum(grad_upper.astype(jnp.float32), 0)
    up_grad = summation_axes_spec(normed_two, grad_upper, 0, 0)
    grad_two = lax.psum(
        summation_axes_spec(grad_upper, up_full, 1, 1).astype(jnp.bfloat16), "mp"
    ).astype(jnp.float32)
    _, norm_two_back = jax.vjp(layer_norm, resid, affine_wide[2], affine_wide[3])
    grad_resid_norm, gain_two_grad, shift_two_grad = norm_two_back(grad_two)
    grad_resid = grad_output + grad_resid_norm
    grad_resid_low = grad_resid.astype(jnp.bfloat16)
    out_grad = summation_axes_spec(grad_resid_low, mixed, 0, 0)
    grad_mixed = jnp.dot(grad_resid_low, out_full, preferred_element_type=jnp.float32)
    grad_mixed = grad_mixed.astype(jnp.bfloat16).reshape(shape4)
    probs_wide = jnp.exp(masked_scores() - log_total)
    probs_low = probs_wide.astype(jnp.bfloat16)
    grad_value = jnp.einsum(
        "phqk,pqhe->pkhe", probs_low, grad_mixed, preferred_element_type=jnp.float32
    )
    grad_probs = jnp.einsum(
        "pqhe,pkhe->phqk", grad_mixed, values, preferred_element_type=jnp.float32
    )
    grad_scores = probs_wide * (grad_probs - jnp.sum(probs_wide * grad_probs, -1, keepdims=True))
    grad_scores = grad_scores.astype(jnp.bfloat16)
    grad_query = (
        jnp.einsum("phqk,pkhe->pqhe", grad_scores, keys, preferred_element_type=jnp.float32)
        * root_scale
    )
    grad_key = (
        jnp.einsum("phqk,pqhe->pkhe", grad_scores, query, preferred_element_type=jnp.float32)
        * root_scale
    )
    grad_qkv = (
        jnp.stack([grad_query, grad_key, grad_value]).reshape(3, rows, half).astype(jnp.bfloat16)
    )
    head_grad = jnp.stack(
        [jnp.sum(grad_qkv[0].astype(jnp.float32), 0), jnp.sum(grad_qkv[2].astype(jnp.float32), 0)]
    )
    qkv_grad = jnp.einsum("td,kte->kde", normed_one, grad_qkv, preferred_element_type=jnp.float32)
    grad_one = lax.psum(
        jnp.einsum("kte,kde->td", grad_qkv, qkv_full, preferred_element_type=jnp.float32).astype(
            jnp.bfloat16
        ),
        "mp",
    ).astype(jnp.float32)
    _, norm_one_back = jax.vjp(layer_norm, inputs, affine_wide[0], affine_wide[1])
    grad_input_norm, gain_one_grad, shift_one_grad = norm_one_back(grad_one)
    grad_input = (grad_resid + grad_input_norm).reshape(packs, length, width)
    affine_grad = jnp.stack(
        [
            gain_one_grad,
            shift_one_grad,
            gain_two_grad,
            shift_two_grad,
            jnp.sum(grad_resid, 0),
            jnp.sum(grad_output, 0),
        ]
    )
    qkv_part, out_part, up_part, down_part, affine_part, head_part, inner_part = (
        lax.psum_scatter(qkv_grad, "dp", scatter_dimension=1, tiled=True),
        lax.psum_scatter(out_grad, "dp", scatter_dimension=0, tiled=True),
        lax.psum_scatter(up_grad, "dp", scatter_dimension=0, tiled=True),
        lax.psum_scatter(down_grad, "dp", scatter_dimension=0, tiled=True),
        lax.psum_scatter(affine_grad, "dp", scatter_dimension=1, tiled=True),
        lax.psum_scatter(head_grad, "dp", scatter_dimension=1, tiled=True),
        lax.psum_scatter(inner_grad, "dp", scatter_dimension=0, tiled=True),
    )
    weights = (qkv_weight, out_weight, up_weight, down_weight, affine, head_bias, inner_bias)
    firsts = (qkv_first, out_first, up_first, down_first, affine_first, head_first, inner_first)
    seconds = (
        qkv_second,
        out_second,
        up_second,
        down_second,
        affine_second,
        head_second,
        inner_second,
    )
    grads = (qkv_part, out_part, up_part, down_part, affine_part, head_part, inner_part)
    decays = (weight_decay, weight_decay, weight_decay, weight_decay, 0.0, 0.0, 0.0)
    parts = [
        moments(weights[index], firsts[index], seconds[index], grads[index], decays[index])
        for index in range(7)
    ]
    updates = [packed_sequence_slice[2] for packed_sequence_slice in parts]
    weight_squares = tensor_squares(*weights, float(model_size))
    update_squares = tensor_squares(*updates, float(model_size))
    weight_total, update_total = lax.psum((weight_squares, update_squares), ("dp", "mp"))
    weight_norm = jnp.sqrt(weight_total)
    update_norm = jnp.sqrt(update_total)
    weight_split = split_norms(weight_norm)
    update_split = split_norms(update_norm)
    news = [
        scaled_step(weights[index], updates[index], weight_split[index], update_split[index])
        for index in range(7)
    ]
    return (
        mean_loss,
        grad_input,
        news[0],
        parts[0][0],
        parts[0][1],
        news[1],
        parts[1][0],
        parts[1][1],
        news[2],
        parts[2][0],
        parts[2][1],
        news[3],
        parts[3][0],
        parts[3][1],
        news[4],
        parts[4][0],
        parts[4][1],
        news[5],
        parts[5][0],
        parts[5][1],
        news[6],
        parts[6][0],
        parts[6][1],
        jnp.stack([weight_norm, update_norm]),
    )


def solution(mesh):
    depth = mesh.shape["dp"] // 4
    fits = mesh.shape["mp"] == 2 and mesh.shape["dp"] % 8 == 0 and 768 // mesh.shape["dp"] % 16 == 0
    return jax.shard_map(
        functools.partial(body_near, depth) if fits else body,
        mesh=mesh,
        in_specs=(
            P("dp", None, None),
            P("dp", None),
            P("dp", None),
            P("dp", None),
            P(None, "dp", "mp"),
            P(None, "dp", "mp"),
            P(None, "dp", "mp"),
            P("dp", "mp"),
            P("dp", "mp"),
            P("dp", "mp"),
            P("dp", "mp"),
            P("dp", "mp"),
            P("dp", "mp"),
            P("dp", "mp"),
            P("dp", "mp"),
            P("dp", "mp"),
            P(None, "dp"),
            P(None, "dp"),
            P(None, "dp"),
            P(None, ("mp", "dp")),
            P(None, ("mp", "dp")),
            P(None, ("mp", "dp")),
            P(("mp", "dp")),
            P(("mp", "dp")),
            P(("mp", "dp")),
        ),
        out_specs=(
            P(),
            P("dp", None, None),
            P(None, "dp", "mp"),
            P(None, "dp", "mp"),
            P(None, "dp", "mp"),
            P("dp", "mp"),
            P("dp", "mp"),
            P("dp", "mp"),
            P("dp", "mp"),
            P("dp", "mp"),
            P("dp", "mp"),
            P("dp", "mp"),
            P("dp", "mp"),
            P("dp", "mp"),
            P(None, "dp"),
            P(None, "dp"),
            P(None, "dp"),
            P(None, ("mp", "dp")),
            P(None, ("mp", "dp")),
            P(None, ("mp", "dp")),
            P(("mp", "dp")),
            P(("mp", "dp")),
            P(("mp", "dp")),
            P(),
        ),
        check_vma=False,
    )
```

```python
import functools
import heapq

import jax
import jax.numpy as jnp
from jax import lax
from jax.experimental import pallas as pl
from jax.experimental.pallas import tpu as pltpu
from jax.sharding import PartitionSpec as P

HD = 64
STEP = 10


norm_epsilon = 1e-06
mask_value = -1000000000.0
sharpness_divisor = 50.0
loss_scale = 128.0
beta_first = 0.9
beta_second = 0.999
adam_epsilon = 1e-06
weight_decay = 0.01
learning_rate = 0.5
exact_arithmetic_mode = lax.Precision.HIGHEST


def layer_norm(values, gain, shift):
    center = values - jnp.mean(values, -1, keepdims=True)
    spread = jnp.mean(center * center, -1, keepdims=True)
    return center * lax.rsqrt(spread + norm_epsilon) * gain + shift


def normalize(values):
    return values * lax.rsqrt(jnp.sum(values * values, -1, keepdims=True) + norm_epsilon)


def summation_axes_spec(left, right, left_dim, right_dim):
    return lax.dot_general(
        left, right, (((left_dim,), (right_dim,)), ((), ())), preferred_element_type=jnp.float32
    )


def moments(weight, first, second, grad, decay):
    first_new = beta_first * first + (1.0 - beta_first) * grad
    second_new = beta_second * second + (1.0 - beta_second) * grad * grad
    first_hat = first_new / (1.0 - beta_first**STEP)
    second_hat = second_new / (1.0 - beta_second**STEP)
    update = first_hat / (jnp.sqrt(second_hat) + adam_epsilon) + decay * weight
    return (first_new, second_new, update)


def tensor_squares(qkv, out, upper, lower, affine, head, inner, replicas):
    return jnp.concatenate(
        [
            jnp.sum(qkv * qkv, (1, 2)),
            jnp.sum(out * out)[None],
            jnp.sum(upper * upper)[None],
            jnp.sum(lower * lower)[None],
            jnp.sum(affine * affine, 1) / replicas,
            jnp.sum(head * head, 1),
            jnp.sum(inner * inner)[None],
        ]
    )


def split_norms(norms):
    return (
        norms[0:3].reshape(3, 1, 1),
        norms[3],
        norms[4],
        norms[5],
        norms[6:12].reshape(6, 1),
        norms[12:14].reshape(2, 1),
        norms[14],
    )


def scaled_step(weight, update, weight_norm, update_norm):
    return weight - learning_rate * weight_norm / update_norm * update


MESH = pl.DeviceIdType.MESH
f32 = jnp.float32
bf16 = jnp.bfloat16
NROWS, SMALL, FAR = 32, 4.0, 8.0
PACE = (3.0, 2.2, 6.0, 6.0, 6.0)
WAYS = "xxxxxxxxxxxx"


class Place:
    def __init__(self, depth):
        self.depth = depth
        dp = lax.axis_index("dp")
        self.dp = dp
        self.x = lax.axis_index("mp")
        self.z, self.y, self.c = dp // 4, (dp // 2) % 2, dp % 2

    def at(self, z, y, c, x):
        return ((z * 2 + y) * 2 + c, x)

    def over_x(self):
        return self.at(self.z, self.y, self.c, 1 - self.x)

    def over_y(self):
        return self.at(self.z, 1 - self.y, self.c, self.x)

    def over_c(self):
        return self.at(self.z, self.y, 1 - self.c, self.x)

    def over_z(self, k):
        return self.at(lax.rem(self.z + k, self.depth), self.y, self.c, self.x)

    def in_plane(self, d):
        return self.at(self.z, 1 - self.y if d & 4 else self.y, 1 - self.c if d & 2 else self.c, 1 - self.x if d & 1 else self.x)

    def greet(self):
        sem = pltpu.get_barrier_semaphore()
        for peer in [self.in_plane(d) for d in range(1, 8)] + [self.over_z(k) for k in range(1, self.depth)]:
            pl.semaphore_signal(sem, inc=1, device_id=peer, device_id_type=MESH)

    def meet(self):
        pl.semaphore_wait(pltpu.get_barrier_semaphore(), 7 + self.depth - 1)


class Wire:
    def __init__(self, send, recv):
        self.send, self.recv, self.used, self.open = send, recv, 0, []

    def start(self, src, dst, device):
        i = self.used
        self.used += 1
        copy = pltpu.make_async_remote_copy(
            src_ref=src, dst_ref=dst, send_sem=self.send.at[i], recv_sem=self.recv.at[i], device_id=device, device_id_type=MESH
        )
        copy.start()
        self.open.append(copy)
        return copy

    def close(self):
        for copy in self.open:
            copy.wait_send()
        self.open = []


def arrive(copies):
    for copy in copies:
        copy.wait_recv()


class Timeline:
    def __init__(self):
        self.steps, self.count, self.now = [], 0, 0.0

    def add(self, time, step):
        heapq.heappush(self.steps, (time, self.count, step))
        self.count += 1

    def until(self, time):
        while self.steps and self.steps[0][0] <= time:
            at, _, step = heapq.heappop(self.steps)
            step(at)
        self.now = max(self.now, time)

    def tick(self, span):
        self.until(self.now + span)

    def drain(self):
        while self.steps:
            self.until(self.steps[0][0])


class Sheet:
    def __init__(self, full, u):
        self.full, self.u, self.half = full, u, full.shape[-1] // 2

    def part(self, z, y, c, x=None):
        lanes = pl.ds(0, 2 * self.half) if x is None else pl.ds(pl.multiple_of(x * self.half, 128), self.half)
        return self.full.at[self.u, z, y, c, :, lanes]


class Gather:
    def __init__(self, place, wire, line, items, pace):
        self.p, self.wire, self.line, self.items = place, wire, line, items
        self.flight, self.at = {}, []
        second, far_rate, to_one, rate, to_two, to_core, to_whole = pace
        one = -rate
        for i in range(len(items)):
            far = second + far_rate * (i - 1) if i else 0.0
            one = max(far + to_one, one + rate)
            two = one + to_two
            core = two + to_core
            self.at.append(core + to_whole)
            times = (far, one, two, core, core + to_whole)
            for time, step in zip(times, (self.far, self.one, self.two, self.core, self.whole)):
                line.add(time, lambda at, step=step, i=i: step(i))

    def far(self, i):
        p, it = self.p, self.items[i]
        mine = it.part(p.z, p.y, p.c, p.x)
        self.flight["z", i] = [self.wire.start(mine, mine, p.over_z(k)) for k in range(1, p.depth)]

    def one(self, i):
        p, it, h = self.p, self.items[i], self.p.depth // 2
        arrive(self.flight["z", i])
        a = it.part(pl.ds(0, h), p.y, p.c, p.x)
        b = it.part(pl.ds(h, p.depth - h), p.y, p.c, p.x)
        self.flight["1", i] = [self.wire.start(a, a, p.over_x()), self.wire.start(b, b, p.over_y())]

    def two(self, i):
        p, it, h = self.p, self.items[i], self.p.depth // 2
        arrive(self.flight["1", i])
        a = it.part(pl.ds(0, h), p.y, p.c)
        b = it.part(pl.ds(h, p.depth - h), slice(None), p.c, p.x)
        self.flight["2", i] = [self.wire.start(a, a, p.over_y()), self.wire.start(b, b, p.over_x())]

    def core(self, i):
        p, it = self.p, self.items[i]
        arrive(self.flight["2", i])
        r = it.part(slice(None), slice(None), p.c)
        self.flight["c", i] = [self.wire.start(r, r, p.over_c())]

    def whole(self, i):
        arrive(self.flight["c", i])

    def until(self, i):
        self.line.until(self.at[i])


def add_blocks(dst, src, count):
    for i in range(count):
        (d, at), (s, of) = dst(i), src(i)
        d[at] = d[at] + s[of]


class Reduce:
    def __init__(self, place, wire, line, order, ways, pace, free, part, from_core, one_a, one_b, two_a, two_b, from_z, total, use):
        self.p, self.wire, self.line, self.order, self.ways, self.free, self.use = place, wire, line, order, ways, free, use
        self.rate, self.to_one, self.to_two, self.to_far, self.to_last = pace
        self.next_one, self.count, self.takes = 0.0, 0, []
        self.part, self.from_core, self.one_a, self.one_b = part, from_core, one_a, one_b
        self.two_a, self.two_b, self.from_z, self.total = two_a, two_b, from_z, total
        self.h = place.depth // 2
        self.half = part.shape[-1] // 2
        self.slots = from_core.shape[0]
        self.flight = {}

    def lanes(self, x):
        return pl.ds(x * self.half if isinstance(x, int) else pl.multiple_of(x * self.half, 128), self.half)

    def core(self, i):
        p, u = self.p, self.order[i]
        if i >= self.slots:
            pl.semaphore_wait(self.free, 1)
        self.flight["c", i] = [self.wire.start(self.part.at[u, :, :, 1 - p.c], self.from_core.at[i % self.slots], p.over_c())]

    def take(self, i):
        p, u, Z, part = self.p, self.order[i], self.p.depth, self.part
        arrive(self.flight["c", i])
        add_blocks(
            lambda j: (part, (u, j // 2, j % 2, p.c)),
            lambda j: (self.from_core, (i % self.slots, j // 2, j % 2)), 2 * Z,
        )
        if i + self.slots < len(self.order):
            pl.semaphore_signal(self.free, inc=1, device_id=p.over_c(), device_id_type=MESH)

    def one(self, i):
        p, u, h, Z, part, way = self.p, self.order[i], self.h, self.p.depth, self.part, self.ways[i]
        start, flight = self.wire.start, []
        if way == "z":
            z1, z2, z3 = (lax.rem(p.z + k, Z) for k in (1, 2, 3))
            flight.append(start(part.at[u, z1, :, p.c], self.one_b.at[u], p.over_z(1)))
            for m in range(2):
                flight.append(start(part.at[u, z2, :, p.c, :, self.lanes(m)], self.one_a.at[u, :, m], p.over_z(2)))
                flight.append(start(part.at[u, z3, :, p.c, :, self.lanes(m)], (self.two_a, self.two_b)[m].at[u], p.over_z(3)))
        else:
            if way == "y":
                for m in range(2):
                    flight.append(start(part.at[u, pl.ds(0, h), 1 - p.y, p.c, :, self.lanes(m)], self.one_a.at[u, :, m], p.over_y()))
            else:
                flight.append(start(part.at[u, pl.ds(0, h), :, p.c, :, self.lanes(1 - p.x)], self.one_a.at[u], p.over_x()))
            flight.append(start(part.at[u, pl.ds(h, Z - h), 1 - p.y, p.c], self.one_b.at[u], p.over_y()))
        self.flight["1", i] = flight

    def two(self, i):
        p, u, h, Z, part, way = self.p, self.order[i], self.h, self.p.depth, self.part, self.ways[i]
        if way == "z":
            return
        arrive(self.flight["1", i])
        mine = self.lanes(p.x)
        if way == "y":
            for m in range(2):
                add_blocks(
                    lambda j: (part, (u, j, p.y, p.c, slice(None), self.lanes(m))), lambda j: (self.one_a, (u, j, m)), h
                )
            a, to_a = part.at[u, pl.ds(0, h), p.y, p.c, :, self.lanes(1 - p.x)], p.over_x()
        else:
            add_blocks(lambda j: (part, (u, j // 2, j % 2, p.c, slice(None), mine)), lambda j: (self.one_a, (u, j // 2, j % 2)), 2 * h)
            a, to_a = part.at[u, pl.ds(0, h), 1 - p.y, p.c, :, mine], p.over_y()
        add_blocks(lambda j: (part, (u, h + j, p.y, p.c)), lambda j: (self.one_b, (u, j)), Z - h)
        self.flight["2", i] = [
            self.wire.start(a, self.two_a.at[u], to_a),
            self.wire.start(part.at[u, pl.ds(h, Z - h), p.y, p.c, :, self.lanes(1 - p.x)], self.two_b.at[u], p.over_x()),
        ]

    def far(self, i):
        p, u, h, Z, part, way = self.p, self.order[i], self.h, self.p.depth, self.part, self.ways[i]
        mine = self.lanes(p.x)
        if way == "z":
            arrive(self.flight["1", i])
            for y in range(2):
                t = part[u, p.z, y, p.c].astype(f32) + self.one_b[u, y].astype(f32)
                left = t[:, : self.half] + self.one_a[u, y, 0].astype(f32) + self.two_a[u, y].astype(f32)
                right = t[:, self.half :] + self.one_a[u, y, 1].astype(f32) + self.two_b[u, y].astype(f32)
                part[u, p.z, y, p.c] = jnp.concatenate([left, right], 1).astype(part.dtype)
            others = ((p.y, 1 - p.x, 1), (1 - p.y, p.x, 4), (1 - p.y, 1 - p.x, 5))
            self.flight["z", i] = [
                self.wire.start(part.at[u, p.z, y, p.c, :, self.lanes(x)], self.from_z.at[k, u], p.in_plane(d))
                for k, (y, x, d) in enumerate(others)
            ]
            return
        arrive(self.flight["2", i])
        add_blocks(lambda j: (part, (u, j, p.y, p.c, slice(None), mine)), lambda j: (self.two_a, (u, j)), h)
        add_blocks(lambda j: (part, (u, h + j, p.y, p.c, slice(None), mine)), lambda j: (self.two_b, (u, j)), Z - h)
        self.flight["z", i] = [
            self.wire.start(part.at[u, lax.rem(p.z + k, Z), p.y, p.c, :, mine], self.from_z.at[k - 1, u], p.over_z(k))
            for k in range(1, Z)
        ]

    def last(self, i):
        p, u = self.p, self.order[i]
        arrive(self.flight["z", i])
        t = self.part[u, p.z, p.y, p.c, :, self.lanes(p.x)].astype(f32)
        for j in range(p.depth - 1):
            t = t + self.from_z[j, u].astype(f32)
        self.total[u] = t
        self.use(u, t)

    def step(self):
        i, line = self.count, self.line
        self.count += 1
        if i >= self.slots:
            line.until(self.takes[i - self.slots])
        self.core(i)
        time = line.now + self.to_one
        self.takes.append(time)
        line.add(time, lambda at: self.take(i))
        time = max(time, self.next_one)
        self.next_one = time + self.rate
        far = self.to_far + FAR if self.ways[i] == "z" else self.to_far
        for span, step in ((0.0, self.one), (self.to_two, self.two), (far, self.far), (self.to_last, self.last)):
            time += span
            line.add(time, lambda at, step=step: step(i))


class SumAll:
    def __init__(self, place, wire, own, room):
        self.p, self.wire, self.own, self.room = place, wire, own, room
        self.stage = 0

    def start(self):
        p = self.p
        if self.stage < 3:
            device = (p.over_c, p.over_x, p.over_y)[self.stage]()
            self.flight = [self.wire.start(self.own, self.room.at[self.stage], device)]
        else:
            self.flight = [self.wire.start(self.own, self.room.at[3 + p.z], p.over_z(k)) for k in range(1, p.depth)]

    def finish(self):
        p = self.p
        arrive(self.flight)
        for copy in self.flight:
            copy.wait_send()
        self.wire.open = [c for c in self.wire.open if all(c is not f for f in self.flight)]
        if self.stage < 3:
            self.own[...] = self.own[...] + self.room[self.stage]
        else:
            self.room[3 + p.z] = self.own[...]
            t = self.room[3]
            for z in range(1, p.depth):
                t = t + self.room[3 + z]
            self.own[...] = t
        self.stage += 1

    def run(self):
        while self.stage < 4:
            self.start()
            self.finish()


class SumSoon:
    def __init__(self, place, wire, own, plane, line):
        p = place
        slot = (p.y * 2 + p.c) * 2 + p.x
        plane[slot] = own[...]
        arrive([wire.start(own, plane.at[slot], p.in_plane(d)) for d in range(1, 8)])
        value = plane[0]
        for d in range(1, 8):
            value = value + plane[d]
        line[p.z] = value
        arrive([wire.start(line.at[p.z], line.at[p.z], p.over_z(k)) for k in range(1, p.depth)])
        value = line[0]
        for z in range(1, p.depth):
            value = value + line[z]
        self.value = value


class Pictures:
    def __init__(self, place, wire, line, full, size, pace):
        self.p, self.wire, self.full = place, wire, full
        mine = full.at[place.z, place.y, place.c]
        self.flight = [wire.start(mine, mine, place.over_y())]
        self.pieces = [(k, at, size) for at in range(0, full.shape[3], size) for k in range(1, place.depth)]
        self.sent = 0
        first, rate, to_core, to_whole = pace
        for i in range(len(self.pieces)):
            line.add(first + rate * i, lambda at: self.step())
        core = first + rate * len(self.pieces) + to_core
        self.at = core + to_whole
        line.add(core, lambda at: self.core())
        line.add(self.at, lambda at: self.whole())

    def step(self):
        p = self.p
        if self.sent == 0:
            arrive(self.flight)
            self.flight = []
        k, at, size = self.pieces[self.sent]
        mine = self.full.at[p.z, :, p.c, pl.ds(at, size)]
        self.flight.append(self.wire.start(mine, mine, p.over_z(k)))
        self.sent += 1

    def core(self):
        arrive(self.flight)
        r = self.full.at[:, :, self.p.c]
        self.flight = [self.wire.start(r, r, self.p.over_c())]

    def whole(self):
        arrive(self.flight)


def dot(a, b, left=1, right=0):
    return lax.dot_general(a, b, (((left,), (right,)), ((), ())), preferred_element_type=f32)


def row_loop(count, size, f, start=0):
    def step(i, carry):
        f(pl.ds(pl.multiple_of(start + i * size, size), size))
        return carry

    lax.fori_loop(0, count // size, step, 0)


def center_scale(x):
    center = x - jnp.mean(x, -1, keepdims=True)
    return center, lax.rsqrt(jnp.mean(center * center, -1, keepdims=True) + norm_epsilon)


def three(x):
    hi = x.astype(bf16)
    rest = x - hi.astype(f32)
    mid = rest.astype(bf16)
    return hi, mid, (rest - mid.astype(f32)).astype(bf16)


def fold(x):
    return jnp.sum(x.reshape(x.shape[0] // 8, 8, x.shape[1]), 0)


def placing(n, at, lanes):
    spot = lax.broadcasted_iota(jnp.int32, (n, lanes), 1) == lax.broadcasted_iota(jnp.int32, (n, lanes), 0) + at
    return jnp.where(spot, 1.0, 0.0).astype(bf16)


def picked(a, at, n):
    spot = placing(n, at, a.shape[1])
    return sum(dot(term, spot, 1, 1) for term in three(a))


def row_of(a, at):
    rows = lax.broadcasted_iota(jnp.int32, a.shape, 0) == at
    return jnp.sum(jnp.where(rows, a, jnp.zeros_like(a)), 0, keepdims=True)


def block_kernel(
    depth,
    tokens, segment, pairing, images, qkv_weight, out_weight, up_weight, down_weight, affine, head_bias, inner_bias,
    qkv_first, qkv_second, out_first, out_second, up_first, up_second, down_first, down_second,
    affine_first, affine_second, head_first, head_second, inner_first, inner_second,
    total, small_grad, norms, grad_low,
    full, pictures, part, from_core, one_a, one_b, two_a, two_b, from_z,
    tok, normed_one, qkv, mixed, resid, normed_two, hidden, slope, stream, grad_mixed, acc, low,
    probs, same, wide, sums, room, room2, folds, cap,
    old_qkv, old_out, old_up, old_down, squares, tile_sums, plane, line,
    send, recv, free, local, local_old,
):
    place = Place(depth)
    place.greet()
    x, dp = place.x, place.dp
    rows, width = tok.shape
    packs, length = 2, rows // 2
    half = qkv_weight.shape[2]
    units = full.shape[0]
    share = full.shape[4]
    blocks = up_weight.shape[1] // half
    up0, down0 = 4, 4 + blocks

    token_copies = [
        pltpu.make_async_copy(tokens.at[packs * x + p], tok.at[pl.ds(p * length, length)], local.at[p]) for p in range(packs)
    ]
    pairs_old = ((qkv_first, qkv_second, old_qkv), (out_first, out_second, old_out), (up_first, up_second, old_up), (down_first, down_second, old_down))
    old_copies = []
    for i, (one, two, kept) in enumerate(pairs_old):
        old_copies += [pltpu.make_async_copy(one, kept.at[0], local_old.at[2 * i]), pltpu.make_async_copy(two, kept.at[1], local_old.at[2 * i + 1])]
    for copy in token_copies + old_copies:
        copy.start()

    mine_lanes = pl.ds(pl.multiple_of(x * half, 128), half)

    def keep(u, value):
        full[u, place.z, place.y, place.c, :, mine_lanes] = value.astype(bf16)

    for k in range(3):
        keep(k, qkv_weight[k])
    keep(3, out_weight[...])
    for j in range(blocks):
        keep(up0 + j, up_weight[:, j * half : (j + 1) * half])
        keep(down0 + j, down_weight[:, j * half : (j + 1) * half])
    pictures[place.z, place.y, place.c] = normalize(images[...].astype(f32)).astype(bf16)

    place.meet()
    wire = Wire(send, recv)
    moves = Timeline()
    tick = moves.tick
    scenes = Pictures(place, wire, moves, pictures, 16, (14.2, 3.2, 3.0, 3.0))
    gather = Gather(place, wire, moves, [Sheet(full, u) for u in range(units)], (2.5, 3.5, 2.6, 3.8, 3.9, 8.0, 6.0))
    ready = gather.until
    tick(0.0)

    owner = x * (4 * depth) + dp
    n_affine, n_head, n_inner = affine.shape[1], head_bias.shape[1], inner_bias.shape[1]
    first = jnp.where(x == 0, 1.0, 0.0)
    inner_rows = 2 * blocks * half // width
    inner_at, inner_row = (owner * n_inner) % width, (owner * n_inner) // width
    wide[...] = jnp.zeros_like(wide)
    wide[0:6] = dot(affine[...].astype(bf16), placing(n_affine, dp * n_affine, width)) * first
    wide[6:8] = dot(head_bias[...].astype(bf16), placing(n_head, owner * n_head, width))
    inner_wide = dot(inner_bias[...].astype(bf16), placing(n_inner, inner_at, width))
    at_row = lax.broadcasted_iota(jnp.int32, (inner_rows, width), 0) == inner_row
    wide[8 : 8 + inner_rows] = jnp.where(at_row, jnp.broadcast_to(inner_wide, (inner_rows, width)), 0.0)
    spread = SumAll(place, wire, wide, room)
    spread.start()

    slots = pairing.shape[1]
    tile, window = 64, 128
    starts = [min(max(t * tile - (window - tile) // 2, 0), length - window) for t in range(length // tile)]
    onehots = []
    for p in range(packs):
        seg = jnp.broadcast_to(row_of(segment[...], packs * x + p), (slots, length))
        onehot = jnp.where(seg == lax.broadcasted_iota(jnp.int32, (slots, length), 0), 1.0, 0.0)
        onehots.append(onehot)
        low_hot = onehot.astype(bf16)
        both = acc.at[pl.ds(0, length), pl.ds(0, length)]
        both[...] = dot(low_hot, low_hot, 0, 0)
        for t, w in enumerate(starts):
            shared = dot(both[pl.ds(t * tile, tile)].astype(bf16), placing(window, w, length), 1, 1)
            same[p, t, 0:tile] = shared
            same[p, t, tile : 2 * tile] = shared
        tick(1.5)
        if p == 0:
            spread.finish()
            spread.start()
    while spread.stage < 4:
        tick(2.0)
        spread.finish()
        if spread.stage < 4:
            spread.start()

    for copy in token_copies:
        copy.wait()

    def norm_one(r):
        center, scale = center_scale(tok[r].astype(f32))
        normed_one[r] = (center * scale * wide[0:1] + wide[1:2]).astype(bf16)

    row_loop(rows, NROWS, norm_one)
    tick(3.0)

    def unit(u):
        return full[u].reshape(width, width)

    chunk = 256

    def unit_lanes(u, j):
        return full[u, :, :, :, :, pl.ds(j * chunk, chunk)].reshape(width, chunk)

    for k in range(3):
        ready(k)
        for j in range(width // chunk):
            lanes = pl.ds(j * chunk, chunk)
            value = dot(normed_one[...], unit_lanes(k, j))
            if k != 1:
                row = 6 if k == 0 else 7
                value = value + wide[row : row + 1, lanes]
            qkv[k, :, lanes] = value.astype(bf16)
        tick(1.0)

    root_scale = HD**-0.5
    pair = 2 * HD
    pairs = width // pair
    lower = lax.broadcasted_iota(jnp.int32, (tile, pair), 1) < HD

    def doubled(a):
        zero = jnp.zeros_like(a)
        return jnp.concatenate([jnp.where(lower, a, zero), jnp.where(lower, zero, a)], 0)

    def joined(a):
        return jnp.where(lower, a[:tile], a[tile:])

    def attend(p, g):
        lanes = pl.ds(pl.multiple_of(g * pair, pair), pair)
        span = pl.ds(p * length, length)
        query, keys, values = qkv[0, span, lanes], qkv[1, span, lanes], qkv[2, span, lanes]
        found, weights = [], []
        for t, w in enumerate(starts):
            scores = dot(doubled(query[t * tile : (t + 1) * tile]), keys[w : w + window], 1, 1) * root_scale
            scores = jnp.where(same[p, t] > 0.5, scores, mask_value)
            e = jnp.exp(scores - jnp.max(scores, -1, keepdims=True))
            prob = (e * (1.0 / jnp.sum(e, -1, keepdims=True))).astype(bf16)
            weights.append(prob)
            found.append(joined(dot(prob, values[w : w + window])).astype(bf16))
        for t in range(len(starts)):
            probs[p, g, t] = weights[t]
        mixed[span, lanes] = jnp.concatenate(found, 0)

    def each_pair(f, p, some):
        def step(g, carry):
            f(p, g)
            return carry

        lax.fori_loop(some[0], some[1], step, 0, unroll=some[1] - some[0])

    for p in range(packs):
        for some in ((0, pairs // 2), (pairs // 2, pairs)):
            each_pair(attend, p, some)
            tick(1.5)

    ready(3)
    acc[...] = dot(mixed[...], unit(3), 1, 1)
    tick(1.0)

    def norm_two(r):
        value = tok[r].astype(f32) + acc[r] + wide[4:5]
        resid[r] = value
        center, scale = center_scale(value)
        normed_two[r] = (center * scale * wide[2:3] + wide[3:4]).astype(bf16)
        stream[r] = value + wide[5:6]

    row_loop(rows, NROWS, norm_two)
    tick(3.0)

    def inner_lanes(j):
        at = j * half
        return ((8 + at // width, at % width), (8 + (blocks * half + at) // width, (blocks * half + at) % width))

    curve = (2.0 / jnp.pi) ** 0.5
    for j in range(blocks):
        ready(up0 + j)
        bias = jnp.concatenate([wide[row : row + 1, lane : lane + half] for row, lane in inner_lanes(j)], 1)
        for k in range(width // chunk):
            lanes = pl.ds(k * chunk, chunk)
            acc[:, lanes] = dot(normed_two[...], unit_lanes(up0 + j, k))

        def activate(r, j=j, bias=bias):
            u = acc[r] + bias
            square = u * u
            t = jnp.tanh(curve * (u + 0.044715 * (square * u)))
            hidden[j, r] = (0.5 * u * (1.0 + t)).astype(bf16)
            slope[j, r] = (0.5 * (1.0 + t) + 0.5 * u * (1.0 - t * t) * (curve * (1.0 + 3.0 * 0.044715 * square))).astype(bf16)

        row_loop(rows, 16, activate)
        tick(2.5)

    for j in range(blocks):
        ready(down0 + j)
        stream[...] += dot(hidden[j], unit(down0 + j), 1, 1)
    moves.drain()

    count_rows, target_rows = [], []
    for p in range(packs):
        count = jnp.sum(onehots[p], 1, keepdims=True)
        hot = onehots[p].astype(bf16)
        hi, mid, lo = three(stream[pl.ds(p * length, length)])
        pooled = dot(hot, hi) + dot(hot, mid) + dot(hot, lo)
        cap[pl.ds(p * slots, slots)] = pooled / jnp.maximum(count, 1.0)
        count_rows.append(count)
        names = jnp.broadcast_to(row_of(pairing[...], packs * x + p), (slots, slots)).astype(f32)
        diagonal = lax.broadcasted_iota(jnp.int32, (slots, slots), 0) == lax.broadcasted_iota(jnp.int32, (slots, slots), 1)
        target_rows.append(jnp.sum(jnp.where(diagonal, names, 0.0), 1, keepdims=True))
    counts = jnp.concatenate(count_rows, 0)
    target = jnp.concatenate(target_rows, 0)
    live = jnp.where(counts > 0.0, 1.0, 0.0)
    pooled = cap[...]
    radius = lax.rsqrt(jnp.sum(pooled * pooled, -1, keepdims=True) + norm_epsilon)
    caption = (pooled * radius).astype(bf16)
    all_images = pictures[...].reshape(-1, width)
    logits = sharpness_divisor * dot(caption, all_images, 1, 1)
    hit = lax.broadcasted_iota(jnp.int32, logits.shape, 1).astype(f32) == target
    best = jnp.max(logits, -1, keepdims=True)
    e = jnp.exp(logits - best)
    sum_e = jnp.sum(e, -1, keepdims=True)
    positive = jnp.sum(jnp.where(hit, logits, 0.0), -1, keepdims=True)
    cross = best + jnp.log(sum_e) - positive
    loss = jnp.sum(live * cross, 0, keepdims=True)
    grad_logits = (loss_scale * live * (e * (1.0 / sum_e) - jnp.where(hit, 1.0, 0.0))).astype(bf16)
    grad_caption = sharpness_divisor * dot(grad_logits, all_images)
    inner = jnp.sum(pooled * grad_caption, -1, keepdims=True)
    grad_pooled = radius * grad_caption - (radius * radius * radius) * inner * pooled
    grad_pooled = grad_pooled / jnp.maximum(counts, 1.0)
    folds[...] = jnp.zeros_like(folds)
    for p in range(packs):
        hot = onehots[p].astype(bf16)
        hi, mid, lo = three(grad_pooled[p * slots : (p + 1) * slots])
        stream[pl.ds(p * length, length)] = dot(hot, hi, 0, 0) + dot(hot, mid, 0, 0) + dot(hot, lo, 0, 0)

    def lower_stream(r):
        value = stream[r]
        low[r] = value.astype(bf16)
        folds[5] += fold(value)

    row_loop(rows, 32, lower_stream)

    squares[...] = jnp.zeros_like(squares)
    for copy in old_copies:
        copy.wait()

    def lanes_folded(a):
        a = fold(a)
        return sum(a[:, i * 128 : (i + 1) * 128] for i in range(a.shape[1] // 128))

    def use(u, grad):
        if u < 3:
            weight, one, two, row = qkv_weight[u], old_qkv[0, u], old_qkv[1, u], u
        elif u == 3:
            weight, one, two, row = out_weight[...], old_out[0], old_out[1], 3
        else:
            row = 4 if u < down0 else 5
            at = (u - up0) % blocks * half
            weights, kept = (up_weight, old_up) if row == 4 else (down_weight, old_down)
            weight, one, two = weights[:, at : at + half], kept[0, :, at : at + half], kept[1, :, at : at + half]
        update = moments(weight, one, two, grad, weight_decay)[2]
        squares[0, row] += lanes_folded(weight * weight)
        squares[1, row] += lanes_folded(update * update)

    order = [down0 + j for j in range(blocks)] + [up0 + j for j in range(blocks)] + [3, 0, 1, 2]
    reduce = Reduce(place, wire, moves, order, WAYS if depth == 4 and len(order) == len(WAYS) else "x" * len(order), PACE, free, part, from_core, one_a, one_b, two_a, two_b, from_z, total, use)

    def weight_grad(u, left, right):
        for j in range(width // chunk):
            lanes = pl.ds(j * chunk, chunk)
            value = dot(left, right(lanes), 0, 0).astype(bf16)
            part[u, :, :, :, :, lanes] = value.reshape(depth, 2, 2, share, chunk)
        tick(0.7)
        reduce.step()

    sums[...] = jnp.zeros_like(sums)
    for j in range(blocks):
        weight_grad(down0 + j, low[...], lambda lanes, j=j: hidden[j, :, lanes])
        for k in range(width // chunk):
            lanes = pl.ds(k * chunk, chunk)
            acc[:, lanes] = dot(low[...], unit_lanes(down0 + j, k))

        def upper_back(r, j=j):
            value = (acc[r] * slope[j, r].astype(f32)).astype(bf16)
            hidden[j, r] = value
            folds[6] += fold(value.astype(f32))

        folds[6] = jnp.zeros_like(folds[6])
        row_loop(rows, 32, upper_back)
        tick(1.2)
        inner_sum = jnp.sum(folds[6], 0, keepdims=True)
        for i, (row, lane) in enumerate(inner_lanes(j)):
            sums[row : row + 1, lane : lane + half] = inner_sum[:, i * half : (i + 1) * half]

    for j in range(blocks):
        weight_grad(up0 + j, normed_two[...], lambda lanes, j=j: hidden[j, :, lanes])
        value = dot(hidden[j], unit(up0 + j), 1, 1)
        if j == 0:
            acc[...] = value
        else:
            acc[...] += value
        tick(0.7)

    def norm_two_back(r):
        center, scale = center_scale(resid[r])
        hat = center * scale
        grad = acc[r]
        weighted = grad * wide[2:3]
        value = stream[r] + scale * (
            weighted - jnp.mean(weighted, -1, keepdims=True) - hat * jnp.mean(weighted * hat, -1, keepdims=True)
        )
        stream[r] = value
        low[r] = value.astype(bf16)
        folds[2] += fold(grad * hat)
        folds[3] += fold(grad)
        folds[4] += fold(value)

    row_loop(rows, NROWS, norm_two_back)
    tick(4.0)
    weight_grad(3, low[...], lambda lanes: mixed[:, lanes])
    for k in range(width // chunk):
        lanes = pl.ds(k * chunk, chunk)
        grad_mixed[:, lanes] = dot(low[...], unit_lanes(3, k)).astype(bf16)
    tick(0.7)

    def overlaid(pieces):
        step = 32
        found = []
        for at in range(0, length, step):
            found.append(sum(piece[at - w : at - w + step] for w, piece in zip(starts, pieces) if w <= at < w + window))
        return jnp.concatenate(found, 0)

    def attend_back(p, g):
        lanes = pl.ds(pl.multiple_of(g * pair, pair), pair)
        span = pl.ds(p * length, length)
        query, keys, values, grads = qkv[0, span, lanes], qkv[1, span, lanes], qkv[2, span, lanes], grad_mixed[span, lanes]
        of_query, of_keys, of_values = [], [], []
        for t, w in enumerate(starts):
            some = doubled(query[t * tile : (t + 1) * tile])
            grad = doubled(grads[t * tile : (t + 1) * tile])
            prob = probs[p, g, t]
            prob_wide = prob.astype(f32)
            grad_prob = dot(grad, values[w : w + window], 1, 1)
            grad_score = prob_wide * (grad_prob - jnp.sum(prob_wide * grad_prob, -1, keepdims=True))
            grad_score = grad_score.astype(bf16)
            of_keys.append(dot(grad_score, some, 0, 0))
            of_values.append(dot(prob, grad, 0, 0))
            of_query.append((joined(dot(grad_score, keys[w : w + window])) * root_scale).astype(bf16))
        qkv[0, span, lanes] = jnp.concatenate(of_query, 0)
        qkv[1, span, lanes] = (overlaid(of_keys) * root_scale).astype(bf16)
        qkv[2, span, lanes] = overlaid(of_values).astype(bf16)

    for p in range(packs):
        for some in ((0, pairs // 2), (pairs // 2, pairs)):
            each_pair(attend_back, p, some)
            tick(3.2)

    for k in range(3):
        value = dot(qkv[k], unit(k), 1, 1)
        if k == 0:
            acc[...] = value
        else:
            acc[...] += value
    tick(2.0)

    def norm_one_back(r):
        center, scale = center_scale(tok[r].astype(f32))
        hat = center * scale
        grad = acc[r]
        weighted = grad * wide[0:1]
        value = stream[r] + scale * (
            weighted - jnp.mean(weighted, -1, keepdims=True) - hat * jnp.mean(weighted * hat, -1, keepdims=True)
        )
        low[r] = value.astype(bf16)
        folds[0] += fold(grad * hat)
        folds[1] += fold(grad)

    swaps, outs = [], []
    for p in range(packs):
        row_loop(length, NROWS, norm_one_back, p * length)
        mine, there = low.at[pl.ds(p * length, length)], grad_low.at[packs * x + p]
        swaps.append(wire.start(mine, there, place.over_x()))
        outs.append(pltpu.make_async_copy(mine, there, local.at[p]))
        outs[-1].start()
        tick(2.3)

    for k in range(3):
        weight_grad(k, normed_one[...], lambda lanes, k=k: qkv[k, :, lanes])
        tick(0.3)

    def head_sums(r):
        folds[7] += fold(qkv[0, r].astype(f32))
        folds[8] += fold(qkv[2, r].astype(f32))

    row_loop(rows, 32, head_sums)
    for k, row in ((0, 0), (1, 1), (2, 2), (3, 3), (4, 4), (5, 5), (7, 6), (8, 7)):
        sums[row : row + 1] = jnp.sum(folds[k], 0, keepdims=True)
    last_row = 8 + inner_rows
    sums[last_row : last_row + 1] = jnp.broadcast_to(loss, (1, width))
    small_sum = SumAll(place, wire, sums, room2)
    small_sum.start()

    def small_step(at):
        small_sum.finish()
        if small_sum.stage < 4:
            small_sum.start()

    def small_parts(at):
        small_grad[...] = jnp.zeros_like(small_grad)
        tile_sums[...] = jnp.zeros_like(tile_sums)
        of_affine = picked(sums[0:6], dp * n_affine, n_affine)
        of_head = picked(sums[6:8], owner * n_head, n_head)
        of_inner = picked(row_of(sums[8 : 8 + inner_rows], inner_row), inner_at, n_inner)
        small_grad[0:6, 0:n_affine] = of_affine
        small_grad[6:8, 0:n_head] = of_head
        small_grad[8:9, 0:n_inner] = of_inner
        small_grad[9:10] = sums[last_row : last_row + 1, 0:128]
        smalls = (
            (6, 6, n_affine, affine[...], affine_first[...], affine_second[...], of_affine, first),
            (12, 2, n_head, head_bias[...], head_first[...], head_second[...], of_head, 1.0),
            (14, 1, n_inner, inner_bias[...], inner_first[...], inner_second[...], of_inner, 1.0),
        )
        for row, n, lanes, weight, one, two, grad, share_of in smalls:
            update = moments(weight, one, two, grad, 0.0)[2]
            tile_sums[row : row + n, 0:lanes] = weight * weight * share_of
            tile_sums[16 + row : 16 + row + n, 0:lanes] = update * update * share_of


    for k in range(4):
        moves.add(moves.now + SMALL * (k + 1), small_step)
    moves.add(moves.now + SMALL * 4 + 1.0, small_parts)
    moves.drain()
    for k in range(2):
        for row in range(6):
            tile_sums[16 * k + row : 16 * k + row + 1] = jnp.sum(squares[k, row], 0, keepdims=True)
    every = SumSoon(place, wire, tile_sums, plane, line).value
    norms[...] = jnp.broadcast_to(jnp.sqrt(jnp.sum(every, -1, keepdims=True)), norms.shape)
    arrive(swaps)
    for copy in outs:
        copy.wait()
    wire.close()


def block_step(depth, *arrays):
    tokens, segment, pairing, images, qkv_weight, out_weight, up_weight, down_weight = arrays[:8]
    packs, length, width = tokens.shape
    rows = packs // 2 * length
    share, half = qkv_weight.shape[1:]
    blocks = up_weight.shape[1] // half
    units = 4 + 2 * blocks
    slots = pairing.shape[1]
    h = depth // 2
    few = images.shape[0]
    ring = 4
    small = (16, width)
    low = lambda *shape: pltpu.VMEM(shape, bf16)
    wide = lambda *shape: pltpu.VMEM(shape, f32)
    count = units * (depth - 1 + 5) + (depth - 1) * (few // 16) + 2 + units * (8 + depth - 1) + 2 * (3 + depth - 1) + 2 + 7 + depth - 1
    vmem = pl.BlockSpec(memory_space=pltpu.VMEM)
    hbm = pl.BlockSpec(memory_space=pl.ANY)
    return pl.pallas_call(
        functools.partial(block_kernel, depth),
        out_shape=(
            jax.ShapeDtypeStruct((units, share, half), f32),
            jax.ShapeDtypeStruct((16, 128), f32),
            jax.ShapeDtypeStruct((32, 128), f32),
            jax.ShapeDtypeStruct(tokens.shape, bf16),
        ),
        in_specs=[hbm] + [vmem] * 10 + [hbm] * 8 + [vmem] * 6,
        out_specs=[vmem, vmem, vmem, hbm],
        scratch_shapes=[
            low(units, depth, 2, 2, share, width), low(depth, 2, 2, few, width),
            low(units, depth, 2, 2, share, width), low(ring, depth, 2, share, width), low(units, h, 2, share, half),
            low(units, depth - h, share, width), low(units, h, share, half), low(units, depth - h, share, half),
            low(depth - 1, units, share, half),
            low(rows, width), low(rows, width), low(3, rows, width), low(rows, width), wide(rows, width), low(rows, width),
            low(blocks, rows, width), low(blocks, rows, width), wide(rows, width), low(rows, width), wide(rows, width), low(rows, width),
            low(2, width // (2 * HD), length // 64, 128, 128), wide(2, length // 64, 128, 128), wide(*small), wide(*small),
            wide(3 + depth, *small), wide(3 + depth, *small), wide(9, 8, width), wide(2 * slots, width),
            wide(2, *qkv_weight.shape), wide(2, *out_weight.shape), wide(2, *up_weight.shape), wide(2, *down_weight.shape),
            wide(2, 6, 8, 128), wide(32, 128), wide(8, 32, 128), wide(depth, 32, 128),
            pltpu.SemaphoreType.DMA((count,)), pltpu.SemaphoreType.DMA((count,)), pltpu.SemaphoreType.REGULAR,
            pltpu.SemaphoreType.DMA((2,)), pltpu.SemaphoreType.DMA((8,)),
        ],
        compiler_params=pltpu.CompilerParams(collective_id=1, has_side_effects=True, vmem_limit_bytes=64 << 20),
        name="train_block",
    )(*arrays)


def finish_kernel(slot_total, total, small_grad, norms, grad_low, *refs):
    weights, firsts, seconds = refs[0:7], refs[7:14], refs[14:21]
    grad_input = refs[21]
    nexts, first_nexts, second_nexts = refs[22:29], refs[29:36], refs[36:43]
    mean_loss, tensor_norms, room, wide_room, sems = refs[43:48]
    packs = grad_low.shape[0]
    reads = [pltpu.make_async_copy(grad_low.at[p], room.at[p], sems.at[p]) for p in range(packs)]
    writes = [pltpu.make_async_copy(wide_room.at[p], grad_input.at[p], sems.at[packs + p]) for p in range(packs)]
    for copy in reads:
        copy.start()

    def update(i, at, grad, row, decay):
        weight, one, two = weights[i][at], firsts[i][at], seconds[i][at]
        first_new, second_new, change = moments(weight, one, two, grad, decay)
        first_nexts[i][at] = first_new
        second_nexts[i][at] = second_new
        count = 1 if isinstance(row, int) else row[1]
        row = row if isinstance(row, int) else row[0]
        weight_norm, update_norm = norms[row : row + count, 0:1], norms[16 + row : 16 + row + count, 0:1]
        nexts[i][at] = weight - learning_rate * weight_norm / update_norm * change

    every = slice(None)
    half = total.shape[2]
    blocks = weights[2].shape[1] // half
    for p in range(packs):
        reads[p].wait()

        def widen(r, p=p):
            wide_room[p, r] = room[p, r].astype(f32)

        row_loop(room.shape[1], 32, widen)
        writes[p].start()
    for k in range(3):
        update(0, (k,), total[k], k, weight_decay)
    update(1, (every,), total[3], 3, weight_decay)
    for i in range(2):
        for j in range(blocks):
            update(2 + i, (every, slice(j * half, (j + 1) * half)), total[4 + i * blocks + j], 4 + i, weight_decay)
    update(4, (every,), small_grad[0:6, 0 : weights[4].shape[1]], (6, 6), 0.0)
    update(5, (every,), small_grad[6:8, 0 : weights[5].shape[1]], (12, 2), 0.0)
    update(6, (every,), small_grad[8:9, 0 : weights[6].shape[1]], 14, 0.0)
    mean_loss[...] = small_grad[9:10, 0:1] / slot_total
    square = norms.shape[0] // 2
    diagonal = lax.broadcasted_iota(jnp.int32, (square, square), 0) == lax.broadcasted_iota(jnp.int32, (square, square), 1)
    for k in range(2):
        column = jnp.broadcast_to(norms[square * k : square * (k + 1), 0:1], (square, square))
        tensor_norms[k : k + 1] = jnp.sum(jnp.where(diagonal, column, 0.0), 0, keepdims=True)[:, 0:15]
    for copy in writes:
        copy.wait()


def finish_step(slot_total, total, small_grad, norms, grad_low, weights, firsts, seconds):
    vmem = pl.BlockSpec(memory_space=pltpu.VMEM)
    hbm = pl.BlockSpec(memory_space=pl.ANY)
    packs, length, width = grad_low.shape
    like = [jax.ShapeDtypeStruct(a.shape, f32) for a in weights]
    return pl.pallas_call(
        functools.partial(finish_kernel, slot_total),
        out_shape=(
            jax.ShapeDtypeStruct(grad_low.shape, f32), *like, *like, *like,
            jax.ShapeDtypeStruct((1, 1), f32), jax.ShapeDtypeStruct((2, 15), f32),
        ),
        in_specs=[vmem] * 3 + [hbm] + [vmem] * 21,
        out_specs=[hbm] + [vmem] * 23,
        scratch_shapes=[
            pltpu.VMEM((packs, length, width), bf16), pltpu.VMEM((packs, length, width), f32),
            pltpu.SemaphoreType.DMA((2 * packs,)),
        ],
        compiler_params=pltpu.CompilerParams(vmem_limit_bytes=64 << 20),
        name="optimizer",
    )(total, small_grad, norms, grad_low, *weights, *firsts, *seconds)


def body_near(depth, *arrays):
    (
        tokens, segment, pairing, images,
        qkv_weight, qkv_first, qkv_second, out_weight, out_first, out_second,
        up_weight, up_first, up_second, down_weight, down_first, down_second,
        affine, affine_first, affine_second, head_bias, head_first, head_second,
        inner_bias, inner_first, inner_second,
    ) = arrays
    inner_bias, inner_first, inner_second = (a.reshape(1, -1) for a in (inner_bias, inner_first, inner_second))
    total, small_grad, norms, grad_low = block_step(
        depth, tokens, segment, pairing, images, qkv_weight, out_weight, up_weight, down_weight, affine, head_bias, inner_bias,
        qkv_first, qkv_second, out_first, out_second, up_first, up_second, down_first, down_second,
        affine_first, affine_second, head_first, head_second, inner_first, inner_second,
    )
    weights = (qkv_weight, out_weight, up_weight, down_weight, affine, head_bias, inner_bias)
    firsts = (qkv_first, out_first, up_first, down_first, affine_first, head_first, inner_first)
    seconds = (qkv_second, out_second, up_second, down_second, affine_second, head_second, inner_second)
    slot_total = float(pairing.size * 4 * depth)
    grad_input, *news, mean_loss, tensor_norms = finish_step(slot_total, total, small_grad, norms, grad_low, weights, firsts, seconds)
    results = [mean_loss.reshape(()), grad_input]
    for i in range(7):
        triple = (news[i], news[7 + i], news[14 + i])
        results += [a.reshape(-1) for a in triple] if i == 6 else triple
    return (*results, tensor_norms)


def body(
    tokens,
    segment,
    pairing,
    images,
    qkv_weight,
    qkv_first,
    qkv_second,
    out_weight,
    out_first,
    out_second,
    up_weight,
    up_first,
    up_second,
    down_weight,
    down_first,
    down_second,
    affine,
    affine_first,
    affine_second,
    head_bias,
    head_first,
    head_second,
    inner_bias,
    inner_first,
    inner_second,
):
    model_size = lax.axis_size("mp")
    packs, length, width = tokens.shape
    rows = packs * length
    qkv_full, out_full, up_full, down_full, affine_full, head_full, inner_full = (
        lax.all_gather(qkv_weight.astype(jnp.bfloat16), "dp", axis=1, tiled=True),
        lax.all_gather(out_weight.astype(jnp.bfloat16), "dp", axis=0, tiled=True),
        lax.all_gather(up_weight.astype(jnp.bfloat16), "dp", axis=0, tiled=True),
        lax.all_gather(down_weight.astype(jnp.bfloat16), "dp", axis=0, tiled=True),
        lax.all_gather(affine.astype(jnp.bfloat16), "dp", axis=1, tiled=True),
        lax.all_gather(head_bias.astype(jnp.bfloat16), "dp", axis=1, tiled=True),
        lax.all_gather(inner_bias.astype(jnp.bfloat16), "dp", axis=0, tiled=True),
    )
    affine_wide = affine_full.astype(jnp.float32)
    head_wide = head_full.astype(jnp.float32)
    inner_wide = inner_full.astype(jnp.float32)
    half = qkv_full.shape[2]
    local_heads = half // HD
    shape4 = (packs, length, local_heads, HD)
    root_scale = HD ** (-0.5)
    inputs = tokens.reshape(rows, width).astype(jnp.float32)
    normed_one = layer_norm(inputs, affine_wide[0], affine_wide[1]).astype(jnp.bfloat16)
    projected = jnp.einsum("td,kde->kte", normed_one, qkv_full, preferred_element_type=jnp.float32)
    query = (projected[0] + head_wide[0]).astype(jnp.bfloat16).reshape(shape4)
    keys = projected[1].astype(jnp.bfloat16).reshape(shape4)
    values = (projected[2] + head_wide[1]).astype(jnp.bfloat16).reshape(shape4)
    same = segment[:, None, :, None] == segment[:, None, None, :]

    def masked_scores():
        raw = (
            jnp.einsum("pqhe,pkhe->phqk", query, keys, preferred_element_type=jnp.float32)
            * root_scale
        )
        return jnp.where(same, raw, mask_value)

    scores = masked_scores()
    top = jnp.max(scores, -1, keepdims=True)
    log_total = top + jnp.log(jnp.sum(jnp.exp(scores - top), -1, keepdims=True))
    probs = jnp.exp(scores - log_total).astype(jnp.bfloat16)
    mixed = jnp.einsum("phqk,pkhe->pqhe", probs, values, preferred_element_type=jnp.float32)
    mixed = mixed.reshape(rows, half).astype(jnp.bfloat16)
    attended = lax.psum(summation_axes_spec(mixed, out_full, 1, 1), "mp")
    resid = inputs + attended + affine_wide[4]
    normed_two = layer_norm(resid, affine_wide[2], affine_wide[3]).astype(jnp.bfloat16)
    upper = jnp.dot(normed_two, up_full, preferred_element_type=jnp.float32) + inner_wide
    activated, gelu_back = jax.vjp(jax.nn.gelu, upper)
    hidden = activated.astype(jnp.bfloat16)
    lowered = lax.psum(
        summation_axes_spec(hidden, down_full, 1, 1).astype(jnp.bfloat16), "mp"
    ).astype(jnp.float32)
    output = resid + lowered + affine_wide[5]
    slots = pairing.shape[1]
    onehot = (segment[:, None, :] == jnp.arange(slots, dtype=jnp.int32)[None, :, None]).astype(
        jnp.float32
    )
    counts = jnp.sum(onehot, -1)
    divisor = jnp.maximum(counts, 1.0)[..., None]
    pooled = (
        jnp.einsum(
            "pcl,pld->pcd",
            onehot,
            output.reshape(packs, length, width),
            precision=exact_arithmetic_mode,
        )
        / divisor
    )
    flat = pooled.reshape(packs * slots, width)
    caption_wide, normalize_back = jax.vjp(normalize, flat)
    sentence_words = caption_wide.astype(jnp.bfloat16)
    live = (counts > 0).reshape(-1).astype(jnp.float32)
    target = pairing.reshape(-1)
    captions_count = flat.shape[0]
    slot_total = float(captions_count * lax.axis_size("dp"))
    picture_summed = normalize(images.astype(jnp.float32)).astype(jnp.bfloat16)

    def similarity(packed_sequence_slice):
        return sharpness_divisor * summation_axes_spec(sentence_words, packed_sequence_slice, 1, 1)

    score_packed_sequence_slice = lax.all_gather(picture_summed, "dp", axis=0, tiled=True)
    best = jnp.full((captions_count,), mask_value, jnp.float32)
    similarity_grid = similarity(score_packed_sequence_slice)
    new_best = jnp.maximum(best, jnp.max(similarity_grid, 1))
    total = jnp.sum(jnp.exp(similarity_grid - new_best[:, None]), 1)
    column = jnp.arange(score_packed_sequence_slice.shape[0], dtype=jnp.int32)
    hit = target[:, None] == column[None, :]
    positive = jnp.sum(jnp.where(hit, similarity_grid, 0.0), 1)
    best_all, total_all, positive = (new_best, total, positive)
    log_sum = best_all + jnp.log(total_all)
    grad_packed_sequence_slice = lax.all_gather(picture_summed, "dp", axis=0, tiled=True)
    similarity_grid = similarity(grad_packed_sequence_slice)
    column = jnp.arange(grad_packed_sequence_slice.shape[0], dtype=jnp.int32)
    hit = (target[:, None] == column[None, :]).astype(jnp.float32)
    logit_gradient = (
        loss_scale * live[:, None] * (jnp.exp(similarity_grid - log_sum[:, None]) - hit)
    ).astype(jnp.bfloat16)
    sentence_derivative = sharpness_divisor * jnp.dot(
        logit_gradient, grad_packed_sequence_slice, preferred_element_type=jnp.float32
    )
    cross = log_sum - positive
    loss_local = jnp.sum(live * cross)
    loss_total = lax.psum(loss_local, "dp")
    mean_loss = loss_total / slot_total
    (grad_flat,) = normalize_back(sentence_derivative)
    grad_pooled = grad_flat.reshape(packs, slots, width) / divisor
    grad_output = jnp.einsum(
        "pcl,pcd->pld", onehot, grad_pooled, precision=exact_arithmetic_mode
    ).reshape(rows, width)
    grad_output_low = grad_output.astype(jnp.bfloat16)
    down_grad = summation_axes_spec(grad_output_low, hidden, 0, 0)
    grad_hidden = jnp.dot(grad_output_low, down_full, preferred_element_type=jnp.float32)
    (grad_upper,) = gelu_back(grad_hidden)
    grad_upper = grad_upper.astype(jnp.bfloat16)
    inner_grad = jnp.sum(grad_upper.astype(jnp.float32), 0)
    up_grad = summation_axes_spec(normed_two, grad_upper, 0, 0)
    grad_two = lax.psum(
        summation_axes_spec(grad_upper, up_full, 1, 1).astype(jnp.bfloat16), "mp"
    ).astype(jnp.float32)
    _, norm_two_back = jax.vjp(layer_norm, resid, affine_wide[2], affine_wide[3])
    grad_resid_norm, gain_two_grad, shift_two_grad = norm_two_back(grad_two)
    grad_resid = grad_output + grad_resid_norm
    grad_resid_low = grad_resid.astype(jnp.bfloat16)
    out_grad = summation_axes_spec(grad_resid_low, mixed, 0, 0)
    grad_mixed = jnp.dot(grad_resid_low, out_full, preferred_element_type=jnp.float32)
    grad_mixed = grad_mixed.astype(jnp.bfloat16).reshape(shape4)
    probs_wide = jnp.exp(masked_scores() - log_total)
    probs_low = probs_wide.astype(jnp.bfloat16)
    grad_value = jnp.einsum(
        "phqk,pqhe->pkhe", probs_low, grad_mixed, preferred_element_type=jnp.float32
    )
    grad_probs = jnp.einsum(
        "pqhe,pkhe->phqk", grad_mixed, values, preferred_element_type=jnp.float32
    )
    grad_scores = probs_wide * (grad_probs - jnp.sum(probs_wide * grad_probs, -1, keepdims=True))
    grad_scores = grad_scores.astype(jnp.bfloat16)
    grad_query = (
        jnp.einsum("phqk,pkhe->pqhe", grad_scores, keys, preferred_element_type=jnp.float32)
        * root_scale
    )
    grad_key = (
        jnp.einsum("phqk,pqhe->pkhe", grad_scores, query, preferred_element_type=jnp.float32)
        * root_scale
    )
    grad_qkv = (
        jnp.stack([grad_query, grad_key, grad_value]).reshape(3, rows, half).astype(jnp.bfloat16)
    )
    head_grad = jnp.stack(
        [jnp.sum(grad_qkv[0].astype(jnp.float32), 0), jnp.sum(grad_qkv[2].astype(jnp.float32), 0)]
    )
    qkv_grad = jnp.einsum("td,kte->kde", normed_one, grad_qkv, preferred_element_type=jnp.float32)
    grad_one = lax.psum(
        jnp.einsum("kte,kde->td", grad_qkv, qkv_full, preferred_element_type=jnp.float32).astype(
            jnp.bfloat16
        ),
        "mp",
    ).astype(jnp.float32)
    _, norm_one_back = jax.vjp(layer_norm, inputs, affine_wide[0], affine_wide[1])
    grad_input_norm, gain_one_grad, shift_one_grad = norm_one_back(grad_one)
    grad_input = (grad_resid + grad_input_norm).reshape(packs, length, width)
    affine_grad = jnp.stack(
        [
            gain_one_grad,
            shift_one_grad,
            gain_two_grad,
            shift_two_grad,
            jnp.sum(grad_resid, 0),
            jnp.sum(grad_output, 0),
        ]
    )
    qkv_part, out_part, up_part, down_part, affine_part, head_part, inner_part = (
        lax.psum_scatter(qkv_grad, "dp", scatter_dimension=1, tiled=True),
        lax.psum_scatter(out_grad, "dp", scatter_dimension=0, tiled=True),
        lax.psum_scatter(up_grad, "dp", scatter_dimension=0, tiled=True),
        lax.psum_scatter(down_grad, "dp", scatter_dimension=0, tiled=True),
        lax.psum_scatter(affine_grad, "dp", scatter_dimension=1, tiled=True),
        lax.psum_scatter(head_grad, "dp", scatter_dimension=1, tiled=True),
        lax.psum_scatter(inner_grad, "dp", scatter_dimension=0, tiled=True),
    )
    weights = (qkv_weight, out_weight, up_weight, down_weight, affine, head_bias, inner_bias)
    firsts = (qkv_first, out_first, up_first, down_first, affine_first, head_first, inner_first)
    seconds = (
        qkv_second,
        out_second,
        up_second,
        down_second,
        affine_second,
        head_second,
        inner_second,
    )
    grads = (qkv_part, out_part, up_part, down_part, affine_part, head_part, inner_part)
    decays = (weight_decay, weight_decay, weight_decay, weight_decay, 0.0, 0.0, 0.0)
    parts = [
        moments(weights[index], firsts[index], seconds[index], grads[index], decays[index])
        for index in range(7)
    ]
    updates = [packed_sequence_slice[2] for packed_sequence_slice in parts]
    weight_squares = tensor_squares(*weights, float(model_size))
    update_squares = tensor_squares(*updates, float(model_size))
    weight_total, update_total = lax.psum((weight_squares, update_squares), ("dp", "mp"))
    weight_norm = jnp.sqrt(weight_total)
    update_norm = jnp.sqrt(update_total)
    weight_split = split_norms(weight_norm)
    update_split = split_norms(update_norm)
    news = [
        scaled_step(weights[index], updates[index], weight_split[index], update_split[index])
        for index in range(7)
    ]
    return (
        mean_loss,
        grad_input,
        news[0],
        parts[0][0],
        parts[0][1],
        news[1],
        parts[1][0],
        parts[1][1],
        news[2],
        parts[2][0],
        parts[2][1],
        news[3],
        parts[3][0],
        parts[3][1],
        news[4],
        parts[4][0],
        parts[4][1],
        news[5],
        parts[5][0],
        parts[5][1],
        news[6],
        parts[6][0],
        parts[6][1],
        jnp.stack([weight_norm, update_norm]),
    )


def solution(mesh):
    depth = mesh.shape["dp"] // 4
    fits = mesh.shape["mp"] == 2 and mesh.shape["dp"] % 8 == 0 and 768 // mesh.shape["dp"] % 16 == 0
    return jax.shard_map(
        functools.partial(body_near, depth) if fits else body,
        mesh=mesh,
        in_specs=(
            P("dp", None, None),
            P("dp", None),
            P("dp", None),
            P("dp", None),
            P(None, "dp", "mp"),
            P(None, "dp", "mp"),
            P(None, "dp", "mp"),
            P("dp", "mp"),
            P("dp", "mp"),
            P("dp", "mp"),
            P("dp", "mp"),
            P("dp", "mp"),
            P("dp", "mp"),
            P("dp", "mp"),
            P("dp", "mp"),
            P("dp", "mp"),
            P(None, "dp"),
            P(None, "dp"),
            P(None, "dp"),
            P(None, ("mp", "dp")),
            P(None, ("mp", "dp")),
            P(None, ("mp", "dp")),
            P(("mp", "dp")),
            P(("mp", "dp")),
            P(("mp", "dp")),
        ),
        out_specs=(
            P(),
            P("dp", None, None),
            P(None, "dp", "mp"),
            P(None, "dp", "mp"),
            P(None, "dp", "mp"),
            P("dp", "mp"),
            P("dp", "mp"),
            P("dp", "mp"),
            P("dp", "mp"),
            P("dp", "mp"),
            P("dp", "mp"),
            P("dp", "mp"),
            P("dp", "mp"),
            P("dp", "mp"),
            P(None, "dp"),
            P(None, "dp"),
            P(None, "dp"),
            P(None, ("mp", "dp")),
            P(None, ("mp", "dp")),
            P(None, ("mp", "dp")),
            P(("mp", "dp")),
            P(("mp", "dp")),
            P(("mp", "dp")),
            P(),
        ),
        check_vma=False,
    )
```

```python
import functools
import heapq

import jax
import jax.numpy as jnp
from jax import lax
from jax.experimental import pallas as pl
from jax.experimental.pallas import tpu as pltpu
from jax.sharding import PartitionSpec as P

HD = 64
STEP = 10


norm_epsilon = 1e-06
mask_value = -1000000000.0
sharpness_divisor = 50.0
loss_scale = 128.0
beta_first = 0.9
beta_second = 0.999
adam_epsilon = 1e-06
weight_decay = 0.01
learning_rate = 0.5
exact_arithmetic_mode = lax.Precision.HIGHEST


def layer_norm(values, gain, shift):
    center = values - jnp.mean(values, -1, keepdims=True)
    spread = jnp.mean(center * center, -1, keepdims=True)
    return center * lax.rsqrt(spread + norm_epsilon) * gain + shift


def normalize(values):
    return values * lax.rsqrt(jnp.sum(values * values, -1, keepdims=True) + norm_epsilon)


def summation_axes_spec(left, right, left_dim, right_dim):
    return lax.dot_general(
        left, right, (((left_dim,), (right_dim,)), ((), ())), preferred_element_type=jnp.float32
    )


def moments(weight, first, second, grad, decay):
    first_new = beta_first * first + (1.0 - beta_first) * grad
    second_new = beta_second * second + (1.0 - beta_second) * grad * grad
    first_hat = first_new / (1.0 - beta_first**STEP)
    second_hat = second_new / (1.0 - beta_second**STEP)
    update = first_hat / (jnp.sqrt(second_hat) + adam_epsilon) + decay * weight
    return (first_new, second_new, update)


def tensor_squares(qkv, out, upper, lower, affine, head, inner, replicas):
    return jnp.concatenate(
        [
            jnp.sum(qkv * qkv, (1, 2)),
            jnp.sum(out * out)[None],
            jnp.sum(upper * upper)[None],
            jnp.sum(lower * lower)[None],
            jnp.sum(affine * affine, 1) / replicas,
            jnp.sum(head * head, 1),
            jnp.sum(inner * inner)[None],
        ]
    )


def split_norms(norms):
    return (
        norms[0:3].reshape(3, 1, 1),
        norms[3],
        norms[4],
        norms[5],
        norms[6:12].reshape(6, 1),
        norms[12:14].reshape(2, 1),
        norms[14],
    )


def scaled_step(weight, update, weight_norm, update_norm):
    return weight - learning_rate * weight_norm / update_norm * update


MESH = pl.DeviceIdType.MESH
f32 = jnp.float32
bf16 = jnp.bfloat16
NROWS, SMALL, FAR = 32, 4.0, 8.0
PACE = (3.4, 2.2, 6.0, 5.0, 6.0)
WAYS = "xxxxxxxxxxxx"


class Place:
    def __init__(self, depth):
        self.depth = depth
        dp = lax.axis_index("dp")
        self.dp = dp
        self.x = lax.axis_index("mp")
        self.z, self.y, self.c = dp // 4, (dp // 2) % 2, dp % 2

    def at(self, z, y, c, x):
        return ((z * 2 + y) * 2 + c, x)

    def over_x(self):
        return self.at(self.z, self.y, self.c, 1 - self.x)

    def over_y(self):
        return self.at(self.z, 1 - self.y, self.c, self.x)

    def over_c(self):
        return self.at(self.z, self.y, 1 - self.c, self.x)

    def over_z(self, k):
        return self.at(lax.rem(self.z + k, self.depth), self.y, self.c, self.x)

    def in_plane(self, d):
        return self.at(self.z, 1 - self.y if d & 4 else self.y, 1 - self.c if d & 2 else self.c, 1 - self.x if d & 1 else self.x)

    def greet(self):
        sem = pltpu.get_barrier_semaphore()
        for peer in [self.in_plane(d) for d in range(1, 8)] + [self.over_z(k) for k in range(1, self.depth)]:
            pl.semaphore_signal(sem, inc=1, device_id=peer, device_id_type=MESH)

    def meet(self):
        pl.semaphore_wait(pltpu.get_barrier_semaphore(), 7 + self.depth - 1)


class Wire:
    def __init__(self, send, recv):
        self.send, self.recv, self.used, self.open = send, recv, 0, []

    def start(self, src, dst, device):
        i = self.used
        self.used += 1
        copy = pltpu.make_async_remote_copy(
            src_ref=src, dst_ref=dst, send_sem=self.send.at[i], recv_sem=self.recv.at[i], device_id=device, device_id_type=MESH
        )
        copy.start()
        self.open.append(copy)
        return copy

    def close(self):
        for copy in self.open:
            copy.wait_send()
        self.open = []


def arrive(copies):
    for copy in copies:
        copy.wait_recv()


class Timeline:
    def __init__(self):
        self.steps, self.count, self.now = [], 0, 0.0

    def add(self, time, step):
        heapq.heappush(self.steps, (time, self.count, step))
        self.count += 1

    def until(self, time):
        while self.steps and self.steps[0][0] <= time:
            at, _, step = heapq.heappop(self.steps)
            step(at)
        self.now = max(self.now, time)

    def tick(self, span):
        self.until(self.now + span)

    def drain(self):
        while self.steps:
            self.until(self.steps[0][0])


class Sheet:
    def __init__(self, full, u):
        self.full, self.u, self.half = full, u, full.shape[-1] // 2

    def part(self, z, y, c, x=None):
        lanes = pl.ds(0, 2 * self.half) if x is None else pl.ds(pl.multiple_of(x * self.half, 128), self.half)
        return self.full.at[self.u, z, y, c, :, lanes]


class Gather:
    def __init__(self, place, wire, line, items, pace):
        self.p, self.wire, self.line, self.items = place, wire, line, items
        self.flight, self.at = {}, []
        second, far_rate, to_one, rate, to_two, to_core, to_whole = pace
        one = -rate
        for i in range(len(items)):
            far = second + far_rate * (i - 1) if i else 0.0
            one = max(far + to_one, one + rate)
            two = one + to_two
            core = two + to_core
            self.at.append(core + to_whole)
            times = (far, one, two, core, core + to_whole)
            for time, step in zip(times, (self.far, self.one, self.two, self.core, self.whole)):
                line.add(time, lambda at, step=step, i=i: step(i))

    def far(self, i):
        p, it = self.p, self.items[i]
        mine = it.part(p.z, p.y, p.c, p.x)
        self.flight["z", i] = [self.wire.start(mine, mine, p.over_z(k)) for k in range(1, p.depth)]

    def one(self, i):
        p, it, h = self.p, self.items[i], self.p.depth // 2
        arrive(self.flight["z", i])
        a = it.part(pl.ds(0, h), p.y, p.c, p.x)
        b = it.part(pl.ds(h, p.depth - h), p.y, p.c, p.x)
        self.flight["1", i] = [self.wire.start(a, a, p.over_x()), self.wire.start(b, b, p.over_y())]

    def two(self, i):
        p, it, h = self.p, self.items[i], self.p.depth // 2
        arrive(self.flight["1", i])
        a = it.part(pl.ds(0, h), p.y, p.c)
        b = it.part(pl.ds(h, p.depth - h), slice(None), p.c, p.x)
        self.flight["2", i] = [self.wire.start(a, a, p.over_y()), self.wire.start(b, b, p.over_x())]

    def core(self, i):
        p, it = self.p, self.items[i]
        arrive(self.flight["2", i])
        r = it.part(slice(None), slice(None), p.c)
        self.flight["c", i] = [self.wire.start(r, r, p.over_c())]

    def whole(self, i):
        arrive(self.flight["c", i])

    def until(self, i):
        self.line.until(self.at[i])


def add_blocks(dst, src, count):
    for i in range(count):
        (d, at), (s, of) = dst(i), src(i)
        d[at] = d[at] + s[of]


class Reduce:
    def __init__(self, place, wire, line, order, ways, pace, free, part, from_core, one_a, one_b, two_a, two_b, from_z, total, use):
        self.p, self.wire, self.line, self.order, self.ways, self.free, self.use = place, wire, line, order, ways, free, use
        self.rate, self.to_one, self.to_two, self.to_far, self.to_last = pace
        self.next_one, self.count, self.takes = 0.0, 0, []
        self.part, self.from_core, self.one_a, self.one_b = part, from_core, one_a, one_b
        self.two_a, self.two_b, self.from_z, self.total = two_a, two_b, from_z, total
        self.h = place.depth // 2
        self.half = part.shape[-1] // 2
        self.slots = from_core.shape[0]
        self.flight = {}

    def lanes(self, x):
        return pl.ds(x * self.half if isinstance(x, int) else pl.multiple_of(x * self.half, 128), self.half)

    def core(self, i):
        p, u = self.p, self.order[i]
        if i >= self.slots:
            pl.semaphore_wait(self.free, 1)
        self.flight["c", i] = [self.wire.start(self.part.at[u, :, :, 1 - p.c], self.from_core.at[i % self.slots], p.over_c())]

    def take(self, i):
        p, u, Z, part = self.p, self.order[i], self.p.depth, self.part
        arrive(self.flight["c", i])
        add_blocks(
            lambda j: (part, (u, j // 2, j % 2, p.c)),
            lambda j: (self.from_core, (i % self.slots, j // 2, j % 2)), 2 * Z,
        )
        if i + self.slots < len(self.order):
            pl.semaphore_signal(self.free, inc=1, device_id=p.over_c(), device_id_type=MESH)

    def one(self, i):
        p, u, h, Z, part, way = self.p, self.order[i], self.h, self.p.depth, self.part, self.ways[i]
        start, flight = self.wire.start, []
        if way == "z":
            z1, z2, z3 = (lax.rem(p.z + k, Z) for k in (1, 2, 3))
            flight.append(start(part.at[u, z1, :, p.c], self.one_b.at[u], p.over_z(1)))
            for m in range(2):
                flight.append(start(part.at[u, z2, :, p.c, :, self.lanes(m)], self.one_a.at[u, :, m], p.over_z(2)))
                flight.append(start(part.at[u, z3, :, p.c, :, self.lanes(m)], (self.two_a, self.two_b)[m].at[u], p.over_z(3)))
        else:
            if way == "y":
                for m in range(2):
                    flight.append(start(part.at[u, pl.ds(0, h), 1 - p.y, p.c, :, self.lanes(m)], self.one_a.at[u, :, m], p.over_y()))
            else:
                flight.append(start(part.at[u, pl.ds(0, h), :, p.c, :, self.lanes(1 - p.x)], self.one_a.at[u], p.over_x()))
            flight.append(start(part.at[u, pl.ds(h, Z - h), 1 - p.y, p.c], self.one_b.at[u], p.over_y()))
        self.flight["1", i] = flight

    def two(self, i):
        p, u, h, Z, part, way = self.p, self.order[i], self.h, self.p.depth, self.part, self.ways[i]
        if way == "z":
            return
        arrive(self.flight["1", i])
        mine = self.lanes(p.x)
        if way == "y":
            for m in range(2):
                add_blocks(
                    lambda j: (part, (u, j, p.y, p.c, slice(None), self.lanes(m))), lambda j: (self.one_a, (u, j, m)), h
                )
            a, to_a = part.at[u, pl.ds(0, h), p.y, p.c, :, self.lanes(1 - p.x)], p.over_x()
        else:
            add_blocks(lambda j: (part, (u, j // 2, j % 2, p.c, slice(None), mine)), lambda j: (self.one_a, (u, j // 2, j % 2)), 2 * h)
            a, to_a = part.at[u, pl.ds(0, h), 1 - p.y, p.c, :, mine], p.over_y()
        add_blocks(lambda j: (part, (u, h + j, p.y, p.c)), lambda j: (self.one_b, (u, j)), Z - h)
        self.flight["2", i] = [
            self.wire.start(a, self.two_a.at[u], to_a),
            self.wire.start(part.at[u, pl.ds(h, Z - h), p.y, p.c, :, self.lanes(1 - p.x)], self.two_b.at[u], p.over_x()),
        ]

    def far(self, i):
        p, u, h, Z, part, way = self.p, self.order[i], self.h, self.p.depth, self.part, self.ways[i]
        mine = self.lanes(p.x)
        if way == "z":
            arrive(self.flight["1", i])
            for y in range(2):
                t = part[u, p.z, y, p.c].astype(f32) + self.one_b[u, y].astype(f32)
                left = t[:, : self.half] + self.one_a[u, y, 0].astype(f32) + self.two_a[u, y].astype(f32)
                right = t[:, self.half :] + self.one_a[u, y, 1].astype(f32) + self.two_b[u, y].astype(f32)
                part[u, p.z, y, p.c] = jnp.concatenate([left, right], 1).astype(part.dtype)
            others = ((p.y, 1 - p.x, 1), (1 - p.y, p.x, 4), (1 - p.y, 1 - p.x, 5))
            self.flight["z", i] = [
                self.wire.start(part.at[u, p.z, y, p.c, :, self.lanes(x)], self.from_z.at[k, u], p.in_plane(d))
                for k, (y, x, d) in enumerate(others)
            ]
            return
        arrive(self.flight["2", i])
        add_blocks(lambda j: (part, (u, j, p.y, p.c, slice(None), mine)), lambda j: (self.two_a, (u, j)), h)
        add_blocks(lambda j: (part, (u, h + j, p.y, p.c, slice(None), mine)), lambda j: (self.two_b, (u, j)), Z - h)
        self.flight["z", i] = [
            self.wire.start(part.at[u, lax.rem(p.z + k, Z), p.y, p.c, :, mine], self.from_z.at[k - 1, u], p.over_z(k))
            for k in range(1, Z)
        ]

    def last(self, i):
        p, u = self.p, self.order[i]
        arrive(self.flight["z", i])
        t = self.part[u, p.z, p.y, p.c, :, self.lanes(p.x)].astype(f32)
        for j in range(p.depth - 1):
            t = t + self.from_z[j, u].astype(f32)
        self.total[u] = t
        self.use(u, t)

    def step(self):
        i, line = self.count, self.line
        self.count += 1
        if i >= self.slots:
            line.until(self.takes[i - self.slots])
        self.core(i)
        time = line.now + self.to_one
        self.takes.append(time)
        line.add(time, lambda at: self.take(i))
        time = max(time, self.next_one)
        self.next_one = time + self.rate
        far = self.to_far + FAR if self.ways[i] == "z" else self.to_far
        for span, step in ((0.0, self.one), (self.to_two, self.two), (far, self.far), (self.to_last, self.last)):
            time += span
            line.add(time, lambda at, step=step: step(i))


class SumAll:
    def __init__(self, place, wire, own, room):
        self.p, self.wire, self.own, self.room = place, wire, own, room
        self.stage = 0

    def start(self):
        p = self.p
        if self.stage < 3:
            device = (p.over_c, p.over_x, p.over_y)[self.stage]()
            self.flight = [self.wire.start(self.own, self.room.at[self.stage], device)]
        else:
            self.flight = [self.wire.start(self.own, self.room.at[3 + p.z], p.over_z(k)) for k in range(1, p.depth)]

    def finish(self):
        p = self.p
        arrive(self.flight)
        for copy in self.flight:
            copy.wait_send()
        self.wire.open = [c for c in self.wire.open if all(c is not f for f in self.flight)]
        if self.stage < 3:
            self.own[...] = self.own[...] + self.room[self.stage]
        else:
            self.room[3 + p.z] = self.own[...]
            t = self.room[3]
            for z in range(1, p.depth):
                t = t + self.room[3 + z]
            self.own[...] = t
        self.stage += 1

    def run(self):
        while self.stage < 4:
            self.start()
            self.finish()


class SumSoon:
    def __init__(self, place, wire, own, plane, line):
        p = place
        slot = (p.y * 2 + p.c) * 2 + p.x
        plane[slot] = own[...]
        arrive([wire.start(own, plane.at[slot], p.in_plane(d)) for d in range(1, 8)])
        value = plane[0]
        for d in range(1, 8):
            value = value + plane[d]
        line[p.z] = value
        arrive([wire.start(line.at[p.z], line.at[p.z], p.over_z(k)) for k in range(1, p.depth)])
        value = line[0]
        for z in range(1, p.depth):
            value = value + line[z]
        self.value = value


class Pictures:
    def __init__(self, place, wire, line, full, size, pace):
        self.p, self.wire, self.full = place, wire, full
        mine = full.at[place.z, place.y, place.c]
        self.flight = [wire.start(mine, mine, place.over_y())]
        self.pieces = [(k, at, size) for at in range(0, full.shape[3], size) for k in range(1, place.depth)]
        self.sent = 0
        first, rate, to_core, to_whole = pace
        for i in range(len(self.pieces)):
            line.add(first + rate * i, lambda at: self.step())
        core = first + rate * len(self.pieces) + to_core
        self.at = core + to_whole
        line.add(core, lambda at: self.core())
        line.add(self.at, lambda at: self.whole())

    def step(self):
        p = self.p
        if self.sent == 0:
            arrive(self.flight)
            self.flight = []
        k, at, size = self.pieces[self.sent]
        mine = self.full.at[p.z, :, p.c, pl.ds(at, size)]
        self.flight.append(self.wire.start(mine, mine, p.over_z(k)))
        self.sent += 1

    def core(self):
        arrive(self.flight)
        r = self.full.at[:, :, self.p.c]
        self.flight = [self.wire.start(r, r, self.p.over_c())]

    def whole(self):
        arrive(self.flight)


def dot(a, b, left=1, right=0):
    return lax.dot_general(a, b, (((left,), (right,)), ((), ())), preferred_element_type=f32)


def row_loop(count, size, f, start=0):
    def step(i, carry):
        f(pl.ds(pl.multiple_of(start + i * size, size), size))
        return carry

    lax.fori_loop(0, count // size, step, 0)


def center_scale(x):
    center = x - jnp.mean(x, -1, keepdims=True)
    return center, lax.rsqrt(jnp.mean(center * center, -1, keepdims=True) + norm_epsilon)


def three(x):
    hi = x.astype(bf16)
    rest = x - hi.astype(f32)
    mid = rest.astype(bf16)
    return hi, mid, (rest - mid.astype(f32)).astype(bf16)


def fold(x):
    return jnp.sum(x.reshape(x.shape[0] // 8, 8, x.shape[1]), 0)


def placing(n, at, lanes):
    spot = lax.broadcasted_iota(jnp.int32, (n, lanes), 1) == lax.broadcasted_iota(jnp.int32, (n, lanes), 0) + at
    return jnp.where(spot, 1.0, 0.0).astype(bf16)


def picked(a, at, n):
    spot = placing(n, at, a.shape[1])
    return sum(dot(term, spot, 1, 1) for term in three(a))


def row_of(a, at):
    rows = lax.broadcasted_iota(jnp.int32, a.shape, 0) == at
    return jnp.sum(jnp.where(rows, a, jnp.zeros_like(a)), 0, keepdims=True)


def block_kernel(
    depth,
    tokens, segment, pairing, images, qkv_weight, out_weight, up_weight, down_weight, affine, head_bias, inner_bias,
    qkv_first, qkv_second, out_first, out_second, up_first, up_second, down_first, down_second,
    affine_first, affine_second, head_first, head_second, inner_first, inner_second,
    total, small_grad, norms, grad_low,
    full, pictures, part, from_core, one_a, one_b, two_a, two_b, from_z,
    tok, normed_one, qkv, mixed, resid, normed_two, hidden, slope, stream, grad_mixed, acc, low,
    probs, same, wide, sums, room, room2, folds, cap,
    old_qkv, old_out, old_up, old_down, squares, tile_sums, plane, line,
    send, recv, free, local, local_old,
):
    place = Place(depth)
    place.greet()
    x, dp = place.x, place.dp
    rows, width = tok.shape
    packs, length = 2, rows // 2
    half = qkv_weight.shape[2]
    units = full.shape[0]
    share = full.shape[4]
    blocks = up_weight.shape[1] // half
    up0, down0 = 4, 4 + blocks

    token_copies = [
        pltpu.make_async_copy(tokens.at[packs * x + p], tok.at[pl.ds(p * length, length)], local.at[p]) for p in range(packs)
    ]
    pairs_old = ((qkv_first, qkv_second, old_qkv), (out_first, out_second, old_out), (up_first, up_second, old_up), (down_first, down_second, old_down))
    old_copies = []
    for i, (one, two, kept) in enumerate(pairs_old):
        old_copies += [pltpu.make_async_copy(one, kept.at[0], local_old.at[2 * i]), pltpu.make_async_copy(two, kept.at[1], local_old.at[2 * i + 1])]
    for copy in token_copies + old_copies:
        copy.start()

    mine_lanes = pl.ds(pl.multiple_of(x * half, 128), half)

    def keep(u, value):
        full[u, place.z, place.y, place.c, :, mine_lanes] = value.astype(bf16)

    for k in range(3):
        keep(k, qkv_weight[k])
    keep(3, out_weight[...])
    for j in range(blocks):
        keep(up0 + j, up_weight[:, j * half : (j + 1) * half])
        keep(down0 + j, down_weight[:, j * half : (j + 1) * half])
    pictures[place.z, place.y, place.c] = normalize(images[...].astype(f32)).astype(bf16)

    place.meet()
    wire = Wire(send, recv)
    moves = Timeline()
    tick = moves.tick
    scenes = Pictures(place, wire, moves, pictures, 16, (24.0, 2.0, 3.0, 3.0))
    gather = Gather(place, wire, moves, [Sheet(full, u) for u in range(units)], (2.5, 3.5, 2.6, 3.8, 3.9, 8.0, 6.0))
    ready = gather.until
    tick(0.0)

    owner = x * (4 * depth) + dp
    n_affine, n_head, n_inner = affine.shape[1], head_bias.shape[1], inner_bias.shape[1]
    first = jnp.where(x == 0, 1.0, 0.0)
    inner_rows = 2 * blocks * half // width
    inner_at, inner_row = (owner * n_inner) % width, (owner * n_inner) // width
    wide[...] = jnp.zeros_like(wide)
    wide[0:6] = dot(affine[...].astype(bf16), placing(n_affine, dp * n_affine, width)) * first
    wide[6:8] = dot(head_bias[...].astype(bf16), placing(n_head, owner * n_head, width))
    inner_wide = dot(inner_bias[...].astype(bf16), placing(n_inner, inner_at, width))
    at_row = lax.broadcasted_iota(jnp.int32, (inner_rows, width), 0) == inner_row
    wide[8 : 8 + inner_rows] = jnp.where(at_row, jnp.broadcast_to(inner_wide, (inner_rows, width)), 0.0)
    spread = SumAll(place, wire, wide, room)
    spread.start()

    slots = pairing.shape[1]
    tile, window = 64, 128
    starts = [min(max(t * tile - (window - tile) // 2, 0), length - window) for t in range(length // tile)]
    onehots = []
    for p in range(packs):
        seg = jnp.broadcast_to(row_of(segment[...], packs * x + p), (slots, length))
        onehot = jnp.where(seg == lax.broadcasted_iota(jnp.int32, (slots, length), 0), 1.0, 0.0)
        onehots.append(onehot)
        low_hot = onehot.astype(bf16)
        both = acc.at[pl.ds(0, length), pl.ds(0, length)]
        both[...] = dot(low_hot, low_hot, 0, 0)
        for t, w in enumerate(starts):
            shared = dot(both[pl.ds(t * tile, tile)].astype(bf16), placing(window, w, length), 1, 1)
            same[p, t, 0:tile] = shared
            same[p, t, tile : 2 * tile] = shared
        tick(1.5)
        if p == 0:
            spread.finish()
            spread.start()
    while spread.stage < 4:
        tick(2.0)
        spread.finish()
        if spread.stage < 4:
            spread.start()

    for copy in token_copies:
        copy.wait()

    def norm_one(r):
        center, scale = center_scale(tok[r].astype(f32))
        normed_one[r] = (center * scale * wide[0:1] + wide[1:2]).astype(bf16)

    row_loop(rows, NROWS, norm_one)
    tick(3.0)

    def unit(u):
        return full[u].reshape(width, width)

    chunk = 256

    def unit_lanes(u, j):
        return full[u, :, :, :, :, pl.ds(j * chunk, chunk)].reshape(width, chunk)

    for k in range(3):
        ready(k)
        for j in range(width // chunk):
            lanes = pl.ds(j * chunk, chunk)
            value = dot(normed_one[...], unit_lanes(k, j))
            if k != 1:
                row = 6 if k == 0 else 7
                value = value + wide[row : row + 1, lanes]
            qkv[k, :, lanes] = value.astype(bf16)
        tick(1.0)

    root_scale = HD**-0.5
    pair = 2 * HD
    pairs = width // pair
    lower = lax.broadcasted_iota(jnp.int32, (tile, pair), 1) < HD

    def doubled(a):
        zero = jnp.zeros_like(a)
        return jnp.concatenate([jnp.where(lower, a, zero), jnp.where(lower, zero, a)], 0)

    def joined(a):
        return jnp.where(lower, a[:tile], a[tile:])

    def attend(p, g):
        lanes = pl.ds(pl.multiple_of(g * pair, pair), pair)
        span = pl.ds(p * length, length)
        query, keys, values = qkv[0, span, lanes], qkv[1, span, lanes], qkv[2, span, lanes]
        found, weights = [], []
        for t, w in enumerate(starts):
            scores = dot(doubled(query[t * tile : (t + 1) * tile]), keys[w : w + window], 1, 1) * root_scale
            scores = jnp.where(same[p, t] > 0.5, scores, mask_value)
            e = jnp.exp(scores - jnp.max(scores, -1, keepdims=True))
            prob = (e * (1.0 / jnp.sum(e, -1, keepdims=True))).astype(bf16)
            weights.append(prob)
            found.append(joined(dot(prob, values[w : w + window])).astype(bf16))
        for t in range(len(starts)):
            probs[p, g, t] = weights[t]
        mixed[span, lanes] = jnp.concatenate(found, 0)

    def each_pair(f, p, some):
        def step(g, carry):
            f(p, g)
            return carry

        lax.fori_loop(some[0], some[1], step, 0, unroll=some[1] - some[0])

    for p in range(packs):
        for some in ((0, pairs // 2), (pairs // 2, pairs)):
            each_pair(attend, p, some)
            tick(1.5)

    ready(3)
    acc[...] = dot(mixed[...], unit(3), 1, 1)
    tick(1.0)

    def norm_two(r):
        value = tok[r].astype(f32) + acc[r] + wide[4:5]
        resid[r] = value
        center, scale = center_scale(value)
        normed_two[r] = (center * scale * wide[2:3] + wide[3:4]).astype(bf16)
        stream[r] = value + wide[5:6]

    row_loop(rows, NROWS, norm_two)
    tick(3.0)

    def inner_lanes(j):
        at = j * half
        return ((8 + at // width, at % width), (8 + (blocks * half + at) // width, (blocks * half + at) % width))

    curve = (2.0 / jnp.pi) ** 0.5
    for j in range(blocks):
        ready(up0 + j)
        bias = jnp.concatenate([wide[row : row + 1, lane : lane + half] for row, lane in inner_lanes(j)], 1)
        for k in range(width // chunk):
            lanes = pl.ds(k * chunk, chunk)
            acc[:, lanes] = dot(normed_two[...], unit_lanes(up0 + j, k))

        def activate(r, j=j, bias=bias):
            u = acc[r] + bias
            square = u * u
            t = jnp.tanh(curve * (u + 0.044715 * (square * u)))
            hidden[j, r] = (0.5 * u * (1.0 + t)).astype(bf16)
            slope[j, r] = (0.5 * (1.0 + t) + 0.5 * u * (1.0 - t * t) * (curve * (1.0 + 3.0 * 0.044715 * square))).astype(bf16)

        row_loop(rows, 16, activate)
        tick(2.5)

    for j in range(blocks):
        ready(down0 + j)
        stream[...] += dot(hidden[j], unit(down0 + j), 1, 1)
    moves.drain()

    count_rows, target_rows = [], []
    for p in range(packs):
        count = jnp.sum(onehots[p], 1, keepdims=True)
        hot = onehots[p].astype(bf16)
        hi, mid, lo = three(stream[pl.ds(p * length, length)])
        pooled = dot(hot, hi) + dot(hot, mid) + dot(hot, lo)
        cap[pl.ds(p * slots, slots)] = pooled / jnp.maximum(count, 1.0)
        count_rows.append(count)
        names = jnp.broadcast_to(row_of(pairing[...], packs * x + p), (slots, slots)).astype(f32)
        diagonal = lax.broadcasted_iota(jnp.int32, (slots, slots), 0) == lax.broadcasted_iota(jnp.int32, (slots, slots), 1)
        target_rows.append(jnp.sum(jnp.where(diagonal, names, 0.0), 1, keepdims=True))
    counts = jnp.concatenate(count_rows, 0)
    target = jnp.concatenate(target_rows, 0)
    live = jnp.where(counts > 0.0, 1.0, 0.0)
    pooled = cap[...]
    radius = lax.rsqrt(jnp.sum(pooled * pooled, -1, keepdims=True) + norm_epsilon)
    caption = (pooled * radius).astype(bf16)
    all_images = pictures[...].reshape(-1, width)
    logits = sharpness_divisor * dot(caption, all_images, 1, 1)
    hit = lax.broadcasted_iota(jnp.int32, logits.shape, 1).astype(f32) == target
    best = jnp.max(logits, -1, keepdims=True)
    e = jnp.exp(logits - best)
    sum_e = jnp.sum(e, -1, keepdims=True)
    positive = jnp.sum(jnp.where(hit, logits, 0.0), -1, keepdims=True)
    cross = best + jnp.log(sum_e) - positive
    loss = jnp.sum(live * cross, 0, keepdims=True)
    grad_logits = (loss_scale * live * (e * (1.0 / sum_e) - jnp.where(hit, 1.0, 0.0))).astype(bf16)
    grad_caption = sharpness_divisor * dot(grad_logits, all_images)
    inner = jnp.sum(pooled * grad_caption, -1, keepdims=True)
    grad_pooled = radius * grad_caption - (radius * radius * radius) * inner * pooled
    grad_pooled = grad_pooled / jnp.maximum(counts, 1.0)
    folds[...] = jnp.zeros_like(folds)
    for p in range(packs):
        hot = onehots[p].astype(bf16)
        hi, mid, lo = three(grad_pooled[p * slots : (p + 1) * slots])
        stream[pl.ds(p * length, length)] = dot(hot, hi, 0, 0) + dot(hot, mid, 0, 0) + dot(hot, lo, 0, 0)

    def lower_stream(r):
        value = stream[r]
        low[r] = value.astype(bf16)
        folds[5] += fold(value)

    row_loop(rows, 32, lower_stream)

    squares[...] = jnp.zeros_like(squares)
    for copy in old_copies:
        copy.wait()

    def lanes_folded(a):
        a = fold(a)
        return sum(a[:, i * 128 : (i + 1) * 128] for i in range(a.shape[1] // 128))

    def use(u, grad):
        if u < 3:
            weight, one, two, row = qkv_weight[u], old_qkv[0, u], old_qkv[1, u], u
        elif u == 3:
            weight, one, two, row = out_weight[...], old_out[0], old_out[1], 3
        else:
            row = 4 if u < down0 else 5
            at = (u - up0) % blocks * half
            weights, kept = (up_weight, old_up) if row == 4 else (down_weight, old_down)
            weight, one, two = weights[:, at : at + half], kept[0, :, at : at + half], kept[1, :, at : at + half]
        update = moments(weight, one, two, grad, weight_decay)[2]
        squares[0, row] += lanes_folded(weight * weight)
        squares[1, row] += lanes_folded(update * update)

    order = [down0 + j for j in range(blocks)] + [up0 + j for j in range(blocks)] + [3, 0, 1, 2]
    reduce = Reduce(place, wire, moves, order, WAYS if depth == 4 and len(order) == len(WAYS) else "x" * len(order), PACE, free, part, from_core, one_a, one_b, two_a, two_b, from_z, total, use)

    def weight_grad(u, left, right):
        for j in range(width // chunk):
            lanes = pl.ds(j * chunk, chunk)
            value = dot(left, right(lanes), 0, 0).astype(bf16)
            part[u, :, :, :, :, lanes] = value.reshape(depth, 2, 2, share, chunk)
        tick(0.7)
        reduce.step()

    sums[...] = jnp.zeros_like(sums)
    for j in range(blocks):
        weight_grad(down0 + j, low[...], lambda lanes, j=j: hidden[j, :, lanes])
        for k in range(width // chunk):
            lanes = pl.ds(k * chunk, chunk)
            acc[:, lanes] = dot(low[...], unit_lanes(down0 + j, k))

        def upper_back(r, j=j):
            value = (acc[r] * slope[j, r].astype(f32)).astype(bf16)
            hidden[j, r] = value
            folds[6] += fold(value.astype(f32))

        folds[6] = jnp.zeros_like(folds[6])
        row_loop(rows, 32, upper_back)
        tick(1.2)
        inner_sum = jnp.sum(folds[6], 0, keepdims=True)
        for i, (row, lane) in enumerate(inner_lanes(j)):
            sums[row : row + 1, lane : lane + half] = inner_sum[:, i * half : (i + 1) * half]

    for j in range(blocks):
        weight_grad(up0 + j, normed_two[...], lambda lanes, j=j: hidden[j, :, lanes])
        value = dot(hidden[j], unit(up0 + j), 1, 1)
        if j == 0:
            acc[...] = value
        else:
            acc[...] += value
        tick(0.7)

    def norm_two_back(r):
        center, scale = center_scale(resid[r])
        hat = center * scale
        grad = acc[r]
        weighted = grad * wide[2:3]
        value = stream[r] + scale * (
            weighted - jnp.mean(weighted, -1, keepdims=True) - hat * jnp.mean(weighted * hat, -1, keepdims=True)
        )
        stream[r] = value
        low[r] = value.astype(bf16)
        folds[2] += fold(grad * hat)
        folds[3] += fold(grad)
        folds[4] += fold(value)

    row_loop(rows, NROWS, norm_two_back)
    tick(4.0)
    weight_grad(3, low[...], lambda lanes: mixed[:, lanes])
    for k in range(width // chunk):
        lanes = pl.ds(k * chunk, chunk)
        grad_mixed[:, lanes] = dot(low[...], unit_lanes(3, k)).astype(bf16)
    tick(0.7)

    def overlaid(pieces):
        step = 32
        found = []
        for at in range(0, length, step):
            found.append(sum(piece[at - w : at - w + step] for w, piece in zip(starts, pieces) if w <= at < w + window))
        return jnp.concatenate(found, 0)

    def attend_back(p, g):
        lanes = pl.ds(pl.multiple_of(g * pair, pair), pair)
        span = pl.ds(p * length, length)
        query, keys, values, grads = qkv[0, span, lanes], qkv[1, span, lanes], qkv[2, span, lanes], grad_mixed[span, lanes]
        of_query, of_keys, of_values = [], [], []
        for t, w in enumerate(starts):
            some = doubled(query[t * tile : (t + 1) * tile])
            grad = doubled(grads[t * tile : (t + 1) * tile])
            prob = probs[p, g, t]
            prob_wide = prob.astype(f32)
            grad_prob = dot(grad, values[w : w + window], 1, 1)
            grad_score = prob_wide * (grad_prob - jnp.sum(prob_wide * grad_prob, -1, keepdims=True))
            grad_score = grad_score.astype(bf16)
            of_keys.append(dot(grad_score, some, 0, 0))
            of_values.append(dot(prob, grad, 0, 0))
            of_query.append((joined(dot(grad_score, keys[w : w + window])) * root_scale).astype(bf16))
        qkv[0, span, lanes] = jnp.concatenate(of_query, 0)
        qkv[1, span, lanes] = (overlaid(of_keys) * root_scale).astype(bf16)
        qkv[2, span, lanes] = overlaid(of_values).astype(bf16)

    for p in range(packs):
        for some in ((0, pairs // 2), (pairs // 2, pairs)):
            each_pair(attend_back, p, some)
            tick(3.2)

    for k in range(3):
        value = dot(qkv[k], unit(k), 1, 1)
        if k == 0:
            acc[...] = value
        else:
            acc[...] += value
    tick(2.0)

    def norm_one_back(r):
        center, scale = center_scale(tok[r].astype(f32))
        hat = center * scale
        grad = acc[r]
        weighted = grad * wide[0:1]
        value = stream[r] + scale * (
            weighted - jnp.mean(weighted, -1, keepdims=True) - hat * jnp.mean(weighted * hat, -1, keepdims=True)
        )
        low[r] = value.astype(bf16)
        folds[0] += fold(grad * hat)
        folds[1] += fold(grad)

    swaps, outs = [], []
    for p in range(packs):
        row_loop(length, NROWS, norm_one_back, p * length)
        mine, there = low.at[pl.ds(p * length, length)], grad_low.at[packs * x + p]
        swaps.append(wire.start(mine, there, place.over_x()))
        outs.append(pltpu.make_async_copy(mine, there, local.at[p]))
        outs[-1].start()
        tick(2.3)

    for k in range(3):
        weight_grad(k, normed_one[...], lambda lanes, k=k: qkv[k, :, lanes])
        tick(0.3)

    def head_sums(r):
        folds[7] += fold(qkv[0, r].astype(f32))
        folds[8] += fold(qkv[2, r].astype(f32))

    row_loop(rows, 32, head_sums)
    for k, row in ((0, 0), (1, 1), (2, 2), (3, 3), (4, 4), (5, 5), (7, 6), (8, 7)):
        sums[row : row + 1] = jnp.sum(folds[k], 0, keepdims=True)
    last_row = 8 + inner_rows
    sums[last_row : last_row + 1] = jnp.broadcast_to(loss, (1, width))
    small_sum = SumAll(place, wire, sums, room2)
    small_sum.start()

    def small_step(at):
        small_sum.finish()
        if small_sum.stage < 4:
            small_sum.start()

    def small_parts(at):
        small_grad[...] = jnp.zeros_like(small_grad)
        tile_sums[...] = jnp.zeros_like(tile_sums)
        of_affine = picked(sums[0:6], dp * n_affine, n_affine)
        of_head = picked(sums[6:8], owner * n_head, n_head)
        of_inner = picked(row_of(sums[8 : 8 + inner_rows], inner_row), inner_at, n_inner)
        small_grad[0:6, 0:n_affine] = of_affine
        small_grad[6:8, 0:n_head] = of_head
        small_grad[8:9, 0:n_inner] = of_inner
        small_grad[9:10] = sums[last_row : last_row + 1, 0:128]
        smalls = (
            (6, 6, n_affine, affine[...], affine_first[...], affine_second[...], of_affine, first),
            (12, 2, n_head, head_bias[...], head_first[...], head_second[...], of_head, 1.0),
            (14, 1, n_inner, inner_bias[...], inner_first[...], inner_second[...], of_inner, 1.0),
        )
        for row, n, lanes, weight, one, two, grad, share_of in smalls:
            update = moments(weight, one, two, grad, 0.0)[2]
            tile_sums[row : row + n, 0:lanes] = weight * weight * share_of
            tile_sums[16 + row : 16 + row + n, 0:lanes] = update * update * share_of


    for k in range(4):
        moves.add(moves.now + SMALL * (k + 1), small_step)
    moves.add(moves.now + SMALL * 4 + 1.0, small_parts)
    moves.drain()
    for k in range(2):
        for row in range(6):
            tile_sums[16 * k + row : 16 * k + row + 1] = jnp.sum(squares[k, row], 0, keepdims=True)
    every = SumSoon(place, wire, tile_sums, plane, line).value
    norms[...] = jnp.broadcast_to(jnp.sqrt(jnp.sum(every, -1, keepdims=True)), norms.shape)
    arrive(swaps)
    for copy in outs:
        copy.wait()
    wire.close()


def block_step(depth, *arrays):
    tokens, segment, pairing, images, qkv_weight, out_weight, up_weight, down_weight = arrays[:8]
    packs, length, width = tokens.shape
    rows = packs // 2 * length
    share, half = qkv_weight.shape[1:]
    blocks = up_weight.shape[1] // half
    units = 4 + 2 * blocks
    slots = pairing.shape[1]
    h = depth // 2
    few = images.shape[0]
    ring = 4
    small = (16, width)
    low = lambda *shape: pltpu.VMEM(shape, bf16)
    wide = lambda *shape: pltpu.VMEM(shape, f32)
    count = units * (depth - 1 + 5) + (depth - 1) * (few // 16) + 2 + units * (8 + depth - 1) + 2 * (3 + depth - 1) + 2 + 7 + depth - 1
    vmem = pl.BlockSpec(memory_space=pltpu.VMEM)
    hbm = pl.BlockSpec(memory_space=pl.ANY)
    return pl.pallas_call(
        functools.partial(block_kernel, depth),
        out_shape=(
            jax.ShapeDtypeStruct((units, share, half), f32),
            jax.ShapeDtypeStruct((16, 128), f32),
            jax.ShapeDtypeStruct((32, 128), f32),
            jax.ShapeDtypeStruct(tokens.shape, bf16),
        ),
        in_specs=[hbm] + [vmem] * 10 + [hbm] * 8 + [vmem] * 6,
        out_specs=[vmem, vmem, vmem, hbm],
        scratch_shapes=[
            low(units, depth, 2, 2, share, width), low(depth, 2, 2, few, width),
            low(units, depth, 2, 2, share, width), low(ring, depth, 2, share, width), low(units, h, 2, share, half),
            low(units, depth - h, share, width), low(units, h, share, half), low(units, depth - h, share, half),
            low(depth - 1, units, share, half),
            low(rows, width), low(rows, width), low(3, rows, width), low(rows, width), wide(rows, width), low(rows, width),
            low(blocks, rows, width), low(blocks, rows, width), wide(rows, width), low(rows, width), wide(rows, width), low(rows, width),
            low(2, width // (2 * HD), length // 64, 128, 128), wide(2, length // 64, 128, 128), wide(*small), wide(*small),
            wide(3 + depth, *small), wide(3 + depth, *small), wide(9, 8, width), wide(2 * slots, width),
            wide(2, *qkv_weight.shape), wide(2, *out_weight.shape), wide(2, *up_weight.shape), wide(2, *down_weight.shape),
            wide(2, 6, 8, 128), wide(32, 128), wide(8, 32, 128), wide(depth, 32, 128),
            pltpu.SemaphoreType.DMA((count,)), pltpu.SemaphoreType.DMA((count,)), pltpu.SemaphoreType.REGULAR,
            pltpu.SemaphoreType.DMA((2,)), pltpu.SemaphoreType.DMA((8,)),
        ],
        compiler_params=pltpu.CompilerParams(collective_id=1, has_side_effects=True, vmem_limit_bytes=64 << 20),
        name="train_block",
    )(*arrays)


def finish_kernel(slot_total, total, small_grad, norms, grad_low, *refs):
    weights, firsts, seconds = refs[0:7], refs[7:14], refs[14:21]
    grad_input = refs[21]
    nexts, first_nexts, second_nexts = refs[22:29], refs[29:36], refs[36:43]
    mean_loss, tensor_norms, room, wide_room, sems = refs[43:48]
    packs = grad_low.shape[0]
    reads = [pltpu.make_async_copy(grad_low.at[p], room.at[p], sems.at[p]) for p in range(packs)]
    writes = [pltpu.make_async_copy(wide_room.at[p], grad_input.at[p], sems.at[packs + p]) for p in range(packs)]
    for copy in reads:
        copy.start()

    def update(i, at, grad, row, decay):
        weight, one, two = weights[i][at], firsts[i][at], seconds[i][at]
        first_new, second_new, change = moments(weight, one, two, grad, decay)
        first_nexts[i][at] = first_new
        second_nexts[i][at] = second_new
        count = 1 if isinstance(row, int) else row[1]
        row = row if isinstance(row, int) else row[0]
        weight_norm, update_norm = norms[row : row + count, 0:1], norms[16 + row : 16 + row + count, 0:1]
        nexts[i][at] = weight - learning_rate * weight_norm / update_norm * change

    every = slice(None)
    half = total.shape[2]
    blocks = weights[2].shape[1] // half
    for p in range(packs):
        reads[p].wait()

        def widen(r, p=p):
            wide_room[p, r] = room[p, r].astype(f32)

        row_loop(room.shape[1], 32, widen)
        writes[p].start()
    for k in range(3):
        update(0, (k,), total[k], k, weight_decay)
    update(1, (every,), total[3], 3, weight_decay)
    for i in range(2):
        for j in range(blocks):
            update(2 + i, (every, slice(j * half, (j + 1) * half)), total[4 + i * blocks + j], 4 + i, weight_decay)
    update(4, (every,), small_grad[0:6, 0 : weights[4].shape[1]], (6, 6), 0.0)
    update(5, (every,), small_grad[6:8, 0 : weights[5].shape[1]], (12, 2), 0.0)
    update(6, (every,), small_grad[8:9, 0 : weights[6].shape[1]], 14, 0.0)
    mean_loss[...] = small_grad[9:10, 0:1] / slot_total
    square = norms.shape[0] // 2
    diagonal = lax.broadcasted_iota(jnp.int32, (square, square), 0) == lax.broadcasted_iota(jnp.int32, (square, square), 1)
    for k in range(2):
        column = jnp.broadcast_to(norms[square * k : square * (k + 1), 0:1], (square, square))
        tensor_norms[k : k + 1] = jnp.sum(jnp.where(diagonal, column, 0.0), 0, keepdims=True)[:, 0:15]
    for copy in writes:
        copy.wait()


def finish_step(slot_total, total, small_grad, norms, grad_low, weights, firsts, seconds):
    vmem = pl.BlockSpec(memory_space=pltpu.VMEM)
    hbm = pl.BlockSpec(memory_space=pl.ANY)
    packs, length, width = grad_low.shape
    like = [jax.ShapeDtypeStruct(a.shape, f32) for a in weights]
    return pl.pallas_call(
        functools.partial(finish_kernel, slot_total),
        out_shape=(
            jax.ShapeDtypeStruct(grad_low.shape, f32), *like, *like, *like,
            jax.ShapeDtypeStruct((1, 1), f32), jax.ShapeDtypeStruct((2, 15), f32),
        ),
        in_specs=[vmem] * 3 + [hbm] + [vmem] * 21,
        out_specs=[hbm] + [vmem] * 23,
        scratch_shapes=[
            pltpu.VMEM((packs, length, width), bf16), pltpu.VMEM((packs, length, width), f32),
            pltpu.SemaphoreType.DMA((2 * packs,)),
        ],
        compiler_params=pltpu.CompilerParams(vmem_limit_bytes=64 << 20),
        name="optimizer",
    )(total, small_grad, norms, grad_low, *weights, *firsts, *seconds)


def body_near(depth, *arrays):
    (
        tokens, segment, pairing, images,
        qkv_weight, qkv_first, qkv_second, out_weight, out_first, out_second,
        up_weight, up_first, up_second, down_weight, down_first, down_second,
        affine, affine_first, affine_second, head_bias, head_first, head_second,
        inner_bias, inner_first, inner_second,
    ) = arrays
    inner_bias, inner_first, inner_second = (a.reshape(1, -1) for a in (inner_bias, inner_first, inner_second))
    total, small_grad, norms, grad_low = block_step(
        depth, tokens, segment, pairing, images, qkv_weight, out_weight, up_weight, down_weight, affine, head_bias, inner_bias,
        qkv_first, qkv_second, out_first, out_second, up_first, up_second, down_first, down_second,
        affine_first, affine_second, head_first, head_second, inner_first, inner_second,
    )
    weights = (qkv_weight, out_weight, up_weight, down_weight, affine, head_bias, inner_bias)
    firsts = (qkv_first, out_first, up_first, down_first, affine_first, head_first, inner_first)
    seconds = (qkv_second, out_second, up_second, down_second, affine_second, head_second, inner_second)
    slot_total = float(pairing.size * 4 * depth)
    grad_input, *news, mean_loss, tensor_norms = finish_step(slot_total, total, small_grad, norms, grad_low, weights, firsts, seconds)
    results = [mean_loss.reshape(()), grad_input]
    for i in range(7):
        triple = (news[i], news[7 + i], news[14 + i])
        results += [a.reshape(-1) for a in triple] if i == 6 else triple
    return (*results, tensor_norms)


def body(
    tokens,
    segment,
    pairing,
    images,
    qkv_weight,
    qkv_first,
    qkv_second,
    out_weight,
    out_first,
    out_second,
    up_weight,
    up_first,
    up_second,
    down_weight,
    down_first,
    down_second,
    affine,
    affine_first,
    affine_second,
    head_bias,
    head_first,
    head_second,
    inner_bias,
    inner_first,
    inner_second,
):
    model_size = lax.axis_size("mp")
    packs, length, width = tokens.shape
    rows = packs * length
    qkv_full, out_full, up_full, down_full, affine_full, head_full, inner_full = (
        lax.all_gather(qkv_weight.astype(jnp.bfloat16), "dp", axis=1, tiled=True),
        lax.all_gather(out_weight.astype(jnp.bfloat16), "dp", axis=0, tiled=True),
        lax.all_gather(up_weight.astype(jnp.bfloat16), "dp", axis=0, tiled=True),
        lax.all_gather(down_weight.astype(jnp.bfloat16), "dp", axis=0, tiled=True),
        lax.all_gather(affine.astype(jnp.bfloat16), "dp", axis=1, tiled=True),
        lax.all_gather(head_bias.astype(jnp.bfloat16), "dp", axis=1, tiled=True),
        lax.all_gather(inner_bias.astype(jnp.bfloat16), "dp", axis=0, tiled=True),
    )
    affine_wide = affine_full.astype(jnp.float32)
    head_wide = head_full.astype(jnp.float32)
    inner_wide = inner_full.astype(jnp.float32)
    half = qkv_full.shape[2]
    local_heads = half // HD
    shape4 = (packs, length, local_heads, HD)
    root_scale = HD ** (-0.5)
    inputs = tokens.reshape(rows, width).astype(jnp.float32)
    normed_one = layer_norm(inputs, affine_wide[0], affine_wide[1]).astype(jnp.bfloat16)
    projected = jnp.einsum("td,kde->kte", normed_one, qkv_full, preferred_element_type=jnp.float32)
    query = (projected[0] + head_wide[0]).astype(jnp.bfloat16).reshape(shape4)
    keys = projected[1].astype(jnp.bfloat16).reshape(shape4)
    values = (projected[2] + head_wide[1]).astype(jnp.bfloat16).reshape(shape4)
    same = segment[:, None, :, None] == segment[:, None, None, :]

    def masked_scores():
        raw = (
            jnp.einsum("pqhe,pkhe->phqk", query, keys, preferred_element_type=jnp.float32)
            * root_scale
        )
        return jnp.where(same, raw, mask_value)

    scores = masked_scores()
    top = jnp.max(scores, -1, keepdims=True)
    log_total = top + jnp.log(jnp.sum(jnp.exp(scores - top), -1, keepdims=True))
    probs = jnp.exp(scores - log_total).astype(jnp.bfloat16)
    mixed = jnp.einsum("phqk,pkhe->pqhe", probs, values, preferred_element_type=jnp.float32)
    mixed = mixed.reshape(rows, half).astype(jnp.bfloat16)
    attended = lax.psum(summation_axes_spec(mixed, out_full, 1, 1), "mp")
    resid = inputs + attended + affine_wide[4]
    normed_two = layer_norm(resid, affine_wide[2], affine_wide[3]).astype(jnp.bfloat16)
    upper = jnp.dot(normed_two, up_full, preferred_element_type=jnp.float32) + inner_wide
    activated, gelu_back = jax.vjp(jax.nn.gelu, upper)
    hidden = activated.astype(jnp.bfloat16)
    lowered = lax.psum(
        summation_axes_spec(hidden, down_full, 1, 1).astype(jnp.bfloat16), "mp"
    ).astype(jnp.float32)
    output = resid + lowered + affine_wide[5]
    slots = pairing.shape[1]
    onehot = (segment[:, None, :] == jnp.arange(slots, dtype=jnp.int32)[None, :, None]).astype(
        jnp.float32
    )
    counts = jnp.sum(onehot, -1)
    divisor = jnp.maximum(counts, 1.0)[..., None]
    pooled = (
        jnp.einsum(
            "pcl,pld->pcd",
            onehot,
            output.reshape(packs, length, width),
            precision=exact_arithmetic_mode,
        )
        / divisor
    )
    flat = pooled.reshape(packs * slots, width)
    caption_wide, normalize_back = jax.vjp(normalize, flat)
    sentence_words = caption_wide.astype(jnp.bfloat16)
    live = (counts > 0).reshape(-1).astype(jnp.float32)
    target = pairing.reshape(-1)
    captions_count = flat.shape[0]
    slot_total = float(captions_count * lax.axis_size("dp"))
    picture_summed = normalize(images.astype(jnp.float32)).astype(jnp.bfloat16)

    def similarity(packed_sequence_slice):
        return sharpness_divisor * summation_axes_spec(sentence_words, packed_sequence_slice, 1, 1)

    score_packed_sequence_slice = lax.all_gather(picture_summed, "dp", axis=0, tiled=True)
    best = jnp.full((captions_count,), mask_value, jnp.float32)
    similarity_grid = similarity(score_packed_sequence_slice)
    new_best = jnp.maximum(best, jnp.max(similarity_grid, 1))
    total = jnp.sum(jnp.exp(similarity_grid - new_best[:, None]), 1)
    column = jnp.arange(score_packed_sequence_slice.shape[0], dtype=jnp.int32)
    hit = target[:, None] == column[None, :]
    positive = jnp.sum(jnp.where(hit, similarity_grid, 0.0), 1)
    best_all, total_all, positive = (new_best, total, positive)
    log_sum = best_all + jnp.log(total_all)
    grad_packed_sequence_slice = lax.all_gather(picture_summed, "dp", axis=0, tiled=True)
    similarity_grid = similarity(grad_packed_sequence_slice)
    column = jnp.arange(grad_packed_sequence_slice.shape[0], dtype=jnp.int32)
    hit = (target[:, None] == column[None, :]).astype(jnp.float32)
    logit_gradient = (
        loss_scale * live[:, None] * (jnp.exp(similarity_grid - log_sum[:, None]) - hit)
    ).astype(jnp.bfloat16)
    sentence_derivative = sharpness_divisor * jnp.dot(
        logit_gradient, grad_packed_sequence_slice, preferred_element_type=jnp.float32
    )
    cross = log_sum - positive
    loss_local = jnp.sum(live * cross)
    loss_total = lax.psum(loss_local, "dp")
    mean_loss = loss_total / slot_total
    (grad_flat,) = normalize_back(sentence_derivative)
    grad_pooled = grad_flat.reshape(packs, slots, width) / divisor
    grad_output = jnp.einsum(
        "pcl,pcd->pld", onehot, grad_pooled, precision=exact_arithmetic_mode
    ).reshape(rows, width)
    grad_output_low = grad_output.astype(jnp.bfloat16)
    down_grad = summation_axes_spec(grad_output_low, hidden, 0, 0)
    grad_hidden = jnp.dot(grad_output_low, down_full, preferred_element_type=jnp.float32)
    (grad_upper,) = gelu_back(grad_hidden)
    grad_upper = grad_upper.astype(jnp.bfloat16)
    inner_grad = jnp.sum(grad_upper.astype(jnp.float32), 0)
    up_grad = summation_axes_spec(normed_two, grad_upper, 0, 0)
    grad_two = lax.psum(
        summation_axes_spec(grad_upper, up_full, 1, 1).astype(jnp.bfloat16), "mp"
    ).astype(jnp.float32)
    _, norm_two_back = jax.vjp(layer_norm, resid, affine_wide[2], affine_wide[3])
    grad_resid_norm, gain_two_grad, shift_two_grad = norm_two_back(grad_two)
    grad_resid = grad_output + grad_resid_norm
    grad_resid_low = grad_resid.astype(jnp.bfloat16)
    out_grad = summation_axes_spec(grad_resid_low, mixed, 0, 0)
    grad_mixed = jnp.dot(grad_resid_low, out_full, preferred_element_type=jnp.float32)
    grad_mixed = grad_mixed.astype(jnp.bfloat16).reshape(shape4)
    probs_wide = jnp.exp(masked_scores() - log_total)
    probs_low = probs_wide.astype(jnp.bfloat16)
    grad_value = jnp.einsum(
        "phqk,pqhe->pkhe", probs_low, grad_mixed, preferred_element_type=jnp.float32
    )
    grad_probs = jnp.einsum(
        "pqhe,pkhe->phqk", grad_mixed, values, preferred_element_type=jnp.float32
    )
    grad_scores = probs_wide * (grad_probs - jnp.sum(probs_wide * grad_probs, -1, keepdims=True))
    grad_scores = grad_scores.astype(jnp.bfloat16)
    grad_query = (
        jnp.einsum("phqk,pkhe->pqhe", grad_scores, keys, preferred_element_type=jnp.float32)
        * root_scale
    )
    grad_key = (
        jnp.einsum("phqk,pqhe->pkhe", grad_scores, query, preferred_element_type=jnp.float32)
        * root_scale
    )
    grad_qkv = (
        jnp.stack([grad_query, grad_key, grad_value]).reshape(3, rows, half).astype(jnp.bfloat16)
    )
    head_grad = jnp.stack(
        [jnp.sum(grad_qkv[0].astype(jnp.float32), 0), jnp.sum(grad_qkv[2].astype(jnp.float32), 0)]
    )
    qkv_grad = jnp.einsum("td,kte->kde", normed_one, grad_qkv, preferred_element_type=jnp.float32)
    grad_one = lax.psum(
        jnp.einsum("kte,kde->td", grad_qkv, qkv_full, preferred_element_type=jnp.float32).astype(
            jnp.bfloat16
        ),
        "mp",
    ).astype(jnp.float32)
    _, norm_one_back = jax.vjp(layer_norm, inputs, affine_wide[0], affine_wide[1])
    grad_input_norm, gain_one_grad, shift_one_grad = norm_one_back(grad_one)
    grad_input = (grad_resid + grad_input_norm).reshape(packs, length, width)
    affine_grad = jnp.stack(
        [
            gain_one_grad,
            shift_one_grad,
            gain_two_grad,
            shift_two_grad,
            jnp.sum(grad_resid, 0),
            jnp.sum(grad_output, 0),
        ]
    )
    qkv_part, out_part, up_part, down_part, affine_part, head_part, inner_part = (
        lax.psum_scatter(qkv_grad, "dp", scatter_dimension=1, tiled=True),
        lax.psum_scatter(out_grad, "dp", scatter_dimension=0, tiled=True),
        lax.psum_scatter(up_grad, "dp", scatter_dimension=0, tiled=True),
        lax.psum_scatter(down_grad, "dp", scatter_dimension=0, tiled=True),
        lax.psum_scatter(affine_grad, "dp", scatter_dimension=1, tiled=True),
        lax.psum_scatter(head_grad, "dp", scatter_dimension=1, tiled=True),
        lax.psum_scatter(inner_grad, "dp", scatter_dimension=0, tiled=True),
    )
    weights = (qkv_weight, out_weight, up_weight, down_weight, affine, head_bias, inner_bias)
    firsts = (qkv_first, out_first, up_first, down_first, affine_first, head_first, inner_first)
    seconds = (
        qkv_second,
        out_second,
        up_second,
        down_second,
        affine_second,
        head_second,
        inner_second,
    )
    grads = (qkv_part, out_part, up_part, down_part, affine_part, head_part, inner_part)
    decays = (weight_decay, weight_decay, weight_decay, weight_decay, 0.0, 0.0, 0.0)
    parts = [
        moments(weights[index], firsts[index], seconds[index], grads[index], decays[index])
        for index in range(7)
    ]
    updates = [packed_sequence_slice[2] for packed_sequence_slice in parts]
    weight_squares = tensor_squares(*weights, float(model_size))
    update_squares = tensor_squares(*updates, float(model_size))
    weight_total, update_total = lax.psum((weight_squares, update_squares), ("dp", "mp"))
    weight_norm = jnp.sqrt(weight_total)
    update_norm = jnp.sqrt(update_total)
    weight_split = split_norms(weight_norm)
    update_split = split_norms(update_norm)
    news = [
        scaled_step(weights[index], updates[index], weight_split[index], update_split[index])
        for index in range(7)
    ]
    return (
        mean_loss,
        grad_input,
        news[0],
        parts[0][0],
        parts[0][1],
        news[1],
        parts[1][0],
        parts[1][1],
        news[2],
        parts[2][0],
        parts[2][1],
        news[3],
        parts[3][0],
        parts[3][1],
        news[4],
        parts[4][0],
        parts[4][1],
        news[5],
        parts[5][0],
        parts[5][1],
        news[6],
        parts[6][0],
        parts[6][1],
        jnp.stack([weight_norm, update_norm]),
    )


def solution(mesh):
    depth = mesh.shape["dp"] // 4
    fits = mesh.shape["mp"] == 2 and mesh.shape["dp"] % 8 == 0 and 768 // mesh.shape["dp"] % 16 == 0
    return jax.shard_map(
        functools.partial(body_near, depth) if fits else body,
        mesh=mesh,
        in_specs=(
            P("dp", None, None),
            P("dp", None),
            P("dp", None),
            P("dp", None),
            P(None, "dp", "mp"),
            P(None, "dp", "mp"),
            P(None, "dp", "mp"),
            P("dp", "mp"),
            P("dp", "mp"),
            P("dp", "mp"),
            P("dp", "mp"),
            P("dp", "mp"),
            P("dp", "mp"),
            P("dp", "mp"),
            P("dp", "mp"),
            P("dp", "mp"),
            P(None, "dp"),
            P(None, "dp"),
            P(None, "dp"),
            P(None, ("mp", "dp")),
            P(None, ("mp", "dp")),
            P(None, ("mp", "dp")),
            P(("mp", "dp")),
            P(("mp", "dp")),
            P(("mp", "dp")),
        ),
        out_specs=(
            P(),
            P("dp", None, None),
            P(None, "dp", "mp"),
            P(None, "dp", "mp"),
            P(None, "dp", "mp"),
            P("dp", "mp"),
            P("dp", "mp"),
            P("dp", "mp"),
            P("dp", "mp"),
            P("dp", "mp"),
            P("dp", "mp"),
            P("dp", "mp"),
            P("dp", "mp"),
            P("dp", "mp"),
            P(None, "dp"),
            P(None, "dp"),
            P(None, "dp"),
            P(None, ("mp", "dp")),
            P(None, ("mp", "dp")),
            P(None, ("mp", "dp")),
            P(("mp", "dp")),
            P(("mp", "dp")),
            P(("mp", "dp")),
            P(),
        ),
        check_vma=False,
    )
```

```python
import functools
import heapq

import jax
import jax.numpy as jnp
from jax import lax
from jax.experimental import pallas as pl
from jax.experimental.pallas import tpu as pltpu
from jax.sharding import PartitionSpec as P

HD = 64
STEP = 10


norm_epsilon = 1e-06
mask_value = -1000000000.0
sharpness_divisor = 50.0
loss_scale = 128.0
beta_first = 0.9
beta_second = 0.999
adam_epsilon = 1e-06
weight_decay = 0.01
learning_rate = 0.5
exact_arithmetic_mode = lax.Precision.HIGHEST


def layer_norm(values, gain, shift):
    center = values - jnp.mean(values, -1, keepdims=True)
    spread = jnp.mean(center * center, -1, keepdims=True)
    return center * lax.rsqrt(spread + norm_epsilon) * gain + shift


def normalize(values):
    return values * lax.rsqrt(jnp.sum(values * values, -1, keepdims=True) + norm_epsilon)


def summation_axes_spec(left, right, left_dim, right_dim):
    return lax.dot_general(
        left, right, (((left_dim,), (right_dim,)), ((), ())), preferred_element_type=jnp.float32
    )


def moments(weight, first, second, grad, decay):
    first_new = beta_first * first + (1.0 - beta_first) * grad
    second_new = beta_second * second + (1.0 - beta_second) * grad * grad
    first_hat = first_new / (1.0 - beta_first**STEP)
    second_hat = second_new / (1.0 - beta_second**STEP)
    update = first_hat / (jnp.sqrt(second_hat) + adam_epsilon) + decay * weight
    return (first_new, second_new, update)


def tensor_squares(qkv, out, upper, lower, affine, head, inner, replicas):
    return jnp.concatenate(
        [
            jnp.sum(qkv * qkv, (1, 2)),
            jnp.sum(out * out)[None],
            jnp.sum(upper * upper)[None],
            jnp.sum(lower * lower)[None],
            jnp.sum(affine * affine, 1) / replicas,
            jnp.sum(head * head, 1),
            jnp.sum(inner * inner)[None],
        ]
    )


def split_norms(norms):
    return (
        norms[0:3].reshape(3, 1, 1),
        norms[3],
        norms[4],
        norms[5],
        norms[6:12].reshape(6, 1),
        norms[12:14].reshape(2, 1),
        norms[14],
    )


def scaled_step(weight, update, weight_norm, update_norm):
    return weight - learning_rate * weight_norm / update_norm * update


MESH = pl.DeviceIdType.MESH
f32 = jnp.float32
bf16 = jnp.bfloat16
NROWS, SMALL, FAR = 32, 4.0, 8.0
PACE = (3.4, 2.2, 6.0, 5.0, 6.0)
WAYS = "xxxxxxxxxxxx"


class Place:
    def __init__(self, depth):
        self.depth = depth
        dp = lax.axis_index("dp")
        self.dp = dp
        self.x = lax.axis_index("mp")
        self.z, self.y, self.c = dp // 4, (dp // 2) % 2, dp % 2

    def at(self, z, y, c, x):
        return ((z * 2 + y) * 2 + c, x)

    def over_x(self):
        return self.at(self.z, self.y, self.c, 1 - self.x)

    def over_y(self):
        return self.at(self.z, 1 - self.y, self.c, self.x)

    def over_c(self):
        return self.at(self.z, self.y, 1 - self.c, self.x)

    def over_z(self, k):
        return self.at(lax.rem(self.z + k, self.depth), self.y, self.c, self.x)

    def in_plane(self, d):
        return self.at(self.z, 1 - self.y if d & 4 else self.y, 1 - self.c if d & 2 else self.c, 1 - self.x if d & 1 else self.x)

    def greet(self):
        sem = pltpu.get_barrier_semaphore()
        for peer in [self.in_plane(d) for d in range(1, 8)] + [self.over_z(k) for k in range(1, self.depth)]:
            pl.semaphore_signal(sem, inc=1, device_id=peer, device_id_type=MESH)

    def meet(self):
        pl.semaphore_wait(pltpu.get_barrier_semaphore(), 7 + self.depth - 1)


class Wire:
    def __init__(self, send, recv):
        self.send, self.recv, self.used, self.open = send, recv, 0, []

    def start(self, src, dst, device):
        i = self.used
        self.used += 1
        copy = pltpu.make_async_remote_copy(
            src_ref=src, dst_ref=dst, send_sem=self.send.at[i], recv_sem=self.recv.at[i], device_id=device, device_id_type=MESH
        )
        copy.start()
        self.open.append(copy)
        return copy

    def close(self):
        for copy in self.open:
            copy.wait_send()
        self.open = []


def arrive(copies):
    for copy in copies:
        copy.wait_recv()


class Timeline:
    def __init__(self):
        self.steps, self.count, self.now = [], 0, 0.0

    def add(self, time, step):
        heapq.heappush(self.steps, (time, self.count, step))
        self.count += 1

    def until(self, time):
        while self.steps and self.steps[0][0] <= time:
            at, _, step = heapq.heappop(self.steps)
            step(at)
        self.now = max(self.now, time)

    def tick(self, span):
        self.until(self.now + span)

    def drain(self):
        while self.steps:
            self.until(self.steps[0][0])


class Sheet:
    def __init__(self, full, u):
        self.full, self.u, self.half = full, u, full.shape[-1] // 2

    def part(self, z, y, c, x=None):
        lanes = pl.ds(0, 2 * self.half) if x is None else pl.ds(pl.multiple_of(x * self.half, 128), self.half)
        return self.full.at[self.u, z, y, c, :, lanes]


class Gather:
    def __init__(self, place, wire, line, items, pace):
        self.p, self.wire, self.line, self.items = place, wire, line, items
        self.flight, self.at = {}, []
        second, far_rate, to_one, rate, to_two, to_core, to_whole = pace
        one = -rate
        for i in range(len(items)):
            far = second + far_rate * (i - 1) if i else 0.0
            one = max(far + to_one, one + rate)
            two = one + to_two
            core = two + to_core
            self.at.append(core + to_whole)
            times = (far, one, two, core, core + to_whole)
            for time, step in zip(times, (self.far, self.one, self.two, self.core, self.whole)):
                line.add(time, lambda at, step=step, i=i: step(i))

    def far(self, i):
        p, it = self.p, self.items[i]
        mine = it.part(p.z, p.y, p.c, p.x)
        self.flight["z", i] = [self.wire.start(mine, mine, p.over_z(k)) for k in range(1, p.depth)]

    def one(self, i):
        p, it, h = self.p, self.items[i], self.p.depth // 2
        arrive(self.flight["z", i])
        a = it.part(pl.ds(0, h), p.y, p.c, p.x)
        b = it.part(pl.ds(h, p.depth - h), p.y, p.c, p.x)
        self.flight["1", i] = [self.wire.start(a, a, p.over_x()), self.wire.start(b, b, p.over_y())]

    def two(self, i):
        p, it, h = self.p, self.items[i], self.p.depth // 2
        first, second = self.flight["1", i]
        a = it.part(pl.ds(0, h), p.y, p.c)
        b = it.part(pl.ds(h, p.depth - h), slice(None), p.c, p.x)
        first.wait_recv()
        to_y = self.wire.start(a, a, p.over_y())
        second.wait_recv()
        self.flight["2", i] = [to_y, self.wire.start(b, b, p.over_x())]

    def core(self, i):
        p, it = self.p, self.items[i]
        arrive(self.flight["2", i])
        r = it.part(slice(None), slice(None), p.c)
        self.flight["c", i] = [self.wire.start(r, r, p.over_c())]

    def whole(self, i):
        arrive(self.flight["c", i])

    def until(self, i):
        self.line.until(self.at[i])


def add_blocks(dst, src, count):
    for i in range(count):
        (d, at), (s, of) = dst(i), src(i)
        d[at] = d[at] + s[of]


class Reduce:
    def __init__(self, place, wire, line, order, ways, pace, free, part, from_core, one_a, one_b, two_a, two_b, from_z, total, use):
        self.p, self.wire, self.line, self.order, self.ways, self.free, self.use = place, wire, line, order, ways, free, use
        self.rate, self.to_one, self.to_two, self.to_far, self.to_last = pace
        self.next_one, self.count, self.takes = 0.0, 0, []
        self.part, self.from_core, self.one_a, self.one_b = part, from_core, one_a, one_b
        self.two_a, self.two_b, self.from_z, self.total = two_a, two_b, from_z, total
        self.h = place.depth // 2
        self.half = part.shape[-1] // 2
        self.slots = from_core.shape[0]
        self.flight = {}

    def lanes(self, x):
        return pl.ds(x * self.half if isinstance(x, int) else pl.multiple_of(x * self.half, 128), self.half)

    def core(self, i):
        p, u = self.p, self.order[i]
        if i >= self.slots:
            pl.semaphore_wait(self.free, 1)
        self.flight["c", i] = [self.wire.start(self.part.at[u, :, :, 1 - p.c], self.from_core.at[i % self.slots], p.over_c())]

    def take(self, i):
        p, u, Z, part = self.p, self.order[i], self.p.depth, self.part
        arrive(self.flight["c", i])
        add_blocks(
            lambda j: (part, (u, j // 2, j % 2, p.c)),
            lambda j: (self.from_core, (i % self.slots, j // 2, j % 2)), 2 * Z,
        )
        if i + self.slots < len(self.order):
            pl.semaphore_signal(self.free, inc=1, device_id=p.over_c(), device_id_type=MESH)

    def one(self, i):
        p, u, h, Z, part, way = self.p, self.order[i], self.h, self.p.depth, self.part, self.ways[i]
        start, flight = self.wire.start, []
        if way == "z":
            z1, z2, z3 = (lax.rem(p.z + k, Z) for k in (1, 2, 3))
            flight.append(start(part.at[u, z1, :, p.c], self.one_b.at[u], p.over_z(1)))
            for m in range(2):
                flight.append(start(part.at[u, z2, :, p.c, :, self.lanes(m)], self.one_a.at[u, :, m], p.over_z(2)))
                flight.append(start(part.at[u, z3, :, p.c, :, self.lanes(m)], (self.two_a, self.two_b)[m].at[u], p.over_z(3)))
        else:
            if way == "y":
                for m in range(2):
                    flight.append(start(part.at[u, pl.ds(0, h), 1 - p.y, p.c, :, self.lanes(m)], self.one_a.at[u, :, m], p.over_y()))
            else:
                flight.append(start(part.at[u, pl.ds(0, h), :, p.c, :, self.lanes(1 - p.x)], self.one_a.at[u], p.over_x()))
            flight.append(start(part.at[u, pl.ds(h, Z - h), 1 - p.y, p.c], self.one_b.at[u], p.over_y()))
        self.flight["1", i] = flight

    def two(self, i):
        p, u, h, Z, part, way = self.p, self.order[i], self.h, self.p.depth, self.part, self.ways[i]
        if way == "z":
            return
        *first, second = self.flight["1", i]
        arrive(first)
        mine = self.lanes(p.x)
        if way == "y":
            for m in range(2):
                add_blocks(
                    lambda j: (part, (u, j, p.y, p.c, slice(None), self.lanes(m))), lambda j: (self.one_a, (u, j, m)), h
                )
            a, to_a = part.at[u, pl.ds(0, h), p.y, p.c, :, self.lanes(1 - p.x)], p.over_x()
        else:
            add_blocks(lambda j: (part, (u, j // 2, j % 2, p.c, slice(None), mine)), lambda j: (self.one_a, (u, j // 2, j % 2)), 2 * h)
            a, to_a = part.at[u, pl.ds(0, h), 1 - p.y, p.c, :, mine], p.over_y()
        sent = self.wire.start(a, self.two_a.at[u], to_a)
        second.wait_recv()
        add_blocks(lambda j: (part, (u, h + j, p.y, p.c)), lambda j: (self.one_b, (u, j)), Z - h)
        self.flight["2", i] = [
            sent,
            self.wire.start(part.at[u, pl.ds(h, Z - h), p.y, p.c, :, self.lanes(1 - p.x)], self.two_b.at[u], p.over_x()),
        ]

    def far(self, i):
        p, u, h, Z, part, way = self.p, self.order[i], self.h, self.p.depth, self.part, self.ways[i]
        mine = self.lanes(p.x)
        if way == "z":
            arrive(self.flight["1", i])
            for y in range(2):
                t = part[u, p.z, y, p.c].astype(f32) + self.one_b[u, y].astype(f32)
                left = t[:, : self.half] + self.one_a[u, y, 0].astype(f32) + self.two_a[u, y].astype(f32)
                right = t[:, self.half :] + self.one_a[u, y, 1].astype(f32) + self.two_b[u, y].astype(f32)
                part[u, p.z, y, p.c] = jnp.concatenate([left, right], 1).astype(part.dtype)
            others = ((p.y, 1 - p.x, 1), (1 - p.y, p.x, 4), (1 - p.y, 1 - p.x, 5))
            self.flight["z", i] = [
                self.wire.start(part.at[u, p.z, y, p.c, :, self.lanes(x)], self.from_z.at[k, u], p.in_plane(d))
                for k, (y, x, d) in enumerate(others)
            ]
            return
        first, second = self.flight["2", i]
        first.wait_recv()
        add_blocks(lambda j: (part, (u, j, p.y, p.c, slice(None), mine)), lambda j: (self.two_a, (u, j)), h)
        second.wait_recv()
        add_blocks(lambda j: (part, (u, h + j, p.y, p.c, slice(None), mine)), lambda j: (self.two_b, (u, j)), Z - h)
        self.flight["z", i] = [
            self.wire.start(part.at[u, lax.rem(p.z + k, Z), p.y, p.c, :, mine], self.from_z.at[k - 1, u], p.over_z(k))
            for k in range(1, Z)
        ]

    def last(self, i):
        p, u = self.p, self.order[i]
        arrive(self.flight["z", i])
        t = self.part[u, p.z, p.y, p.c, :, self.lanes(p.x)].astype(f32)
        for j in range(p.depth - 1):
            t = t + self.from_z[j, u].astype(f32)
        self.total[u] = t
        self.use(u, t)

    def step(self):
        i, line = self.count, self.line
        self.count += 1
        if i >= self.slots:
            line.until(self.takes[i - self.slots])
        self.core(i)
        time = line.now + self.to_one
        self.takes.append(time)
        line.add(time, lambda at: self.take(i))
        time = max(time, self.next_one)
        self.next_one = time + self.rate
        far = self.to_far + FAR if self.ways[i] == "z" else self.to_far
        for span, step in ((0.0, self.one), (self.to_two, self.two), (far, self.far), (self.to_last, self.last)):
            time += span
            line.add(time, lambda at, step=step: step(i))


class SumAll:
    def __init__(self, place, wire, own, room):
        self.p, self.wire, self.own, self.room = place, wire, own, room
        self.stage = 0

    def start(self):
        p = self.p
        if self.stage < 3:
            device = (p.over_c, p.over_x, p.over_y)[self.stage]()
            self.flight = [self.wire.start(self.own, self.room.at[self.stage], device)]
        else:
            self.flight = [self.wire.start(self.own, self.room.at[3 + p.z], p.over_z(k)) for k in range(1, p.depth)]

    def finish(self):
        p = self.p
        arrive(self.flight)
        for copy in self.flight:
            copy.wait_send()
        self.wire.open = [c for c in self.wire.open if all(c is not f for f in self.flight)]
        if self.stage < 3:
            self.own[...] = self.own[...] + self.room[self.stage]
        else:
            self.room[3 + p.z] = self.own[...]
            t = self.room[3]
            for z in range(1, p.depth):
                t = t + self.room[3 + z]
            self.own[...] = t
        self.stage += 1

    def run(self):
        while self.stage < 4:
            self.start()
            self.finish()


class SumSoon:
    def __init__(self, place, wire, own, plane, line):
        p = place
        slot = (p.y * 2 + p.c) * 2 + p.x
        plane[slot] = own[...]
        arrive([wire.start(own, plane.at[slot], p.in_plane(d)) for d in range(1, 8)])
        value = plane[0]
        for d in range(1, 8):
            value = value + plane[d]
        line[p.z] = value
        arrive([wire.start(line.at[p.z], line.at[p.z], p.over_z(k)) for k in range(1, p.depth)])
        value = line[0]
        for z in range(1, p.depth):
            value = value + line[z]
        self.value = value


class Pictures:
    def __init__(self, place, wire, line, full, size, pace):
        self.p, self.wire, self.full = place, wire, full
        mine = full.at[place.z, place.y, place.c]
        self.flight = [wire.start(mine, mine, place.over_y())]
        self.pieces = [(k, at, size) for at in range(0, full.shape[3], size) for k in range(1, place.depth)]
        self.sent = 0
        first, rate, to_core, to_whole = pace
        for i in range(len(self.pieces)):
            line.add(first + rate * i, lambda at: self.step())
        core = first + rate * len(self.pieces) + to_core
        self.at = core + to_whole
        line.add(core, lambda at: self.core())
        line.add(self.at, lambda at: self.whole())

    def step(self):
        p = self.p
        if self.sent == 0:
            arrive(self.flight)
            self.flight = []
        k, at, size = self.pieces[self.sent]
        mine = self.full.at[p.z, :, p.c, pl.ds(at, size)]
        self.flight.append(self.wire.start(mine, mine, p.over_z(k)))
        self.sent += 1

    def core(self):
        arrive(self.flight)
        r = self.full.at[:, :, self.p.c]
        self.flight = [self.wire.start(r, r, self.p.over_c())]

    def whole(self):
        arrive(self.flight)


def dot(a, b, left=1, right=0):
    return lax.dot_general(a, b, (((left,), (right,)), ((), ())), preferred_element_type=f32)


def row_loop(count, size, f, start=0):
    def step(i, carry):
        f(pl.ds(pl.multiple_of(start + i * size, size), size))
        return carry

    lax.fori_loop(0, count // size, step, 0)


def center_scale(x):
    center = x - jnp.mean(x, -1, keepdims=True)
    return center, lax.rsqrt(jnp.mean(center * center, -1, keepdims=True) + norm_epsilon)


def three(x):
    hi = x.astype(bf16)
    rest = x - hi.astype(f32)
    mid = rest.astype(bf16)
    return hi, mid, (rest - mid.astype(f32)).astype(bf16)


def fold(x):
    return jnp.sum(x.reshape(x.shape[0] // 8, 8, x.shape[1]), 0)


def placing(n, at, lanes):
    spot = lax.broadcasted_iota(jnp.int32, (n, lanes), 1) == lax.broadcasted_iota(jnp.int32, (n, lanes), 0) + at
    return jnp.where(spot, 1.0, 0.0).astype(bf16)


def picked(a, at, n):
    spot = placing(n, at, a.shape[1])
    return sum(dot(term, spot, 1, 1) for term in three(a))


def row_of(a, at):
    rows = lax.broadcasted_iota(jnp.int32, a.shape, 0) == at
    return jnp.sum(jnp.where(rows, a, jnp.zeros_like(a)), 0, keepdims=True)


def block_kernel(
    depth,
    tokens, segment, pairing, images, qkv_weight, out_weight, up_weight, down_weight, affine, head_bias, inner_bias,
    qkv_first, qkv_second, out_first, out_second, up_first, up_second, down_first, down_second,
    affine_first, affine_second, head_first, head_second, inner_first, inner_second,
    total, small_grad, norms, grad_low,
    full, pictures, part, from_core, one_a, one_b, two_a, two_b, from_z,
    tok, normed_one, qkv, mixed, resid, normed_two, hidden, slope, stream, grad_mixed, acc, low,
    probs, same, wide, sums, room, room2, folds, cap,
    old_qkv, old_out, old_up, old_down, squares, tile_sums, plane, line,
    send, recv, free, local, local_old,
):
    place = Place(depth)
    place.greet()
    x, dp = place.x, place.dp
    rows, width = tok.shape
    packs, length = 2, rows // 2
    half = qkv_weight.shape[2]
    units = full.shape[0]
    share = full.shape[4]
    blocks = up_weight.shape[1] // half
    up0, down0 = 4, 4 + blocks

    token_copies = [
        pltpu.make_async_copy(tokens.at[packs * x + p], tok.at[pl.ds(p * length, length)], local.at[p]) for p in range(packs)
    ]
    pairs_old = ((qkv_first, qkv_second, old_qkv), (out_first, out_second, old_out), (up_first, up_second, old_up), (down_first, down_second, old_down))
    old_copies = []
    for i, (one, two, kept) in enumerate(pairs_old):
        old_copies += [pltpu.make_async_copy(one, kept.at[0], local_old.at[2 * i]), pltpu.make_async_copy(two, kept.at[1], local_old.at[2 * i + 1])]
    for copy in token_copies + old_copies:
        copy.start()

    mine_lanes = pl.ds(pl.multiple_of(x * half, 128), half)

    def keep(u, value):
        full[u, place.z, place.y, place.c, :, mine_lanes] = value.astype(bf16)

    for k in range(3):
        keep(k, qkv_weight[k])
    keep(3, out_weight[...])
    for j in range(blocks):
        keep(up0 + j, up_weight[:, j * half : (j + 1) * half])
        keep(down0 + j, down_weight[:, j * half : (j + 1) * half])
    pictures[place.z, place.y, place.c] = normalize(images[...].astype(f32)).astype(bf16)

    place.meet()
    wire = Wire(send, recv)
    moves = Timeline()
    tick = moves.tick
    scenes = Pictures(place, wire, moves, pictures, 16, (24.0, 2.0, 3.0, 3.0))
    gather = Gather(place, wire, moves, [Sheet(full, u) for u in range(units)], (2.5, 3.5, 2.6, 3.8, 3.9, 8.0, 6.0))
    ready = gather.until
    tick(0.0)

    owner = x * (4 * depth) + dp
    n_affine, n_head, n_inner = affine.shape[1], head_bias.shape[1], inner_bias.shape[1]
    first = jnp.where(x == 0, 1.0, 0.0)
    inner_rows = 2 * blocks * half // width
    inner_at, inner_row = (owner * n_inner) % width, (owner * n_inner) // width
    wide[...] = jnp.zeros_like(wide)
    wide[0:6] = dot(affine[...].astype(bf16), placing(n_affine, dp * n_affine, width)) * first
    wide[6:8] = dot(head_bias[...].astype(bf16), placing(n_head, owner * n_head, width))
    inner_wide = dot(inner_bias[...].astype(bf16), placing(n_inner, inner_at, width))
    at_row = lax.broadcasted_iota(jnp.int32, (inner_rows, width), 0) == inner_row
    wide[8 : 8 + inner_rows] = jnp.where(at_row, jnp.broadcast_to(inner_wide, (inner_rows, width)), 0.0)
    spread = SumAll(place, wire, wide, room)
    spread.start()

    slots = pairing.shape[1]
    tile, window = 64, 128
    starts = [min(max(t * tile - (window - tile) // 2, 0), length - window) for t in range(length // tile)]
    onehots = []
    for p in range(packs):
        seg = jnp.broadcast_to(row_of(segment[...], packs * x + p), (slots, length))
        onehot = jnp.where(seg == lax.broadcasted_iota(jnp.int32, (slots, length), 0), 1.0, 0.0)
        onehots.append(onehot)
        low_hot = onehot.astype(bf16)
        both = acc.at[pl.ds(0, length), pl.ds(0, length)]
        both[...] = dot(low_hot, low_hot, 0, 0)
        for t, w in enumerate(starts):
            shared = dot(both[pl.ds(t * tile, tile)].astype(bf16), placing(window, w, length), 1, 1)
            same[p, t, 0:tile] = shared
            same[p, t, tile : 2 * tile] = shared
        tick(1.5)
        if p == 0:
            spread.finish()
            spread.start()
    while spread.stage < 4:
        tick(2.0)
        spread.finish()
        if spread.stage < 4:
            spread.start()

    for copy in token_copies:
        copy.wait()

    def norm_one(r):
        center, scale = center_scale(tok[r].astype(f32))
        normed_one[r] = (center * scale * wide[0:1] + wide[1:2]).astype(bf16)

    row_loop(rows, NROWS, norm_one)
    tick(3.0)

    def unit(u):
        return full[u].reshape(width, width)

    chunk = 256

    def unit_lanes(u, j):
        return full[u, :, :, :, :, pl.ds(j * chunk, chunk)].reshape(width, chunk)

    for k in range(3):
        ready(k)
        for j in range(width // chunk):
            lanes = pl.ds(j * chunk, chunk)
            value = dot(normed_one[...], unit_lanes(k, j))
            if k != 1:
                row = 6 if k == 0 else 7
                value = value + wide[row : row + 1, lanes]
            qkv[k, :, lanes] = value.astype(bf16)
        tick(1.0)

    root_scale = HD**-0.5
    pair = 2 * HD
    pairs = width // pair
    lower = lax.broadcasted_iota(jnp.int32, (tile, pair), 1) < HD

    def doubled(a):
        zero = jnp.zeros_like(a)
        return jnp.concatenate([jnp.where(lower, a, zero), jnp.where(lower, zero, a)], 0)

    def joined(a):
        return jnp.where(lower, a[:tile], a[tile:])

    def attend(p, g):
        lanes = pl.ds(pl.multiple_of(g * pair, pair), pair)
        span = pl.ds(p * length, length)
        query, keys, values = qkv[0, span, lanes], qkv[1, span, lanes], qkv[2, span, lanes]
        found, weights = [], []
        for t, w in enumerate(starts):
            scores = dot(doubled(query[t * tile : (t + 1) * tile]), keys[w : w + window], 1, 1) * root_scale
            scores = jnp.where(same[p, t] > 0.5, scores, mask_value)
            e = jnp.exp(scores - jnp.max(scores, -1, keepdims=True))
            prob = (e * (1.0 / jnp.sum(e, -1, keepdims=True))).astype(bf16)
            weights.append(prob)
            found.append(joined(dot(prob, values[w : w + window])).astype(bf16))
        for t in range(len(starts)):
            probs[p, g, t] = weights[t]
        mixed[span, lanes] = jnp.concatenate(found, 0)

    def each_pair(f, p, some):
        def step(g, carry):
            f(p, g)
            return carry

        lax.fori_loop(some[0], some[1], step, 0, unroll=some[1] - some[0])

    for p in range(packs):
        for some in ((0, pairs // 2), (pairs // 2, pairs)):
            each_pair(attend, p, some)
            tick(1.5)

    ready(3)
    acc[...] = dot(mixed[...], unit(3), 1, 1)
    tick(1.0)

    def norm_two(r):
        value = tok[r].astype(f32) + acc[r] + wide[4:5]
        resid[r] = value
        center, scale = center_scale(value)
        normed_two[r] = (center * scale * wide[2:3] + wide[3:4]).astype(bf16)
        stream[r] = value + wide[5:6]

    row_loop(rows, NROWS, norm_two)
    tick(3.0)

    def inner_lanes(j):
        at = j * half
        return ((8 + at // width, at % width), (8 + (blocks * half + at) // width, (blocks * half + at) % width))

    curve = (2.0 / jnp.pi) ** 0.5
    for j in range(blocks):
        ready(up0 + j)
        bias = jnp.concatenate([wide[row : row + 1, lane : lane + half] for row, lane in inner_lanes(j)], 1)
        for k in range(width // chunk):
            lanes = pl.ds(k * chunk, chunk)
            acc[:, lanes] = dot(normed_two[...], unit_lanes(up0 + j, k))

        def activate(r, j=j, bias=bias):
            u = acc[r] + bias
            square = u * u
            t = jnp.tanh(curve * (u + 0.044715 * (square * u)))
            hidden[j, r] = (0.5 * u * (1.0 + t)).astype(bf16)
            slope[j, r] = (0.5 * (1.0 + t) + 0.5 * u * (1.0 - t * t) * (curve * (1.0 + 3.0 * 0.044715 * square))).astype(bf16)

        row_loop(rows, 16, activate)
        tick(2.5)

    for j in range(blocks):
        ready(down0 + j)
        stream[...] += dot(hidden[j], unit(down0 + j), 1, 1)
    moves.drain()

    count_rows, target_rows = [], []
    for p in range(packs):
        count = jnp.sum(onehots[p], 1, keepdims=True)
        hot = onehots[p].astype(bf16)
        hi, mid, lo = three(stream[pl.ds(p * length, length)])
        pooled = dot(hot, hi) + dot(hot, mid) + dot(hot, lo)
        cap[pl.ds(p * slots, slots)] = pooled / jnp.maximum(count, 1.0)
        count_rows.append(count)
        names = jnp.broadcast_to(row_of(pairing[...], packs * x + p), (slots, slots)).astype(f32)
        diagonal = lax.broadcasted_iota(jnp.int32, (slots, slots), 0) == lax.broadcasted_iota(jnp.int32, (slots, slots), 1)
        target_rows.append(jnp.sum(jnp.where(diagonal, names, 0.0), 1, keepdims=True))
    counts = jnp.concatenate(count_rows, 0)
    target = jnp.concatenate(target_rows, 0)
    live = jnp.where(counts > 0.0, 1.0, 0.0)
    pooled = cap[...]
    radius = lax.rsqrt(jnp.sum(pooled * pooled, -1, keepdims=True) + norm_epsilon)
    caption = (pooled * radius).astype(bf16)
    all_images = pictures[...].reshape(-1, width)
    logits = sharpness_divisor * dot(caption, all_images, 1, 1)
    hit = lax.broadcasted_iota(jnp.int32, logits.shape, 1).astype(f32) == target
    best = jnp.max(logits, -1, keepdims=True)
    e = jnp.exp(logits - best)
    sum_e = jnp.sum(e, -1, keepdims=True)
    positive = jnp.sum(jnp.where(hit, logits, 0.0), -1, keepdims=True)
    cross = best + jnp.log(sum_e) - positive
    loss = jnp.sum(live * cross, 0, keepdims=True)
    grad_logits = (loss_scale * live * (e * (1.0 / sum_e) - jnp.where(hit, 1.0, 0.0))).astype(bf16)
    grad_caption = sharpness_divisor * dot(grad_logits, all_images)
    inner = jnp.sum(pooled * grad_caption, -1, keepdims=True)
    grad_pooled = radius * grad_caption - (radius * radius * radius) * inner * pooled
    grad_pooled = grad_pooled / jnp.maximum(counts, 1.0)
    folds[...] = jnp.zeros_like(folds)
    for p in range(packs):
        hot = onehots[p].astype(bf16)
        hi, mid, lo = three(grad_pooled[p * slots : (p + 1) * slots])
        stream[pl.ds(p * length, length)] = dot(hot, hi, 0, 0) + dot(hot, mid, 0, 0) + dot(hot, lo, 0, 0)

    def lower_stream(r):
        value = stream[r]
        low[r] = value.astype(bf16)
        folds[5] += fold(value)

    row_loop(rows, 32, lower_stream)

    squares[...] = jnp.zeros_like(squares)
    for copy in old_copies:
        copy.wait()

    def lanes_folded(a):
        a = fold(a)
        return sum(a[:, i * 128 : (i + 1) * 128] for i in range(a.shape[1] // 128))

    def use(u, grad):
        if u < 3:
            weight, one, two, row = qkv_weight[u], old_qkv[0, u], old_qkv[1, u], u
        elif u == 3:
            weight, one, two, row = out_weight[...], old_out[0], old_out[1], 3
        else:
            row = 4 if u < down0 else 5
            at = (u - up0) % blocks * half
            weights, kept = (up_weight, old_up) if row == 4 else (down_weight, old_down)
            weight, one, two = weights[:, at : at + half], kept[0, :, at : at + half], kept[1, :, at : at + half]
        update = moments(weight, one, two, grad, weight_decay)[2]
        squares[0, row] += lanes_folded(weight * weight)
        squares[1, row] += lanes_folded(update * update)

    order = [down0 + j for j in range(blocks)] + [up0 + j for j in range(blocks)] + [3, 0, 1, 2]
    reduce = Reduce(place, wire, moves, order, WAYS if depth == 4 and len(order) == len(WAYS) else "x" * len(order), PACE, free, part, from_core, one_a, one_b, two_a, two_b, from_z, total, use)

    def weight_grad(u, left, right):
        for j in range(width // chunk):
            lanes = pl.ds(j * chunk, chunk)
            value = dot(left, right(lanes), 0, 0).astype(bf16)
            part[u, :, :, :, :, lanes] = value.reshape(depth, 2, 2, share, chunk)
        tick(0.7)
        reduce.step()

    sums[...] = jnp.zeros_like(sums)
    for j in range(blocks):
        weight_grad(down0 + j, low[...], lambda lanes, j=j: hidden[j, :, lanes])
        for k in range(width // chunk):
            lanes = pl.ds(k * chunk, chunk)
            acc[:, lanes] = dot(low[...], unit_lanes(down0 + j, k))

        def upper_back(r, j=j):
            value = (acc[r] * slope[j, r].astype(f32)).astype(bf16)
            hidden[j, r] = value
            folds[6] += fold(value.astype(f32))

        folds[6] = jnp.zeros_like(folds[6])
        row_loop(rows, 32, upper_back)
        tick(1.2)
        inner_sum = jnp.sum(folds[6], 0, keepdims=True)
        for i, (row, lane) in enumerate(inner_lanes(j)):
            sums[row : row + 1, lane : lane + half] = inner_sum[:, i * half : (i + 1) * half]

    for j in range(blocks):
        weight_grad(up0 + j, normed_two[...], lambda lanes, j=j: hidden[j, :, lanes])
        value = dot(hidden[j], unit(up0 + j), 1, 1)
        if j == 0:
            acc[...] = value
        else:
            acc[...] += value
        tick(0.7)

    def norm_two_back(r):
        center, scale = center_scale(resid[r])
        hat = center * scale
        grad = acc[r]
        weighted = grad * wide[2:3]
        value = stream[r] + scale * (
            weighted - jnp.mean(weighted, -1, keepdims=True) - hat * jnp.mean(weighted * hat, -1, keepdims=True)
        )
        stream[r] = value
        low[r] = value.astype(bf16)
        folds[2] += fold(grad * hat)
        folds[3] += fold(grad)
        folds[4] += fold(value)

    row_loop(rows, NROWS, norm_two_back)
    tick(4.0)
    weight_grad(3, low[...], lambda lanes: mixed[:, lanes])
    for k in range(width // chunk):
        lanes = pl.ds(k * chunk, chunk)
        grad_mixed[:, lanes] = dot(low[...], unit_lanes(3, k)).astype(bf16)
    tick(0.7)

    def overlaid(pieces):
        step = 32
        found = []
        for at in range(0, length, step):
            found.append(sum(piece[at - w : at - w + step] for w, piece in zip(starts, pieces) if w <= at < w + window))
        return jnp.concatenate(found, 0)

    def attend_back(p, g):
        lanes = pl.ds(pl.multiple_of(g * pair, pair), pair)
        span = pl.ds(p * length, length)
        query, keys, values, grads = qkv[0, span, lanes], qkv[1, span, lanes], qkv[2, span, lanes], grad_mixed[span, lanes]
        of_query, of_keys, of_values = [], [], []
        for t, w in enumerate(starts):
            some = doubled(query[t * tile : (t + 1) * tile])
            grad = doubled(grads[t * tile : (t + 1) * tile])
            prob = probs[p, g, t]
            prob_wide = prob.astype(f32)
            grad_prob = dot(grad, values[w : w + window], 1, 1)
            grad_score = prob_wide * (grad_prob - jnp.sum(prob_wide * grad_prob, -1, keepdims=True))
            grad_score = grad_score.astype(bf16)
            of_keys.append(dot(grad_score, some, 0, 0))
            of_values.append(dot(prob, grad, 0, 0))
            of_query.append((joined(dot(grad_score, keys[w : w + window])) * root_scale).astype(bf16))
        qkv[0, span, lanes] = jnp.concatenate(of_query, 0)
        qkv[1, span, lanes] = (overlaid(of_keys) * root_scale).astype(bf16)
        qkv[2, span, lanes] = overlaid(of_values).astype(bf16)

    for p in range(packs):
        for some in ((0, pairs // 2), (pairs // 2, pairs)):
            each_pair(attend_back, p, some)
            tick(3.2)

    for k in range(3):
        value = dot(qkv[k], unit(k), 1, 1)
        if k == 0:
            acc[...] = value
        else:
            acc[...] += value
    tick(2.0)

    def norm_one_back(r):
        center, scale = center_scale(tok[r].astype(f32))
        hat = center * scale
        grad = acc[r]
        weighted = grad * wide[0:1]
        value = stream[r] + scale * (
            weighted - jnp.mean(weighted, -1, keepdims=True) - hat * jnp.mean(weighted * hat, -1, keepdims=True)
        )
        low[r] = value.astype(bf16)
        folds[0] += fold(grad * hat)
        folds[1] += fold(grad)

    swaps, outs = [], []
    for p in range(packs):
        row_loop(length, NROWS, norm_one_back, p * length)
        mine, there = low.at[pl.ds(p * length, length)], grad_low.at[packs * x + p]
        swaps.append(wire.start(mine, there, place.over_x()))
        outs.append(pltpu.make_async_copy(mine, there, local.at[p]))
        outs[-1].start()
        tick(2.3)

    for k in range(3):
        weight_grad(k, normed_one[...], lambda lanes, k=k: qkv[k, :, lanes])
        tick(0.3)

    def head_sums(r):
        folds[7] += fold(qkv[0, r].astype(f32))
        folds[8] += fold(qkv[2, r].astype(f32))

    row_loop(rows, 32, head_sums)
    for k, row in ((0, 0), (1, 1), (2, 2), (3, 3), (4, 4), (5, 5), (7, 6), (8, 7)):
        sums[row : row + 1] = jnp.sum(folds[k], 0, keepdims=True)
    last_row = 8 + inner_rows
    sums[last_row : last_row + 1] = jnp.broadcast_to(loss, (1, width))
    small_sum = SumAll(place, wire, sums, room2)
    small_sum.start()

    def small_step(at):
        small_sum.finish()
        if small_sum.stage < 4:
            small_sum.start()

    def small_parts(at):
        small_grad[...] = jnp.zeros_like(small_grad)
        tile_sums[...] = jnp.zeros_like(tile_sums)
        of_affine = picked(sums[0:6], dp * n_affine, n_affine)
        of_head = picked(sums[6:8], owner * n_head, n_head)
        of_inner = picked(row_of(sums[8 : 8 + inner_rows], inner_row), inner_at, n_inner)
        small_grad[0:6, 0:n_affine] = of_affine
        small_grad[6:8, 0:n_head] = of_head
        small_grad[8:9, 0:n_inner] = of_inner
        small_grad[9:10] = sums[last_row : last_row + 1, 0:128]
        smalls = (
            (6, 6, n_affine, affine[...], affine_first[...], affine_second[...], of_affine, first),
            (12, 2, n_head, head_bias[...], head_first[...], head_second[...], of_head, 1.0),
            (14, 1, n_inner, inner_bias[...], inner_first[...], inner_second[...], of_inner, 1.0),
        )
        for row, n, lanes, weight, one, two, grad, share_of in smalls:
            update = moments(weight, one, two, grad, 0.0)[2]
            tile_sums[row : row + n, 0:lanes] = weight * weight * share_of
            tile_sums[16 + row : 16 + row + n, 0:lanes] = update * update * share_of


    for k in range(4):
        moves.add(moves.now + SMALL * (k + 1), small_step)
    moves.add(moves.now + SMALL * 4 + 1.0, small_parts)
    moves.drain()
    for k in range(2):
        for row in range(6):
            tile_sums[16 * k + row : 16 * k + row + 1] = jnp.sum(squares[k, row], 0, keepdims=True)
    every = SumSoon(place, wire, tile_sums, plane, line).value
    norms[...] = jnp.broadcast_to(jnp.sqrt(jnp.sum(every, -1, keepdims=True)), norms.shape)
    arrive(swaps)
    for copy in outs:
        copy.wait()
    wire.close()


def block_step(depth, *arrays):
    tokens, segment, pairing, images, qkv_weight, out_weight, up_weight, down_weight = arrays[:8]
    packs, length, width = tokens.shape
    rows = packs // 2 * length
    share, half = qkv_weight.shape[1:]
    blocks = up_weight.shape[1] // half
    units = 4 + 2 * blocks
    slots = pairing.shape[1]
    h = depth // 2
    few = images.shape[0]
    ring = 4
    small = (16, width)
    low = lambda *shape: pltpu.VMEM(shape, bf16)
    wide = lambda *shape: pltpu.VMEM(shape, f32)
    count = units * (depth - 1 + 5) + (depth - 1) * (few // 16) + 2 + units * (8 + depth - 1) + 2 * (3 + depth - 1) + 2 + 7 + depth - 1
    vmem = pl.BlockSpec(memory_space=pltpu.VMEM)
    hbm = pl.BlockSpec(memory_space=pl.ANY)
    return pl.pallas_call(
        functools.partial(block_kernel, depth),
        out_shape=(
            jax.ShapeDtypeStruct((units, share, half), f32),
            jax.ShapeDtypeStruct((16, 128), f32),
            jax.ShapeDtypeStruct((32, 128), f32),
            jax.ShapeDtypeStruct(tokens.shape, bf16),
        ),
        in_specs=[hbm] + [vmem] * 10 + [hbm] * 8 + [vmem] * 6,
        out_specs=[vmem, vmem, vmem, hbm],
        scratch_shapes=[
            low(units, depth, 2, 2, share, width), low(depth, 2, 2, few, width),
            low(units, depth, 2, 2, share, width), low(ring, depth, 2, share, width), low(units, h, 2, share, half),
            low(units, depth - h, share, width), low(units, h, share, half), low(units, depth - h, share, half),
            low(depth - 1, units, share, half),
            low(rows, width), low(rows, width), low(3, rows, width), low(rows, width), wide(rows, width), low(rows, width),
            low(blocks, rows, width), low(blocks, rows, width), wide(rows, width), low(rows, width), wide(rows, width), low(rows, width),
            low(2, width // (2 * HD), length // 64, 128, 128), wide(2, length // 64, 128, 128), wide(*small), wide(*small),
            wide(3 + depth, *small), wide(3 + depth, *small), wide(9, 8, width), wide(2 * slots, width),
            wide(2, *qkv_weight.shape), wide(2, *out_weight.shape), wide(2, *up_weight.shape), wide(2, *down_weight.shape),
            wide(2, 6, 8, 128), wide(32, 128), wide(8, 32, 128), wide(depth, 32, 128),
            pltpu.SemaphoreType.DMA((count,)), pltpu.SemaphoreType.DMA((count,)), pltpu.SemaphoreType.REGULAR,
            pltpu.SemaphoreType.DMA((2,)), pltpu.SemaphoreType.DMA((8,)),
        ],
        compiler_params=pltpu.CompilerParams(collective_id=1, has_side_effects=True, vmem_limit_bytes=64 << 20),
        name="train_block",
    )(*arrays)


def finish_kernel(slot_total, total, small_grad, norms, grad_low, *refs):
    weights, firsts, seconds = refs[0:7], refs[7:14], refs[14:21]
    grad_input = refs[21]
    nexts, first_nexts, second_nexts = refs[22:29], refs[29:36], refs[36:43]
    mean_loss, tensor_norms, room, wide_room, sems = refs[43:48]
    packs = grad_low.shape[0]
    reads = [pltpu.make_async_copy(grad_low.at[p], room.at[p], sems.at[p]) for p in range(packs)]
    writes = [pltpu.make_async_copy(wide_room.at[p], grad_input.at[p], sems.at[packs + p]) for p in range(packs)]
    for copy in reads:
        copy.start()

    def update(i, at, grad, row, decay):
        weight, one, two = weights[i][at], firsts[i][at], seconds[i][at]
        first_new, second_new, change = moments(weight, one, two, grad, decay)
        first_nexts[i][at] = first_new
        second_nexts[i][at] = second_new
        count = 1 if isinstance(row, int) else row[1]
        row = row if isinstance(row, int) else row[0]
        weight_norm, update_norm = norms[row : row + count, 0:1], norms[16 + row : 16 + row + count, 0:1]
        nexts[i][at] = weight - learning_rate * weight_norm / update_norm * change

    every = slice(None)
    half = total.shape[2]
    blocks = weights[2].shape[1] // half
    for p in range(packs):
        reads[p].wait()

        def widen(r, p=p):
            wide_room[p, r] = room[p, r].astype(f32)

        row_loop(room.shape[1], 32, widen)
        writes[p].start()
    for k in range(3):
        update(0, (k,), total[k], k, weight_decay)
    update(1, (every,), total[3], 3, weight_decay)
    for i in range(2):
        for j in range(blocks):
            update(2 + i, (every, slice(j * half, (j + 1) * half)), total[4 + i * blocks + j], 4 + i, weight_decay)
    update(4, (every,), small_grad[0:6, 0 : weights[4].shape[1]], (6, 6), 0.0)
    update(5, (every,), small_grad[6:8, 0 : weights[5].shape[1]], (12, 2), 0.0)
    update(6, (every,), small_grad[8:9, 0 : weights[6].shape[1]], 14, 0.0)
    mean_loss[...] = small_grad[9:10, 0:1] / slot_total
    square = norms.shape[0] // 2
    diagonal = lax.broadcasted_iota(jnp.int32, (square, square), 0) == lax.broadcasted_iota(jnp.int32, (square, square), 1)
    for k in range(2):
        column = jnp.broadcast_to(norms[square * k : square * (k + 1), 0:1], (square, square))
        tensor_norms[k : k + 1] = jnp.sum(jnp.where(diagonal, column, 0.0), 0, keepdims=True)[:, 0:15]
    for copy in writes:
        copy.wait()


def finish_step(slot_total, total, small_grad, norms, grad_low, weights, firsts, seconds):
    vmem = pl.BlockSpec(memory_space=pltpu.VMEM)
    hbm = pl.BlockSpec(memory_space=pl.ANY)
    packs, length, width = grad_low.shape
    like = [jax.ShapeDtypeStruct(a.shape, f32) for a in weights]
    return pl.pallas_call(
        functools.partial(finish_kernel, slot_total),
        out_shape=(
            jax.ShapeDtypeStruct(grad_low.shape, f32), *like, *like, *like,
            jax.ShapeDtypeStruct((1, 1), f32), jax.ShapeDtypeStruct((2, 15), f32),
        ),
        in_specs=[vmem] * 3 + [hbm] + [vmem] * 21,
        out_specs=[hbm] + [vmem] * 23,
        scratch_shapes=[
            pltpu.VMEM((packs, length, width), bf16), pltpu.VMEM((packs, length, width), f32),
            pltpu.SemaphoreType.DMA((2 * packs,)),
        ],
        compiler_params=pltpu.CompilerParams(vmem_limit_bytes=64 << 20),
        name="optimizer",
    )(total, small_grad, norms, grad_low, *weights, *firsts, *seconds)


def body_near(depth, *arrays):
    (
        tokens, segment, pairing, images,
        qkv_weight, qkv_first, qkv_second, out_weight, out_first, out_second,
        up_weight, up_first, up_second, down_weight, down_first, down_second,
        affine, affine_first, affine_second, head_bias, head_first, head_second,
        inner_bias, inner_first, inner_second,
    ) = arrays
    inner_bias, inner_first, inner_second = (a.reshape(1, -1) for a in (inner_bias, inner_first, inner_second))
    total, small_grad, norms, grad_low = block_step(
        depth, tokens, segment, pairing, images, qkv_weight, out_weight, up_weight, down_weight, affine, head_bias, inner_bias,
        qkv_first, qkv_second, out_first, out_second, up_first, up_second, down_first, down_second,
        affine_first, affine_second, head_first, head_second, inner_first, inner_second,
    )
    weights = (qkv_weight, out_weight, up_weight, down_weight, affine, head_bias, inner_bias)
    firsts = (qkv_first, out_first, up_first, down_first, affine_first, head_first, inner_first)
    seconds = (qkv_second, out_second, up_second, down_second, affine_second, head_second, inner_second)
    slot_total = float(pairing.size * 4 * depth)
    grad_input, *news, mean_loss, tensor_norms = finish_step(slot_total, total, small_grad, norms, grad_low, weights, firsts, seconds)
    results = [mean_loss.reshape(()), grad_input]
    for i in range(7):
        triple = (news[i], news[7 + i], news[14 + i])
        results += [a.reshape(-1) for a in triple] if i == 6 else triple
    return (*results, tensor_norms)


def body(
    tokens,
    segment,
    pairing,
    images,
    qkv_weight,
    qkv_first,
    qkv_second,
    out_weight,
    out_first,
    out_second,
    up_weight,
    up_first,
    up_second,
    down_weight,
    down_first,
    down_second,
    affine,
    affine_first,
    affine_second,
    head_bias,
    head_first,
    head_second,
    inner_bias,
    inner_first,
    inner_second,
):
    model_size = lax.axis_size("mp")
    packs, length, width = tokens.shape
    rows = packs * length
    qkv_full, out_full, up_full, down_full, affine_full, head_full, inner_full = (
        lax.all_gather(qkv_weight.astype(jnp.bfloat16), "dp", axis=1, tiled=True),
        lax.all_gather(out_weight.astype(jnp.bfloat16), "dp", axis=0, tiled=True),
        lax.all_gather(up_weight.astype(jnp.bfloat16), "dp", axis=0, tiled=True),
        lax.all_gather(down_weight.astype(jnp.bfloat16), "dp", axis=0, tiled=True),
        lax.all_gather(affine.astype(jnp.bfloat16), "dp", axis=1, tiled=True),
        lax.all_gather(head_bias.astype(jnp.bfloat16), "dp", axis=1, tiled=True),
        lax.all_gather(inner_bias.astype(jnp.bfloat16), "dp", axis=0, tiled=True),
    )
    affine_wide = affine_full.astype(jnp.float32)
    head_wide = head_full.astype(jnp.float32)
    inner_wide = inner_full.astype(jnp.float32)
    half = qkv_full.shape[2]
    local_heads = half // HD
    shape4 = (packs, length, local_heads, HD)
    root_scale = HD ** (-0.5)
    inputs = tokens.reshape(rows, width).astype(jnp.float32)
    normed_one = layer_norm(inputs, affine_wide[0], affine_wide[1]).astype(jnp.bfloat16)
    projected = jnp.einsum("td,kde->kte", normed_one, qkv_full, preferred_element_type=jnp.float32)
    query = (projected[0] + head_wide[0]).astype(jnp.bfloat16).reshape(shape4)
    keys = projected[1].astype(jnp.bfloat16).reshape(shape4)
    values = (projected[2] + head_wide[1]).astype(jnp.bfloat16).reshape(shape4)
    same = segment[:, None, :, None] == segment[:, None, None, :]

    def masked_scores():
        raw = (
            jnp.einsum("pqhe,pkhe->phqk", query, keys, preferred_element_type=jnp.float32)
            * root_scale
        )
        return jnp.where(same, raw, mask_value)

    scores = masked_scores()
    top = jnp.max(scores, -1, keepdims=True)
    log_total = top + jnp.log(jnp.sum(jnp.exp(scores - top), -1, keepdims=True))
    probs = jnp.exp(scores - log_total).astype(jnp.bfloat16)
    mixed = jnp.einsum("phqk,pkhe->pqhe", probs, values, preferred_element_type=jnp.float32)
    mixed = mixed.reshape(rows, half).astype(jnp.bfloat16)
    attended = lax.psum(summation_axes_spec(mixed, out_full, 1, 1), "mp")
    resid = inputs + attended + affine_wide[4]
    normed_two = layer_norm(resid, affine_wide[2], affine_wide[3]).astype(jnp.bfloat16)
    upper = jnp.dot(normed_two, up_full, preferred_element_type=jnp.float32) + inner_wide
    activated, gelu_back = jax.vjp(jax.nn.gelu, upper)
    hidden = activated.astype(jnp.bfloat16)
    lowered = lax.psum(
        summation_axes_spec(hidden, down_full, 1, 1).astype(jnp.bfloat16), "mp"
    ).astype(jnp.float32)
    output = resid + lowered + affine_wide[5]
    slots = pairing.shape[1]
    onehot = (segment[:, None, :] == jnp.arange(slots, dtype=jnp.int32)[None, :, None]).astype(
        jnp.float32
    )
    counts = jnp.sum(onehot, -1)
    divisor = jnp.maximum(counts, 1.0)[..., None]
    pooled = (
        jnp.einsum(
            "pcl,pld->pcd",
            onehot,
            output.reshape(packs, length, width),
            precision=exact_arithmetic_mode,
        )
        / divisor
    )
    flat = pooled.reshape(packs * slots, width)
    caption_wide, normalize_back = jax.vjp(normalize, flat)
    sentence_words = caption_wide.astype(jnp.bfloat16)
    live = (counts > 0).reshape(-1).astype(jnp.float32)
    target = pairing.reshape(-1)
    captions_count = flat.shape[0]
    slot_total = float(captions_count * lax.axis_size("dp"))
    picture_summed = normalize(images.astype(jnp.float32)).astype(jnp.bfloat16)

    def similarity(packed_sequence_slice):
        return sharpness_divisor * summation_axes_spec(sentence_words, packed_sequence_slice, 1, 1)

    score_packed_sequence_slice = lax.all_gather(picture_summed, "dp", axis=0, tiled=True)
    best = jnp.full((captions_count,), mask_value, jnp.float32)
    similarity_grid = similarity(score_packed_sequence_slice)
    new_best = jnp.maximum(best, jnp.max(similarity_grid, 1))
    total = jnp.sum(jnp.exp(similarity_grid - new_best[:, None]), 1)
    column = jnp.arange(score_packed_sequence_slice.shape[0], dtype=jnp.int32)
    hit = target[:, None] == column[None, :]
    positive = jnp.sum(jnp.where(hit, similarity_grid, 0.0), 1)
    best_all, total_all, positive = (new_best, total, positive)
    log_sum = best_all + jnp.log(total_all)
    grad_packed_sequence_slice = lax.all_gather(picture_summed, "dp", axis=0, tiled=True)
    similarity_grid = similarity(grad_packed_sequence_slice)
    column = jnp.arange(grad_packed_sequence_slice.shape[0], dtype=jnp.int32)
    hit = (target[:, None] == column[None, :]).astype(jnp.float32)
    logit_gradient = (
        loss_scale * live[:, None] * (jnp.exp(similarity_grid - log_sum[:, None]) - hit)
    ).astype(jnp.bfloat16)
    sentence_derivative = sharpness_divisor * jnp.dot(
        logit_gradient, grad_packed_sequence_slice, preferred_element_type=jnp.float32
    )
    cross = log_sum - positive
    loss_local = jnp.sum(live * cross)
    loss_total = lax.psum(loss_local, "dp")
    mean_loss = loss_total / slot_total
    (grad_flat,) = normalize_back(sentence_derivative)
    grad_pooled = grad_flat.reshape(packs, slots, width) / divisor
    grad_output = jnp.einsum(
        "pcl,pcd->pld", onehot, grad_pooled, precision=exact_arithmetic_mode
    ).reshape(rows, width)
    grad_output_low = grad_output.astype(jnp.bfloat16)
    down_grad = summation_axes_spec(grad_output_low, hidden, 0, 0)
    grad_hidden = jnp.dot(grad_output_low, down_full, preferred_element_type=jnp.float32)
    (grad_upper,) = gelu_back(grad_hidden)
    grad_upper = grad_upper.astype(jnp.bfloat16)
    inner_grad = jnp.sum(grad_upper.astype(jnp.float32), 0)
    up_grad = summation_axes_spec(normed_two, grad_upper, 0, 0)
    grad_two = lax.psum(
        summation_axes_spec(grad_upper, up_full, 1, 1).astype(jnp.bfloat16), "mp"
    ).astype(jnp.float32)
    _, norm_two_back = jax.vjp(layer_norm, resid, affine_wide[2], affine_wide[3])
    grad_resid_norm, gain_two_grad, shift_two_grad = norm_two_back(grad_two)
    grad_resid = grad_output + grad_resid_norm
    grad_resid_low = grad_resid.astype(jnp.bfloat16)
    out_grad = summation_axes_spec(grad_resid_low, mixed, 0, 0)
    grad_mixed = jnp.dot(grad_resid_low, out_full, preferred_element_type=jnp.float32)
    grad_mixed = grad_mixed.astype(jnp.bfloat16).reshape(shape4)
    probs_wide = jnp.exp(masked_scores() - log_total)
    probs_low = probs_wide.astype(jnp.bfloat16)
    grad_value = jnp.einsum(
        "phqk,pqhe->pkhe", probs_low, grad_mixed, preferred_element_type=jnp.float32
    )
    grad_probs = jnp.einsum(
        "pqhe,pkhe->phqk", grad_mixed, values, preferred_element_type=jnp.float32
    )
    grad_scores = probs_wide * (grad_probs - jnp.sum(probs_wide * grad_probs, -1, keepdims=True))
    grad_scores = grad_scores.astype(jnp.bfloat16)
    grad_query = (
        jnp.einsum("phqk,pkhe->pqhe", grad_scores, keys, preferred_element_type=jnp.float32)
        * root_scale
    )
    grad_key = (
        jnp.einsum("phqk,pqhe->pkhe", grad_scores, query, preferred_element_type=jnp.float32)
        * root_scale
    )
    grad_qkv = (
        jnp.stack([grad_query, grad_key, grad_value]).reshape(3, rows, half).astype(jnp.bfloat16)
    )
    head_grad = jnp.stack(
        [jnp.sum(grad_qkv[0].astype(jnp.float32), 0), jnp.sum(grad_qkv[2].astype(jnp.float32), 0)]
    )
    qkv_grad = jnp.einsum("td,kte->kde", normed_one, grad_qkv, preferred_element_type=jnp.float32)
    grad_one = lax.psum(
        jnp.einsum("kte,kde->td", grad_qkv, qkv_full, preferred_element_type=jnp.float32).astype(
            jnp.bfloat16
        ),
        "mp",
    ).astype(jnp.float32)
    _, norm_one_back = jax.vjp(layer_norm, inputs, affine_wide[0], affine_wide[1])
    grad_input_norm, gain_one_grad, shift_one_grad = norm_one_back(grad_one)
    grad_input = (grad_resid + grad_input_norm).reshape(packs, length, width)
    affine_grad = jnp.stack(
        [
            gain_one_grad,
            shift_one_grad,
            gain_two_grad,
            shift_two_grad,
            jnp.sum(grad_resid, 0),
            jnp.sum(grad_output, 0),
        ]
    )
    qkv_part, out_part, up_part, down_part, affine_part, head_part, inner_part = (
        lax.psum_scatter(qkv_grad, "dp", scatter_dimension=1, tiled=True),
        lax.psum_scatter(out_grad, "dp", scatter_dimension=0, tiled=True),
        lax.psum_scatter(up_grad, "dp", scatter_dimension=0, tiled=True),
        lax.psum_scatter(down_grad, "dp", scatter_dimension=0, tiled=True),
        lax.psum_scatter(affine_grad, "dp", scatter_dimension=1, tiled=True),
        lax.psum_scatter(head_grad, "dp", scatter_dimension=1, tiled=True),
        lax.psum_scatter(inner_grad, "dp", scatter_dimension=0, tiled=True),
    )
    weights = (qkv_weight, out_weight, up_weight, down_weight, affine, head_bias, inner_bias)
    firsts = (qkv_first, out_first, up_first, down_first, affine_first, head_first, inner_first)
    seconds = (
        qkv_second,
        out_second,
        up_second,
        down_second,
        affine_second,
        head_second,
        inner_second,
    )
    grads = (qkv_part, out_part, up_part, down_part, affine_part, head_part, inner_part)
    decays = (weight_decay, weight_decay, weight_decay, weight_decay, 0.0, 0.0, 0.0)
    parts = [
        moments(weights[index], firsts[index], seconds[index], grads[index], decays[index])
        for index in range(7)
    ]
    updates = [packed_sequence_slice[2] for packed_sequence_slice in parts]
    weight_squares = tensor_squares(*weights, float(model_size))
    update_squares = tensor_squares(*updates, float(model_size))
    weight_total, update_total = lax.psum((weight_squares, update_squares), ("dp", "mp"))
    weight_norm = jnp.sqrt(weight_total)
    update_norm = jnp.sqrt(update_total)
    weight_split = split_norms(weight_norm)
    update_split = split_norms(update_norm)
    news = [
        scaled_step(weights[index], updates[index], weight_split[index], update_split[index])
        for index in range(7)
    ]
    return (
        mean_loss,
        grad_input,
        news[0],
        parts[0][0],
        parts[0][1],
        news[1],
        parts[1][0],
        parts[1][1],
        news[2],
        parts[2][0],
        parts[2][1],
        news[3],
        parts[3][0],
        parts[3][1],
        news[4],
        parts[4][0],
        parts[4][1],
        news[5],
        parts[5][0],
        parts[5][1],
        news[6],
        parts[6][0],
        parts[6][1],
        jnp.stack([weight_norm, update_norm]),
    )


def solution(mesh):
    depth = mesh.shape["dp"] // 4
    fits = mesh.shape["mp"] == 2 and mesh.shape["dp"] % 8 == 0 and 768 // mesh.shape["dp"] % 16 == 0
    return jax.shard_map(
        functools.partial(body_near, depth) if fits else body,
        mesh=mesh,
        in_specs=(
            P("dp", None, None),
            P("dp", None),
            P("dp", None),
            P("dp", None),
            P(None, "dp", "mp"),
            P(None, "dp", "mp"),
            P(None, "dp", "mp"),
            P("dp", "mp"),
            P("dp", "mp"),
            P("dp", "mp"),
            P("dp", "mp"),
            P("dp", "mp"),
            P("dp", "mp"),
            P("dp", "mp"),
            P("dp", "mp"),
            P("dp", "mp"),
            P(None, "dp"),
            P(None, "dp"),
            P(None, "dp"),
            P(None, ("mp", "dp")),
            P(None, ("mp", "dp")),
            P(None, ("mp", "dp")),
            P(("mp", "dp")),
            P(("mp", "dp")),
            P(("mp", "dp")),
        ),
        out_specs=(
            P(),
            P("dp", None, None),
            P(None, "dp", "mp"),
            P(None, "dp", "mp"),
            P(None, "dp", "mp"),
            P("dp", "mp"),
            P("dp", "mp"),
            P("dp", "mp"),
            P("dp", "mp"),
            P("dp", "mp"),
            P("dp", "mp"),
            P("dp", "mp"),
            P("dp", "mp"),
            P("dp", "mp"),
            P(None, "dp"),
            P(None, "dp"),
            P(None, "dp"),
            P(None, ("mp", "dp")),
            P(None, ("mp", "dp")),
            P(None, ("mp", "dp")),
            P(("mp", "dp")),
            P(("mp", "dp")),
            P(("mp", "dp")),
            P(),
        ),
        check_vma=False,
    )
```
